128 devices in a mesh: row: 64 (over z, y, x_hi, core), col: 2 (over x_lo).
Axes of the slice: x: 4 (x_hi: 2, x_lo: 2; x = x_hi * 2 + x_lo), y: 4, z: 4, core: 2. Of those that a mesh axis runs over, the one named last changes fastest.
Arguments:
- current: bfloat16 [2, 256, 512, 256], P(None, None, 'row', 'col'), may hold values from -6 to 6
- previous: bfloat16 [2, 256, 512, 256], P(None, None, 'row', 'col'), may hold values from -6 to 6
- shift: int32 [2, 2], replicated, may hold values from -4 to 4, as said below
- weight: bfloat16 [128, 81], replicated, may hold values from -0.625 to 0.625
- cotangent: bfloat16 [2, 128, 512, 256], P(None, None, 'row', 'col'), may hold values from -6 to 6
Outputs:
- grad_current: bfloat16 [2, 256, 512, 256], P(None, None, 'row', 'col')
- grad_previous: bfloat16 [2, 256, 512, 256], P(None, None, 'row', 'col')
- grad_weight: float32 [128, 81], replicated
The draws below stay inside these ranges and needn't reach their ends.
Inputs may be any that keep to these rules, and one draw needn't show every extreme that they name: `shift`: in every draw the row offset of the first pair and the column offset of the last pair are 4 and -4 in some order.
All inputs are finite; a program needn't handle non-finite values.
Results may differ from the reference program's by a relative error of at most 0.005.
Values may be sent and summed in bfloat16 or wider, within the bound.
A program may use at most 320 MiB of HBM per device.

```python
import math
import jax
import jax.numpy as jnp
from jax import lax

CHANNELS = 256
ENCODED = 128
OFFSETS = 81
FRAME_PAIRS = 2
GRID_ROWS = 512
GRID_COLS = 256


def draw_shift(key, part):
    key = jax.random.fold_in(key, 7)
    first_key, second_key = jax.random.split(key)
    offsets = jax.random.randint(first_key, (FRAME_PAIRS, 2), -4, 5, dtype=jnp.int32)
    sign_value = jax.random.randint(second_key, (), 0, 2, dtype=jnp.int32) * 8 - 4
    offsets = offsets.at[0, 0].set(sign_value)
    offsets = offsets.at[FRAME_PAIRS - 1, 1].set(-sign_value)
    return offsets


def level_of(key, dims, pieces, smallest, largest):
    gain, own = 1.0, jax.random.fold_in(key, 6)
    for position, blocks in pieces:
        draws = jnp.exp(jax.random.uniform(jax.random.fold_in(own, position), (blocks,), jnp.float32, smallest / len(pieces), largest / len(pieces)))
        gain = gain * jnp.repeat(draws, dims[position] // blocks).reshape([-1 if axis == position else 1 for axis in range(len(dims))])
    return gain


def bell_draw(key, shape, deviation, reach, pieces=(), kind=jnp.bfloat16):
    array = deviation * jax.random.normal(key, shape, jnp.float32)
    if pieces:
        array = array * level_of(key, shape, pieces, -0.22, 0.18)
    return jnp.clip(array, -reach, reach).astype(kind)


def setup_inputs(seed: int = 0) -> dict:
    key_list = jax.random.split(jax.random.key(seed), 6)
    return {
        "current": bell_draw(key_list[0], (FRAME_PAIRS, CHANNELS, GRID_ROWS, GRID_COLS), 1.0, 6.0, ((2, 64), (3, 2))),
        "previous": bell_draw(key_list[1], (FRAME_PAIRS, CHANNELS, GRID_ROWS, GRID_COLS), 1.0, 6.0, ((2, 64), (3, 2))),
        "shift": draw_shift(jax.random.fold_in(key_list[5], 71), 0),
        "weight": bell_draw(key_list[3], (ENCODED, OFFSETS), OFFSETS ** -0.5, 0.625),
        "cotangent": bell_draw(key_list[4], (FRAME_PAIRS, ENCODED, GRID_ROWS, GRID_COLS), 1.0, 6.0, ((2, 64), (3, 2))),
    }


def reference(current, previous, shift, weight, cotangent):
    scale = 1.0 / math.sqrt(CHANNELS)
    zero = jnp.int32(0)
    steps = jnp.arange(81, dtype=jnp.int32)
    weight_total = jnp.zeros((ENCODED, OFFSETS), jnp.float32)
    grads_cur = []
    grads_prev = []
    for pair in range(FRAME_PAIRS):
        row_off = shift[pair, 0].astype(jnp.int32)
        col_off = shift[pair, 1].astype(jnp.int32)
        padded = jnp.pad(previous[pair], ((0, 0), (8, 8), (8, 8)))
        window = lax.dynamic_slice(padded, (zero, (4 + row_off).astype(jnp.int32), (4 + col_off).astype(jnp.int32)), (CHANNELS, GRID_ROWS + 8, GRID_COLS + 8)).astype(jnp.float32)
        cur_f = current[pair].astype(jnp.float32)

        def corr_step(carry, index):
            first = (index // 9).astype(jnp.int32)
            second = (index % 9).astype(jnp.int32)
            piece = lax.dynamic_slice(window, (zero, first, second), (CHANNELS, GRID_ROWS, GRID_COLS))
            return (carry, lax.optimization_barrier(jnp.sum(cur_f * piece, axis=0)) * scale)
        _, volume = lax.scan(corr_step, jnp.float32(0.0), steps)
        activated = jax.nn.silu(volume).astype(jnp.bfloat16)
        cot_f = cotangent[pair].astype(jnp.float32)
        weight_total = weight_total + jnp.einsum('oyx,dyx->od', cot_f, activated.astype(jnp.float32))
        pre = jnp.einsum('od,oyx->dyx', weight.astype(jnp.float32), cot_f)
        sig = jax.nn.sigmoid(volume)
        grad_volume = (pre * sig * (1.0 + volume * (1.0 - sig)) * scale).astype(jnp.bfloat16)
        grad_volume = lax.optimization_barrier(grad_volume).astype(jnp.float32)

        def cur_step(carry, inputs):
            index, gslice = inputs
            first = (index // 9).astype(jnp.int32)
            second = (index % 9).astype(jnp.int32)
            piece = lax.dynamic_slice(window, (zero, first, second), (CHANNELS, GRID_ROWS, GRID_COLS))
            return (carry + gslice[None] * piece, None)
        grad_cur, _ = lax.scan(cur_step, jnp.zeros((CHANNELS, GRID_ROWS, GRID_COLS), jnp.float32), (steps, grad_volume))

        def prev_step(carry, inputs):
            index, gslice = inputs
            first = (index // 9).astype(jnp.int32)
            second = (index % 9).astype(jnp.int32)
            old = lax.dynamic_slice(carry, (zero, first, second), (CHANNELS, GRID_ROWS, GRID_COLS))
            return (lax.dynamic_update_slice(carry, old + gslice[None] * cur_f, (zero, first, second)), None)
        spread, _ = lax.scan(prev_step, jnp.zeros((CHANNELS, GRID_ROWS + 8, GRID_COLS + 8), jnp.float32), (steps, grad_volume))
        spread_pad = jnp.pad(spread, ((0, 0), (8, 8), (8, 8)))
        grad_prev = lax.dynamic_slice(spread_pad, (zero, (12 - row_off).astype(jnp.int32), (12 - col_off).astype(jnp.int32)), (CHANNELS, GRID_ROWS, GRID_COLS))
        grads_cur.append(grad_cur.astype(jnp.bfloat16))
        grads_prev.append(grad_prev.astype(jnp.bfloat16))
    norm = 1.0 / math.sqrt(FRAME_PAIRS * GRID_ROWS * GRID_COLS)
    return (jnp.stack(grads_cur), jnp.stack(grads_prev), weight_total * norm)
```

```python
import math

import jax
import jax.numpy as jnp
import numpy as np
from jax import lax
from jax.experimental import pallas as pl
from jax.experimental.pallas import tpu as pltpu
from jax.sharding import PartitionSpec as P

BF = jnp.bfloat16
F32 = jnp.float32
MESH = pl.DeviceIdType.MESH
NT = (((1,), (1,)), ((), ()))
TN = (((0,), (0,)), ((), ()))
NN = (((1,), (0,)), ((), ()))
WIDE = 144


def dot(a, b, dims=NN):
    return lax.dot_general(a, b, dims, preferred_element_type=F32)


def iota(shape, axis):
    return lax.broadcasted_iota(jnp.int32, shape, axis)


def skew(x, shift):
    return pltpu.roll(x, shift % 256, 1, stride=1, stride_axis=0)


def flip8(x):
    idx = 7 - iota((8, 128), 0)
    parts = [
        jnp.take_along_axis(x[:, at : at + 128], idx, axis=0) for at in range(0, x.shape[1], 128)
    ]
    return parts[0] if len(parts) == 1 else jnp.concatenate(parts, axis=1)


def activation(vol_dot):
    half = vol_dot * (1.0 / 32.0)
    q = 1.0 + jnp.tanh(half)
    act = half * q
    return act, q + act * (2.0 - q)


def cell_part(p, bb, dy, win_ref, cur_ref, cot_ref, wk, out_ref, acc_ref):
    at = pl.multiple_of(bb * 16, 16)
    cur = cur_ref[p, :, pl.ds(at, 16), :].reshape(128, 256)
    cot = cot_ref[p, :, pl.ds(at, 16), :].reshape(128, 128)
    win = win_ref[pl.ds(4 + dy, 16), pl.ds(at, 32), :]
    win_e = win[:, 0:16].reshape(256, 256)
    win_o = win[:, 8:24].reshape(256, 256)
    vol_e = dot(cur, win_e, NT)
    vol_o = dot(cur, win_o, NT)
    pre = dot(cot, wk)
    cot_rev = cot.astype(F32)
    cot_rev = jnp.concatenate([flip8(cot_rev[8 * i : 8 * i + 8]) for i in range(16)], axis=0)
    acts, grads = [], []
    for i in range(16):
        y, odd = divmod(i, 2)
        rows = slice(8 * i, 8 * i + 8)
        act, slope = activation((vol_o if odd else vol_e)[rows])
        grads.append(skew(pre[rows], 16 * y) * slope)
        acts.append(skew(flip8(act), 249 - 16 * y))
    act = jnp.concatenate(acts, axis=0).astype(BF)
    acc_ref[...] += dot(cot_rev.astype(BF), act, TN).reshape(8, 16, 256)
    out_e = dot(jnp.concatenate(grads[0::2], axis=0).astype(BF), win_e)
    out_o = dot(jnp.concatenate(grads[1::2], axis=0).astype(BF), win_o)
    outs = []
    for y in range(8):
        outs += [out_e[8 * y : 8 * y + 8], out_o[8 * y : 8 * y + 8]]
    out_ref[p, :, pl.ds(at, 16), :] = (
        jnp.concatenate(outs, axis=0).astype(BF).reshape(8, 16, 256)
    )


def position_part(p, bb, dy, win_ref, pre_ref, prev_ref, spread, masks, out_ref):
    at = pl.multiple_of(bb * 16, 16)
    prev = prev_ref[p, :, pl.ds(at, 16), :].reshape(128, 256)
    wins, pres = [], []
    for j in range(16):
        row = jnp.where(j < 4 + dy, j, jnp.where(j < 12 + dy, 20 + j - dy, 8 + j))
        wins.append(win_ref[row, pl.ds(at, 32), :][:24])
        pres.append(pre_ref[row, pl.ds(at, 32), :][:24])
    win = jnp.concatenate(wins, axis=0)
    vol = dot(win, prev, NT)
    pre = dot(jnp.concatenate(pres, axis=0), spread)
    grads = []
    for j in range(16):
        for g in range(3):
            rows = slice(24 * j + 8 * g, 24 * j + 8 * g + 8)
            piece = pre[rows]
            if g != 1:
                piece = piece * masks[g // 2]
            piece = skew(piece, 16 * (j - 8) + 8 * (g - 1))[:, :128]
            grads.append(piece * activation(vol[rows])[1])
    grad = jnp.concatenate(grads, axis=0).astype(BF)
    out_ref[p, :, pl.ds(at, 16), :] = dot(grad, win, TN).astype(BF).reshape(8, 16, 256)


def kernel(
    shift_ref, prev_ref, cur_ref, cot_ref, w_ref, e_ref,
    gc_ref, gp_ref, gw_ref,
    edge_s, edge_r, edge_cot_s, edge_cot_r, own, own_cot, own_pre, msg, tri_s, tri_r,
    win0, win1, pre0, pre1, acc, ar1, ar2, ar3,
    side_ss, side_rs, row_ss, row_rs, s1, r1, s2, r2, s3, r3,
):
    row, col = lax.axis_index("row"), lax.axis_index("col")
    last = lax.axis_size("row") - 1
    left = col == 0
    wins, pres = (win0, win1), (pre0, pre1)
    g1, g2 = (row % 4) * 2 + col, row // 4

    def member(a, b):
        return (b * 4 + a // 2, a % 2)

    barrier = pltpu.get_barrier_semaphore()

    def greet(target):
        pl.semaphore_signal(barrier, inc=1, device_id=target, device_id_type=MESH)

    for d in range(1, 8):
        greet(member((g1 + d) % 8, g2))
    for d in range(1, 16):
        greet(member(g1, (g2 + d) % 16))
    greet(((row + 1) % (last + 1), col))
    greet(((row + last) % (last + 1), col))
    pl.semaphore_wait(barrier, 24)

    def side(p, k):
        s, r = ((edge_s, edge_r), (edge_cot_s, edge_cot_r))[k]
        return pltpu.make_async_remote_copy(
            src_ref=s.at[p], dst_ref=r.at[p], send_sem=side_ss.at[p, k],
            recv_sem=side_rs.at[p, k], device_id=(row, 1 - col), device_id_type=MESH,
        )

    def along(p, way, k):
        if k == 0:
            src, dst = msg.at[p, way], wins[p].at[pl.ds(0 if way else 16, 8)]
        else:
            src, dst = tri_s.at[p, way], tri_r.at[p, way]
        target = jnp.where(row == last, row, row + 1) if way else jnp.where(row == 0, row, row - 1)
        return pltpu.make_async_remote_copy(
            src_ref=src, dst_ref=dst, send_sem=row_ss.at[p, way, k],
            recv_sem=row_rs.at[p, way, k], device_id=(target, col), device_id_type=MESH,
        )

    start = jnp.where(left, 112, 0)
    for p in range(2):
        for y in range(8):
            pick = []
            for ref in (prev_ref, cur_ref):
                tile = ref[p, y, pl.ds(pl.multiple_of(start, 16), 16), :].astype(F32)
                pick.append(jnp.where(left, tile[8:], tile[:8]))
            edge_s[p, y] = jnp.concatenate(pick, axis=0).astype(BF)
        for y in range(0, 8, 2):
            pick = []
            for yy in (y, y + 1):
                tile = cot_ref[p, yy, pl.ds(pl.multiple_of(start, 16), 16), :].astype(F32)
                pick.append(jnp.where(left, tile[8:], tile[:8]))
            edge_cot_s[p, y // 2] = jnp.concatenate(pick, axis=0).astype(BF)
        side(p, 0).start()
        side(p, 1).start()

    w9 = w_ref[...]
    e = e_ref[...]
    wk = dot(w9, e).astype(BF)
    spread = jnp.concatenate([wk, e], axis=0)
    sub, lane = iota((8, 256), 0), iota((8, 256), 1) % 16
    masks = (jnp.where(lane >= 8 - sub, 1.0, 0.0), jnp.where(lane < 8 - sub, 1.0, 0.0))
    out_at, in_at = iota((WIDE, WIDE), 0), iota((WIDE, WIDE), 1)
    far = jnp.where(left, 136, 0)
    tri_lane = iota((WIDE, 128), 1)

    def aligner(offset, slots):
        at = jnp.where(in_at < 128, in_at + 8, in_at - 128 - slots + far)
        ok = (in_at < 128) | ((in_at >= 128 + slots) & (in_at < 136 + slots))
        return jnp.where(ok & (at == out_at + offset), 1.0, 0.0).astype(BF)

    for p in range(2):
        dy, dx = shift_ref[p, 0], shift_ref[p, 1]
        win, pre = wins[p], pres[p]
        align_p, align_c0, align_c1 = aligner(4 + dx, 0), aligner(4 - dx, 0), aligner(4 - dx, 8)
        for k in range(2):
            side(p, k).wait()
        for y in range(8):
            edge = edge_r[p, y]
            aligned = dot(align_p, jnp.concatenate([prev_ref[p, y], edge], axis=0)).astype(BF)
            own[y] = aligned
            win[8 + y] = aligned
            aligned = dot(align_c1, jnp.concatenate([cur_ref[p, y], edge], axis=0)).astype(BF)
            own[8 + y] = aligned
            win[24 + y] = aligned
            align = align_c1 if y % 2 else align_c0
            both = jnp.concatenate([cot_ref[p, y], edge_cot_r[p, y // 2]], axis=0)
            aligned = dot(align, both).astype(BF)
            pre[24 + y] = jnp.concatenate([aligned, jnp.zeros_like(aligned)], axis=1)
            own_pre[y] = dot(aligned, w9)

        def pack(s, carry):
            msg[p, 0, s] = own[jnp.where(s < 4 + dy, s, 4 + s - dy)]
            msg[p, 1, s] = own[jnp.where(s < 4 + dy, 12 + s - dy, s)]
            return carry

        lax.fori_loop(0, 8, pack, 0)

        def cell_row(t):
            return own_pre[jnp.where(t < 4 + dy, t + 4 - dy, t - 4 - dy)]

        for s in range(4):
            near, away = cell_row(s), cell_row(7 - s)
            tri_s[p, 1, s] = jnp.where(
                tri_lane >= 9 * (8 - s), near, pltpu.roll(away, 128 - 9 * (s + 1), 1)
            ).astype(BF)
            tri_s[p, 0, s] = jnp.where(
                tri_lane < 9 * (8 - s), near, pltpu.roll(away, 9 * (8 - s), 1)
            ).astype(BF)

        @pl.when(row > 0)
        def _():
            for k in range(2):
                along(p, 0, k).start()

        @pl.when(row < last)
        def _():
            for k in range(2):
                along(p, 1, k).start()

    acc[...] = jnp.zeros_like(acc)

    def arrive(p):
        win, pre = wins[p], pres[p]

        @pl.when(row > 0)
        def _():
            for k in range(2):
                along(p, 1, k).wait_recv()

        @pl.when(row == 0)
        def _():
            win[0:8] = jnp.zeros((8, WIDE, 256), BF)
            tri_r[p, 1] = jnp.zeros((4, WIDE, 128), BF)

        @pl.when(row < last)
        def _():
            for k in range(2):
                along(p, 0, k).wait_recv()

        @pl.when(row == last)
        def _():
            win[16:24] = jnp.zeros((8, WIDE, 256), BF)
            tri_r[p, 0] = jnp.zeros((4, WIDE, 128), BF)

        zero = jnp.zeros((WIDE, 128), BF)
        for s in range(4):
            got = tri_r[p, 1, s]
            pre[s] = jnp.concatenate([zero, got], axis=1)
            got = pltpu.roll(got.astype(F32), 9 * (s + 1), 1).astype(BF)
            pre[7 - s] = jnp.concatenate([zero, got], axis=1)
            got = tri_r[p, 0, s]
            pre[16 + s] = jnp.concatenate([zero, got], axis=1)
            got = pltpu.roll(got.astype(F32), 128 - 9 * (8 - s), 1).astype(BF)
            pre[23 - s] = jnp.concatenate([zero, got], axis=1)

    def run_cells(p):
        def body(bb, carry):
            cell_part(p, bb, shift_ref[p, 0], wins[p], cur_ref, cot_ref, wk, gc_ref, acc)
            return carry

        lax.fori_loop(0, 8, body, 0)

    def run_positions(p, lo, hi):
        def body(bb, carry):
            position_part(
                p, bb, shift_ref[p, 0], wins[p], pres[p], prev_ref, spread, masks, gp_ref
            )
            return carry

        lax.fori_loop(lo, hi, body, 0)

    arrive(0)
    run_cells(0)
    run_positions(0, 0, 8)
    arrive(1)
    run_cells(1)

    def first(d):
        peer = (g1 + d) % 8
        return pltpu.make_async_remote_copy(
            src_ref=acc.at[peer], dst_ref=ar1.at[g1], send_sem=s1.at[peer],
            recv_sem=r1.at[g1], device_id=member(peer, g2), device_id_type=MESH,
        )

    def second(d):
        peer = (g2 + d) % 16
        return pltpu.make_async_remote_copy(
            src_ref=ar2.at[g2], dst_ref=ar2.at[g2], send_sem=s2.at[peer],
            recv_sem=r2.at[g2], device_id=member(g1, peer), device_id_type=MESH,
        )

    def third(d):
        peer = (g1 + d) % 8
        return pltpu.make_async_remote_copy(
            src_ref=ar3.at[g1], dst_ref=ar3.at[g1], send_sem=s3.at[peer],
            recv_sem=r3.at[g1], device_id=member(peer, g2), device_id_type=MESH,
        )

    def got(buffer, sends, receives, source):
        pltpu.make_async_remote_copy(
            src_ref=buffer.at[source], dst_ref=buffer.at[source], send_sem=sends.at[source],
            recv_sem=receives.at[source], device_id=(row, 1 - col), device_id_type=MESH,
        ).wait_recv()

    for d in range(1, 8):
        first(d).start()
    run_positions(1, 0, 3)
    ar1[g1] = acc[g1]
    for d in range(1, 8):
        first(d).wait_send()
        got(ar1, s1, r1, (g1 + d) % 8)
    ar2[g2] = jnp.sum(ar1[...], axis=0)
    for d in range(1, 16):
        second(d).start()
    run_positions(1, 3, 6)
    for d in range(1, 16):
        second(d).wait_send()
        got(ar2, s2, r2, (g2 + d) % 16)
    ar3[g1] = jnp.sum(ar2[...], axis=0)
    for d in range(1, 8):
        third(d).start()
    run_positions(1, 6, 8)
    for d in range(1, 8):
        third(d).wait_send()
        got(ar3, s3, r3, (g1 + d) % 8)
    gw_ref[...] = ar3[...]

    for p in range(2):
        for k in range(2):

            @pl.when(row > 0)
            def _():
                along(p, 0, k).wait_send()

            @pl.when(row < last)
            def _():
                along(p, 1, k).wait_send()


def spread_matrix():
    e = np.zeros((128, 256), np.float32)
    for u in range(9):
        for v in range(9):
            e[9 * u + v, 16 * u + v] = 1.0 / 32.0
    return e


def local(current, previous, shift, weight, cotangent):
    pairs, channels, rows, cols = current.shape
    prev = previous.transpose(0, 2, 3, 1)
    cur = current.transpose(0, 2, 3, 1)
    cot = cotangent.transpose(0, 2, 3, 1)
    w9 = jnp.pad(weight, ((0, 0), (0, 128 - 81)))
    e = jnp.asarray(spread_matrix(), BF)
    vmem = pl.BlockSpec(memory_space=pltpu.VMEM)
    dma = pltpu.SemaphoreType.DMA
    gc, gp, gw = pl.pallas_call(
        kernel,
        in_specs=[pl.BlockSpec(memory_space=pltpu.SMEM)] + [vmem] * 5,
        out_specs=[vmem] * 3,
        out_shape=[
            jax.ShapeDtypeStruct((2, 8, 128, 256), BF),
            jax.ShapeDtypeStruct((2, 8, 128, 256), BF),
            jax.ShapeDtypeStruct((8, 16, 256), F32),
        ],
        scratch_shapes=[
            pltpu.VMEM((2, 8, 16, 256), BF),
            pltpu.VMEM((2, 8, 16, 256), BF),
            pltpu.VMEM((2, 4, 16, 128), BF),
            pltpu.VMEM((2, 4, 16, 128), BF),
            pltpu.VMEM((16, WIDE, 256), BF),
            pltpu.VMEM((8, WIDE, 128), BF),
            pltpu.VMEM((8, WIDE, 128), F32),
            pltpu.VMEM((2, 2, 8, WIDE, 256), BF),
            pltpu.VMEM((2, 2, 4, WIDE, 128), BF),
            pltpu.VMEM((2, 2, 4, WIDE, 128), BF),
            pltpu.VMEM((32, WIDE, 256), BF),
            pltpu.VMEM((32, WIDE, 256), BF),
            pltpu.VMEM((32, WIDE, 256), BF),
            pltpu.VMEM((32, WIDE, 256), BF),
            pltpu.VMEM((8, 16, 256), F32),
            pltpu.VMEM((8, 16, 256), F32),
            pltpu.VMEM((16, 16, 256), F32),
            pltpu.VMEM((8, 16, 256), F32),
            dma((2, 2)), dma((2, 2)), dma((2, 2, 2)), dma((2, 2, 2)),
            dma((8,)), dma((8,)), dma((16,)), dma((16,)), dma((8,)), dma((8,)),
        ],
        compiler_params=pltpu.CompilerParams(
            collective_id=0, has_side_effects=True, vmem_limit_bytes=56 << 20
        ),
        cost_estimate=pl.CostEstimate(
            flops=3_000_000_000, bytes_accessed=8 << 20, transcendentals=1_500_000
        ),
    )(shift, prev, cur, cot, w9, e)
    gw = gw.reshape(128, 16, 16)[:, :9, :9].reshape(128, 81)
    total = pairs * rows * lax.axis_size("row") * cols * lax.axis_size("col")
    return (
        gc.transpose(0, 3, 1, 2),
        gp.transpose(0, 3, 1, 2),
        gw * (1.0 / math.sqrt(total)),
    )


def solution(mesh):
    grid = P(None, None, "row", "col")
    return jax.shard_map(
        local,
        mesh=mesh,
        in_specs=(grid, grid, P(), P(), grid),
        out_specs=(grid, grid, P()),
        check_vma=False,
    )
```

```python
import functools
import math

import jax
import jax.numpy as jnp
import numpy as np
from jax import lax
from jax.experimental import pallas as pl
from jax.experimental.pallas import tpu as pltpu
from jax.sharding import PartitionSpec as P

BF = jnp.bfloat16
F32 = jnp.float32
MESH = pl.DeviceIdType.MESH
NT = (((1,), (1,)), ((), ()))
TN = (((0,), (0,)), ((), ()))
NN = (((1,), (0,)), ((), ()))
WIDE = 144


def dot(a, b, dims=NN):
    return lax.dot_general(a, b, dims, preferred_element_type=F32)


def iota(shape, axis):
    return lax.broadcasted_iota(jnp.int32, shape, axis)


def skew(x, shift):
    return pltpu.roll(x, shift % 256, 1, stride=1, stride_axis=0)


def flip8(x):
    idx = 7 - iota((8, 128), 0)
    parts = [
        jnp.take_along_axis(x[:, at : at + 128], idx, axis=0) for at in range(0, x.shape[1], 128)
    ]
    return parts[0] if len(parts) == 1 else jnp.concatenate(parts, axis=1)


def activation(vol_dot):
    half = vol_dot * (1.0 / 32.0)
    q = 1.0 + jnp.tanh(half)
    act = half * q
    return act, q + act * (2.0 - q)


def cell_block(p, bb, rows_of, cur_ref):
    at = pl.multiple_of(bb * 16, 16)
    cur = cur_ref[p, :, pl.ds(at, 16), :].reshape(128, 256)
    rows = [rows_of(i, at) for i in range(8)]
    win = jnp.concatenate([r[0:16] for r in rows] + [r[8:24] for r in rows], axis=0)
    return win, dot(cur, win, NT)


def split_product(grads, win):
    zero = jnp.zeros((8, 128), F32)
    full = [
        jnp.concatenate([zero, g] if i % 2 else [g, zero], axis=1) for i, g in enumerate(grads)
    ]
    return dot(jnp.concatenate(full, axis=0).astype(BF), win)


def cells_early(p, bb, dy, own, cur_ref, cot_ref, wk, sum_c, act_c, pre_c):
    win, vol = cell_block(p, bb, lambda i, at: own[i, pl.ds(at, 32), :], cur_ref)
    at = pl.multiple_of(bb * 16, 16)
    pre = dot(cot_ref[p, :, pl.ds(at, 16), :].reshape(128, 128), wk)
    grads, acts, rest = [], [], []
    for i in range(16):
        y, odd = divmod(i, 2)
        rows = slice(8 * i, 8 * i + 8)
        act, slope = activation(vol[rows, 128 * odd : 128 * odd + 128])
        piece = skew(pre[rows], 16 * y)
        grads.append(piece[:, :128] * slope)
        rest.append(piece[:, 128:])
        acts.append(flip8(act))
    act_c[p, bb] = jnp.concatenate(acts, axis=0)
    pre_c[p, bb] = jnp.concatenate(rest, axis=0)
    sum_c[p, bb] = split_product(grads, win)


def cells_late(p, bb, dy, halo, cur_ref, cot_ref, sum_c, act_c, pre_c, out_ref, acc_ref):
    def rows_of(i, at):
        return halo[jnp.where(i < 4 + dy, 8 + i, i), pl.ds(at, 32), :]

    win, vol = cell_block(p, bb, rows_of, cur_ref)
    at = pl.multiple_of(bb * 16, 16)
    cot = cot_ref[p, :, pl.ds(at, 16), :].reshape(128, 128).astype(F32)
    cot_rev = jnp.concatenate([flip8(cot[8 * i : 8 * i + 8]) for i in range(16)], axis=0)
    act_own, pre = act_c[p, bb], pre_c[p, bb]
    grads, acts = [], []
    for i in range(16):
        y, odd = divmod(i, 2)
        rows = slice(8 * i, 8 * i + 8)
        act, slope = activation(vol[rows, 128 * odd : 128 * odd + 128])
        grads.append(pre[rows] * slope)
        act = jnp.concatenate([act_own[rows], flip8(act)], axis=1)
        acts.append(skew(act, 249 - 16 * y))
    act = jnp.concatenate(acts, axis=0).astype(BF)
    acc_ref[p] += dot(cot_rev.astype(BF), act, TN)
    out = sum_c[p, bb] + split_product(grads, win)
    out_ref[p, :, pl.ds(at, 16), :] = out.astype(BF).reshape(8, 16, 256)


def position_block(p, bb, rows_of, pres_of, half_of, prev_ref, spread, masks):
    at = pl.multiple_of(bb * 16, 16)
    prev = prev_ref[p, :, pl.ds(at, 16), :].reshape(128, 256)
    win = jnp.concatenate([rows_of(i, at)[:24] for i in range(8)], axis=0)
    vol = dot(win, prev, NT)
    pre = dot(jnp.concatenate([pres_of(i, at)[:24] for i in range(8)], axis=0), spread)
    grads = []
    for i in range(8):
        for g in range(3):
            rows = slice(24 * i + 8 * g, 24 * i + 8 * g + 8)
            piece = pre[rows]
            if g != 1:
                piece = piece * masks[g // 2]
            piece = skew(piece, 16 * i + 8 * (g - 1))
            grads.append(half_of(i, piece) * activation(vol[rows])[1])
    return dot(jnp.concatenate(grads, axis=0).astype(BF), win, TN)


def positions_early(p, bb, dy, own, own_cot, prev_ref, wk, masks, sum_p):
    sum_p[p, bb] = position_block(
        p, bb, lambda i, at: own[8 + i, pl.ds(at, 32), :],
        lambda i, at: own_cot[i, pl.ds(at, 32), :], lambda i, x: x[:, :128],
        prev_ref, wk, masks,
    )


def positions_late(p, bb, dy, halo, pre_halo, prev_ref, e, masks, sum_p, out_ref):
    out = sum_p[p, bb] + position_block(
        p, bb, lambda i, at: halo[jnp.where(i < 4 + dy, i, 8 + i), pl.ds(at, 32), :],
        lambda i, at: pre_halo[i, pl.ds(at, 32), :],
        lambda i, x: jnp.where(i < 4 + dy, x[:, 128:], x[:, :128]),
        prev_ref, e, masks,
    )
    at = pl.multiple_of(bb * 16, 16)
    out_ref[p, :, pl.ds(at, 16), :] = out.astype(BF).reshape(8, 16, 256)


def kernel(
    norm, shift_ref, prev_ref, cur_ref, cot_ref, w_ref, e_ref, eye_ref,
    gc_ref, gp_ref, gw_ref,
    edge_s, edge_r, edge_cot_s, edge_cot_r, own0, own1, own_cot0, own_cot1, own_pre,
    msg, tri_s, tri_r, halo0, halo1, pre_halo0, pre_halo1,
    sum_c, act_c, pre_c, sum_p, acc, ar0, ar1, ar2, ar3,
    side_ss, side_rs, row_ss, row_rs, s1, r1, s2, r2, s3, r3,
):
    row, col = lax.axis_index("row"), lax.axis_index("col")
    last = lax.axis_size("row") - 1
    left = col == 0
    owns, own_cots = (own0, own1), (own_cot0, own_cot1)
    halos, pre_halos = (halo0, halo1), (pre_halo0, pre_halo1)
    g1, g2 = (row % 4) * 2 + col, row // 4

    def member(a, b):
        return (b * 4 + a // 2, a % 2)

    barrier = pltpu.get_barrier_semaphore()

    def greet(target):
        pl.semaphore_signal(barrier, inc=1, device_id=target, device_id_type=MESH)

    for d in range(1, 8):
        greet(member((g1 + d) % 8, g2))
    for d in range(1, 16):
        greet(member(g1, (g2 + d) % 16))
    greet(((row + 1) % (last + 1), col))
    greet(((row + last) % (last + 1), col))

    def side(p, k):
        s, r = ((edge_s, edge_r), (edge_cot_s, edge_cot_r))[k]
        return pltpu.make_async_remote_copy(
            src_ref=s.at[p], dst_ref=r.at[p], send_sem=side_ss.at[p, k],
            recv_sem=side_rs.at[p, k], device_id=(row, 1 - col), device_id_type=MESH,
        )

    def along(p, way, k):
        if k == 0:
            src, dst = msg.at[p, way], halos[p].at[pl.ds(0 if way else 8, 8)]
        else:
            src, dst = tri_s.at[p, way], tri_r.at[p, way]
        target = jnp.where(row == last, row, row + 1) if way else jnp.where(row == 0, row, row - 1)
        return pltpu.make_async_remote_copy(
            src_ref=src, dst_ref=dst, send_sem=row_ss.at[p, way, k],
            recv_sem=row_rs.at[p, way, k], device_id=(target, col), device_id_type=MESH,
        )

    start = jnp.where(left, 112, 0)
    for p in range(2):
        for y in range(8):
            pick = []
            for ref in (prev_ref, cur_ref):
                tile = ref[p, y, pl.ds(pl.multiple_of(start, 16), 16), :].astype(F32)
                pick.append(jnp.where(left, tile[8:], tile[:8]))
            edge_s[p, y] = jnp.concatenate(pick, axis=0).astype(BF)
        for y in range(0, 8, 2):
            pick = []
            for yy in (y, y + 1):
                tile = cot_ref[p, yy, pl.ds(pl.multiple_of(start, 16), 16), :].astype(F32)
                pick.append(jnp.where(left, tile[8:], tile[:8]))
            edge_cot_s[p, y // 2] = jnp.concatenate(pick, axis=0).astype(BF)
    pl.semaphore_wait(barrier, 24)
    for p in range(2):
        for k in range(2):
            side(p, k).start()

    w81 = w_ref[...]
    e = e_ref[...]
    w9 = dot(w81, eye_ref[...], TN).astype(BF)
    wk = dot(w9, e)
    turns = [(16 * (shift_ref[p, 0] + 12)) % 256 for p in range(2)]
    back = [(16 * (4 - shift_ref[p, 0])) % 256 for p in range(2)]
    wks = [pltpu.roll(wk, turns[p], 1).astype(BF) for p in range(2)]
    sub, lane = iota((8, 256), 0), iota((8, 256), 1) % 16
    masks = (jnp.where(lane >= 8 - sub, 1.0, 0.0), jnp.where(lane < 8 - sub, 1.0, 0.0))
    out_at, in_at = iota((WIDE, WIDE), 0), iota((WIDE, WIDE), 1)
    far = jnp.where(left, 136, 0)
    tri_lane = iota((WIDE, 128), 1)
    acc[...] = jnp.zeros_like(acc)

    def aligner(offset, slots):
        at = jnp.where(in_at < 128, in_at + 8, in_at - 128 - slots + far)
        ok = (in_at < 128) | ((in_at >= 128 + slots) & (in_at < 136 + slots))
        return jnp.where(ok & (at == out_at + offset), 1.0, 0.0).astype(BF)

    for p in range(2):
        dy, dx = shift_ref[p, 0], shift_ref[p, 1]
        own, own_cot = owns[p], own_cots[p]
        align_p, align_c0, align_c1 = aligner(4 + dx, 0), aligner(4 - dx, 0), aligner(4 - dx, 8)
        for k in range(2):
            side(p, k).wait()
        for y in range(8):
            edge = edge_r[p, y]
            own[y] = dot(align_p, jnp.concatenate([prev_ref[p, y], edge], axis=0)).astype(BF)
            own[8 + y] = dot(align_c1, jnp.concatenate([cur_ref[p, y], edge], axis=0)).astype(BF)
            align = align_c1 if y % 2 else align_c0
            both = jnp.concatenate([cot_ref[p, y], edge_cot_r[p, y // 2]], axis=0)
            aligned = dot(align, both).astype(BF)
            own_cot[y] = aligned
            own_pre[y] = dot(aligned, w9)

        def pack(s, carry):
            msg[p, 0, s] = own[jnp.where(s < 4 + dy, s, 4 + s - dy)]
            msg[p, 1, s] = own[jnp.where(s < 4 + dy, 12 + s - dy, s)]
            return carry

        lax.fori_loop(0, 8, pack, 0)

        def cell_row(t):
            return own_pre[jnp.where(t < 4 + dy, t + 4 - dy, t - 4 - dy)]

        for s in range(4):
            near, away = cell_row(s), cell_row(7 - s)
            tri_s[p, 1, s] = jnp.where(
                tri_lane >= 9 * (8 - s), near, pltpu.roll(away, 128 - 9 * (s + 1), 1)
            ).astype(BF)
            tri_s[p, 0, s] = jnp.where(
                tri_lane < 9 * (8 - s), near, pltpu.roll(away, 9 * (8 - s), 1)
            ).astype(BF)

        @pl.when(row > 0)
        def _():
            for k in range(2):
                along(p, 0, k).start()

        @pl.when(row < last)
        def _():
            for k in range(2):
                along(p, 1, k).start()

    def arrive(p):
        dy = shift_ref[p, 0]
        halo = halos[p]

        @pl.when(row > 0)
        def _():
            for k in range(2):
                along(p, 1, k).wait_recv()

        @pl.when(row == 0)
        def _():
            halo[0:8] = jnp.zeros((8, WIDE, 256), BF)
            tri_r[p, 1] = jnp.zeros((4, WIDE, 128), BF)

        @pl.when(row < last)
        def _():
            for k in range(2):
                along(p, 0, k).wait_recv()

        @pl.when(row == last)
        def _():
            halo[8:16] = jnp.zeros((8, WIDE, 256), BF)
            tri_r[p, 0] = jnp.zeros((4, WIDE, 128), BF)

        for s in range(4):
            up, down = tri_r[p, 0, s].astype(F32), tri_r[p, 1, s].astype(F32)
            pre_halos[p][s] = jnp.where(s < 4 + dy, down, up).astype(BF)
            down = pltpu.roll(down, 9 * (s + 1), 1)
            up = pltpu.roll(up, 128 - 9 * (8 - s), 1)
            pre_halos[p][7 - s] = jnp.where(7 - s < 4 + dy, down, up).astype(BF)

    def loop(lo, hi, work):
        def body(bb, carry):
            work(bb)
            return carry

        lax.fori_loop(lo, hi, body, 0)

    def early(p):
        dy = shift_ref[p, 0]
        loop(0, 8, lambda bb: cells_early(
            p, bb, dy, owns[p], cur_ref, cot_ref, wks[p], sum_c, act_c, pre_c))
        loop(0, 8, lambda bb: positions_early(
            p, bb, dy, owns[p], own_cots[p], prev_ref, wks[p], masks, sum_p))

    def late_cells(p):
        dy = shift_ref[p, 0]
        loop(0, 8, lambda bb: cells_late(
            p, bb, dy, halos[p], cur_ref, cot_ref, sum_c, act_c, pre_c, gc_ref, acc))

    def late_positions(p, lo, hi):
        dy = shift_ref[p, 0]
        loop(lo, hi, lambda bb: positions_late(
            p, bb, dy, halos[p], pre_halos[p], prev_ref, e, masks, sum_p, gp_ref))

    early(0)
    early(1)
    arrive(0)
    late_cells(0)
    late_positions(0, 0, 8)
    arrive(1)
    late_cells(1)

    turned = (pltpu.roll(acc[0], back[0], 1) + pltpu.roll(acc[1], back[1], 1)).T
    for u in range(9):
        ar0[9 * u : 9 * u + 9] = turned[16 * u : 16 * u + 9]
    ar0[81:128] = jnp.zeros((47, 128), F32)

    def share(ref, i):
        return ref.at[pl.ds(pl.multiple_of(i * 16, 16), 16)]

    def first(d):
        peer = (g1 + d) % 8
        return pltpu.make_async_remote_copy(
            src_ref=share(ar0, peer), dst_ref=ar1.at[g1], send_sem=s1.at[peer],
            recv_sem=r1.at[g1], device_id=member(peer, g2), device_id_type=MESH,
        )

    def second(d):
        peer = (g2 + d) % 16
        return pltpu.make_async_remote_copy(
            src_ref=ar2.at[g2], dst_ref=ar2.at[g2], send_sem=s2.at[peer],
            recv_sem=r2.at[g2], device_id=member(g1, peer), device_id_type=MESH,
        )

    def third(d):
        peer = (g1 + d) % 8
        return pltpu.make_async_remote_copy(
            src_ref=ar3.at[g1], dst_ref=ar3.at[g1], send_sem=s3.at[peer],
            recv_sem=r3.at[g1], device_id=member(peer, g2), device_id_type=MESH,
        )

    def got(buffer, sends, receives, source):
        pltpu.make_async_remote_copy(
            src_ref=buffer.at[source], dst_ref=buffer.at[source], send_sem=sends.at[source],
            recv_sem=receives.at[source], device_id=(row, 1 - col), device_id_type=MESH,
        ).wait_recv()

    for d in range(1, 8):
        first(d).start()
    late_positions(1, 0, 3)
    ar1[g1] = ar0[pl.ds(pl.multiple_of(g1 * 16, 16), 16)]
    for d in range(1, 8):
        first(d).wait_send()
        got(ar1, s1, r1, (g1 + d) % 8)
    ar2[g2] = jnp.sum(ar1[...], axis=0)
    for d in range(1, 16):
        second(d).start()
    late_positions(1, 3, 6)
    for d in range(1, 16):
        second(d).wait_send()
        got(ar2, s2, r2, (g2 + d) % 16)
    ar3[g1] = jnp.sum(ar2[...], axis=0)
    for d in range(1, 8):
        third(d).start()
    late_positions(1, 6, 8)
    for d in range(1, 8):
        third(d).wait_send()
        got(ar3, s3, r3, (g1 + d) % 8)
    gw_ref[...] = ar3[...].reshape(128, 128)[:81] * norm

    for p in range(2):
        for k in range(2):

            @pl.when(row > 0)
            def _():
                along(p, 0, k).wait_send()

            @pl.when(row < last)
            def _():
                along(p, 1, k).wait_send()


def spread_matrix():
    e = np.zeros((128, 256), np.float32)
    for u in range(9):
        for v in range(9):
            e[9 * u + v, 16 * u + v] = 1.0 / 32.0
    return e


def local(current, previous, shift, weight, cotangent):
    pairs, channels, rows, cols = current.shape
    prev = previous.transpose(0, 2, 3, 1)
    cur = current.transpose(0, 2, 3, 1)
    cot = cotangent.transpose(0, 2, 3, 1)
    e = jnp.asarray(spread_matrix(), BF)
    eye = jnp.asarray(np.eye(81, 128), BF)
    total = pairs * rows * lax.axis_size("row") * cols * lax.axis_size("col")
    vmem = pl.BlockSpec(memory_space=pltpu.VMEM)
    dma = pltpu.SemaphoreType.DMA
    v = pltpu.VMEM
    gc, gp, gw = pl.pallas_call(
        functools.partial(kernel, 1.0 / math.sqrt(total)),
        in_specs=[pl.BlockSpec(memory_space=pltpu.SMEM)] + [vmem] * 6,
        out_specs=[vmem] * 3,
        out_shape=[
            jax.ShapeDtypeStruct((2, 8, 128, 256), BF),
            jax.ShapeDtypeStruct((2, 8, 128, 256), BF),
            jax.ShapeDtypeStruct((81, 128), F32),
        ],
        scratch_shapes=[
            v((2, 8, 16, 256), BF), v((2, 8, 16, 256), BF),
            v((2, 4, 16, 128), BF), v((2, 4, 16, 128), BF),
            v((16, WIDE, 256), BF), v((16, WIDE, 256), BF),
            v((8, WIDE, 128), BF), v((8, WIDE, 128), BF),
            v((8, WIDE, 128), F32),
            v((2, 2, 8, WIDE, 256), BF),
            v((2, 2, 4, WIDE, 128), BF), v((2, 2, 4, WIDE, 128), BF),
            v((16, WIDE, 256), BF), v((16, WIDE, 256), BF),
            v((8, WIDE, 128), BF), v((8, WIDE, 128), BF),
            v((2, 8, 128, 256), F32),
            v((2, 8, 128, 128), F32), v((2, 8, 128, 128), F32),
            v((2, 8, 128, 256), F32),
            v((2, 128, 256), F32),
            v((128, 128), F32), v((8, 16, 128), F32), v((16, 16, 128), F32), v((8, 16, 128), F32),
            dma((2, 2)), dma((2, 2)), dma((2, 2, 2)), dma((2, 2, 2)),
            dma((8,)), dma((8,)), dma((16,)), dma((16,)), dma((8,)), dma((8,)),
        ],
        compiler_params=pltpu.CompilerParams(
            collective_id=0, has_side_effects=True, vmem_limit_bytes=56 << 20
        ),
        cost_estimate=pl.CostEstimate(
            flops=3_000_000_000, bytes_accessed=8 << 20, transcendentals=1_500_000
        ),
    )(shift, prev, cur, cot, weight.T, e, eye)
    return gc.transpose(0, 3, 1, 2), gp.transpose(0, 3, 1, 2), gw.T


def solution(mesh):
    grid = P(None, None, "row", "col")
    return jax.shard_map(
        local,
        mesh=mesh,
        in_specs=(grid, grid, P(), P(), grid),
        out_specs=(grid, grid, P()),
        check_vma=False,
    )
```

```python
import functools
import math

import jax
import jax.numpy as jnp
import numpy as np
from jax import lax
from jax.experimental import pallas as pl
from jax.experimental.pallas import tpu as pltpu
from jax.sharding import PartitionSpec as P

BF = jnp.bfloat16
F32 = jnp.float32
MESH = pl.DeviceIdType.MESH
NT = (((1,), (1,)), ((), ()))
TN = (((0,), (0,)), ((), ()))
NN = (((1,), (0,)), ((), ()))
WIDE = 144


def dot(a, b, dims=NN):
    return lax.dot_general(a, b, dims, preferred_element_type=F32)


def iota(shape, axis):
    return lax.broadcasted_iota(jnp.int32, shape, axis)


def skew(x, shift):
    return pltpu.roll(x, shift % 256, 1, stride=1, stride_axis=0)


def flip8(x):
    idx = 7 - iota((8, 128), 0)
    parts = [
        jnp.take_along_axis(x[:, at : at + 128], idx, axis=0) for at in range(0, x.shape[1], 128)
    ]
    return parts[0] if len(parts) == 1 else jnp.concatenate(parts, axis=1)


def activation(vol_dot):
    half = vol_dot * (1.0 / 32.0)
    q = 1.0 + jnp.tanh(half)
    act = half * q
    return act, q + act * (2.0 - q)


def cell_block(p, bb, rows_of, cur_ref):
    at = pl.multiple_of(bb * 16, 16)
    cur = cur_ref[p, :, pl.ds(at, 16), :].reshape(128, 256)
    rows = [rows_of(i, at) for i in range(8)]
    win = jnp.concatenate([r[0:16] for r in rows] + [r[8:24] for r in rows], axis=0)
    return win, dot(cur, win, NT)


def split_product(grads, win):
    zero = jnp.zeros((8, 128), F32)
    full = [
        jnp.concatenate([zero, g] if i % 2 else [g, zero], axis=1) for i, g in enumerate(grads)
    ]
    return dot(jnp.concatenate(full, axis=0).astype(BF), win)


def cells_early(p, bb, dy, own, cur_ref, cot_ref, wk, sum_c, act_c, pre_c):
    win, vol = cell_block(p, bb, lambda i, at: own[i, pl.ds(at, 32), :], cur_ref)
    at = pl.multiple_of(bb * 16, 16)
    pre = dot(cot_ref[p, :, pl.ds(at, 16), :].reshape(128, 128), wk)
    grads, acts, rest = [], [], []
    for i in range(16):
        y, odd = divmod(i, 2)
        rows = slice(8 * i, 8 * i + 8)
        act, slope = activation(vol[rows, 128 * odd : 128 * odd + 128])
        piece = skew(pre[rows], 16 * y)
        grads.append(piece[:, :128] * slope)
        rest.append(piece[:, 128:])
        acts.append(flip8(act))
    act_c[p, bb] = jnp.concatenate(acts, axis=0)
    pre_c[p, bb] = jnp.concatenate(rest, axis=0)
    sum_c[p, bb] = split_product(grads, win)


def cells_late(p, bb, dy, halo, cur_ref, cot_ref, sum_c, act_c, pre_c, out_ref, acc_ref):
    def rows_of(i, at):
        return halo[jnp.where(i < 4 + dy, 8 + i, i), pl.ds(at, 32), :]

    win, vol = cell_block(p, bb, rows_of, cur_ref)
    at = pl.multiple_of(bb * 16, 16)
    cot = cot_ref[p, :, pl.ds(at, 16), :].reshape(128, 128).astype(F32)
    cot_rev = jnp.concatenate([flip8(cot[8 * i : 8 * i + 8]) for i in range(16)], axis=0)
    act_own, pre = act_c[p, bb], pre_c[p, bb]
    grads, acts = [], []
    for i in range(16):
        y, odd = divmod(i, 2)
        rows = slice(8 * i, 8 * i + 8)
        act, slope = activation(vol[rows, 128 * odd : 128 * odd + 128])
        grads.append(pre[rows] * slope)
        act = jnp.concatenate([act_own[rows], flip8(act)], axis=1)
        acts.append(skew(act, 249 - 16 * y))
    act = jnp.concatenate(acts, axis=0).astype(BF)
    acc_ref[p] += dot(cot_rev.astype(BF), act, TN)
    out = sum_c[p, bb] + split_product(grads, win)
    out_ref[p, :, pl.ds(at, 16), :] = out.astype(BF).reshape(8, 16, 256)


def position_block(p, bb, rows_of, pres_of, half_of, prev_ref, spread, masks):
    at = pl.multiple_of(bb * 16, 16)
    prev = prev_ref[p, :, pl.ds(at, 16), :].reshape(128, 256)
    win = jnp.concatenate([rows_of(i, at)[:24] for i in range(8)], axis=0)
    vol = dot(win, prev, NT)
    pre = dot(jnp.concatenate([pres_of(i, at)[:24] for i in range(8)], axis=0), spread)
    grads = []
    for i in range(8):
        for g in range(3):
            rows = slice(24 * i + 8 * g, 24 * i + 8 * g + 8)
            piece = pre[rows]
            if g != 1:
                piece = piece * masks[g // 2]
            piece = skew(piece, 16 * i + 8 * (g - 1))
            grads.append(half_of(i, piece) * activation(vol[rows])[1])
    return dot(jnp.concatenate(grads, axis=0).astype(BF), win, TN)


def positions_early(p, bb, dy, own, own_cot, prev_ref, wk, masks, sum_p):
    sum_p[p, bb] = position_block(
        p, bb, lambda i, at: own[8 + i, pl.ds(at, 32), :],
        lambda i, at: own_cot[i, pl.ds(at, 32), :], lambda i, x: x[:, :128],
        prev_ref, wk, masks,
    )


def positions_late(p, bb, dy, halo, pre_halo, prev_ref, e, masks, sum_p, out_ref):
    out = sum_p[p, bb] + position_block(
        p, bb, lambda i, at: halo[jnp.where(i < 4 + dy, i, 8 + i), pl.ds(at, 32), :],
        lambda i, at: pre_halo[i, pl.ds(at, 32), :],
        lambda i, x: jnp.where(i < 4 + dy, x[:, 128:], x[:, :128]),
        prev_ref, e, masks,
    )
    at = pl.multiple_of(bb * 16, 16)
    out_ref[p, :, pl.ds(at, 16), :] = out.astype(BF).reshape(8, 16, 256)


def kernel(
    norm, shift_ref, prev_ref, cur_ref, cot_ref, w_ref, e_ref, eye_ref,
    gc_ref, gp_ref, gw_ref,
    edge_s, edge_r, edge_cot_s, edge_cot_r, own0, own1, own_cot0, own_cot1, own_pre,
    msg, tri_s, tri_r, halo0, halo1, pre_halo0, pre_halo1,
    sum_c, act_c, pre_c, sum_p, acc, ar0, ar1, ar2, ar3,
    side_ss, side_rs, row_ss, row_rs, s1, r1, s2, r2, s3, r3,
):
    row, col = lax.axis_index("row"), lax.axis_index("col")
    last = lax.axis_size("row") - 1
    left = col == 0
    owns, own_cots = (own0, own1), (own_cot0, own_cot1)
    halos, pre_halos = (halo0, halo1), (pre_halo0, pre_halo1)
    g1, g2 = (row % 4) * 2 + col, row // 4

    def member(a, b):
        return (b * 4 + a // 2, a % 2)

    barrier = pltpu.get_barrier_semaphore()

    def greet(target):
        pl.semaphore_signal(barrier, inc=1, device_id=target, device_id_type=MESH)

    for d in range(1, 8):
        greet(member((g1 + d) % 8, g2))
    for d in range(1, 16):
        greet(member(g1, (g2 + d) % 16))
    greet(((row + 1) % (last + 1), col))
    greet(((row + last) % (last + 1), col))

    def side(p, k):
        s, r = ((edge_s, edge_r), (edge_cot_s, edge_cot_r))[k]
        return pltpu.make_async_remote_copy(
            src_ref=s.at[p], dst_ref=r.at[p], send_sem=side_ss.at[p, k],
            recv_sem=side_rs.at[p, k], device_id=(row, 1 - col), device_id_type=MESH,
        )

    def along(p, way, k):
        if k == 0:
            src, dst = msg.at[p, way], halos[p].at[pl.ds(0 if way else 8, 8)]
        else:
            src, dst = tri_s.at[p, way], tri_r.at[p, way]
        target = jnp.where(row == last, row, row + 1) if way else jnp.where(row == 0, row, row - 1)
        return pltpu.make_async_remote_copy(
            src_ref=src, dst_ref=dst, send_sem=row_ss.at[p, way, k],
            recv_sem=row_rs.at[p, way, k], device_id=(target, col), device_id_type=MESH,
        )

    start = jnp.where(left, 112, 0)
    for p in range(2):
        for y in range(8):
            pick = []
            for ref in (prev_ref, cur_ref):
                tile = ref[p, y, pl.ds(pl.multiple_of(start, 16), 16), :].astype(F32)
                pick.append(jnp.where(left, tile[8:], tile[:8]))
            edge_s[p, y] = jnp.concatenate(pick, axis=0).astype(BF)
        for y in range(0, 8, 2):
            pick = []
            for yy in (y, y + 1):
                tile = cot_ref[p, yy, pl.ds(pl.multiple_of(start, 16), 16), :].astype(F32)
                pick.append(jnp.where(left, tile[8:], tile[:8]))
            edge_cot_s[p, y // 2] = jnp.concatenate(pick, axis=0).astype(BF)
    pl.semaphore_wait(barrier, 24)
    for p in range(2):
        for k in range(2):
            side(p, k).start()

    w81 = w_ref[...]
    e = e_ref[...]
    w9 = dot(w81, eye_ref[...], TN).astype(BF)
    wk = dot(w9, e)
    turns = [(16 * (shift_ref[p, 0] + 12)) % 256 for p in range(2)]
    back = [(16 * (4 - shift_ref[p, 0])) % 256 for p in range(2)]
    wks = [pltpu.roll(wk, turns[p], 1).astype(BF) for p in range(2)]
    sub, lane = iota((8, 256), 0), iota((8, 256), 1) % 16
    masks = (jnp.where(lane >= 8 - sub, 1.0, 0.0), jnp.where(lane < 8 - sub, 1.0, 0.0))
    out_at, in_at = iota((WIDE, WIDE), 0), iota((WIDE, WIDE), 1)
    far = jnp.where(left, 136, 0)
    tri_lane = iota((WIDE, 128), 1)
    acc[...] = jnp.zeros_like(acc)

    def aligner(offset, slots):
        at = jnp.where(in_at < 128, in_at + 8, in_at - 128 - slots + far)
        ok = (in_at < 128) | ((in_at >= 128 + slots) & (in_at < 136 + slots))
        return jnp.where(ok & (at == out_at + offset), 1.0, 0.0).astype(BF)

    for p in range(2):
        dy, dx = shift_ref[p, 0], shift_ref[p, 1]
        own, own_cot = owns[p], own_cots[p]
        align_p, align_c0, align_c1 = aligner(4 + dx, 0), aligner(4 - dx, 0), aligner(4 - dx, 8)
        for k in range(2):
            side(p, k).wait()
        for y in range(8):
            edge = edge_r[p, y]
            own[y] = dot(align_p, jnp.concatenate([prev_ref[p, y], edge], axis=0)).astype(BF)
            own[8 + y] = dot(align_c1, jnp.concatenate([cur_ref[p, y], edge], axis=0)).astype(BF)
            align = align_c1 if y % 2 else align_c0
            both = jnp.concatenate([cot_ref[p, y], edge_cot_r[p, y // 2]], axis=0)
            aligned = dot(align, both).astype(BF)
            own_cot[y] = aligned
            own_pre[y] = dot(aligned, w9)

        def pack(s, carry):
            msg[p, 0, s] = own[jnp.where(s < 4 + dy, s, 4 + s - dy)]
            msg[p, 1, s] = own[jnp.where(s < 4 + dy, 12 + s - dy, s)]
            return carry

        lax.fori_loop(0, 8, pack, 0)

        def cell_row(t):
            return own_pre[jnp.where(t < 4 + dy, t + 4 - dy, t - 4 - dy)]

        for s in range(4):
            near, away = cell_row(s), cell_row(7 - s)
            tri_s[p, 1, s] = jnp.where(
                tri_lane >= 9 * (8 - s), near, pltpu.roll(away, 128 - 9 * (s + 1), 1)
            ).astype(BF)
            tri_s[p, 0, s] = jnp.where(
                tri_lane < 9 * (8 - s), near, pltpu.roll(away, 9 * (8 - s), 1)
            ).astype(BF)

        @pl.when(row > 0)
        def _():
            for k in range(2):
                along(p, 0, k).start()

        @pl.when(row < last)
        def _():
            for k in range(2):
                along(p, 1, k).start()

    def arrive(p):
        dy = shift_ref[p, 0]
        halo = halos[p]

        @pl.when(row > 0)
        def _():
            for k in range(2):
                along(p, 1, k).wait_recv()

        @pl.when(row == 0)
        def _():
            halo[0:8] = jnp.zeros((8, WIDE, 256), BF)
            tri_r[p, 1] = jnp.zeros((4, WIDE, 128), BF)

        @pl.when(row < last)
        def _():
            for k in range(2):
                along(p, 0, k).wait_recv()

        @pl.when(row == last)
        def _():
            halo[8:16] = jnp.zeros((8, WIDE, 256), BF)
            tri_r[p, 0] = jnp.zeros((4, WIDE, 128), BF)

        for s in range(4):
            up, down = tri_r[p, 0, s].astype(F32), tri_r[p, 1, s].astype(F32)
            pre_halos[p][s] = jnp.where(s < 4 + dy, down, up).astype(BF)
            down = pltpu.roll(down, 9 * (s + 1), 1)
            up = pltpu.roll(up, 128 - 9 * (8 - s), 1)
            pre_halos[p][7 - s] = jnp.where(7 - s < 4 + dy, down, up).astype(BF)

    def loop(lo, hi, work):
        def body(bb, carry):
            work(bb)
            return carry

        lax.fori_loop(lo, hi, body, 0)

    def early(p):
        dy = shift_ref[p, 0]

        def work(i):
            for bb in (2 * i, 2 * i + 1):
                cells_early(
                    p, bb, dy, owns[p], cur_ref, cot_ref, wks[p], sum_c, act_c, pre_c)
                positions_early(
                    p, bb, dy, owns[p], own_cots[p], prev_ref, wks[p], masks, sum_p)

        loop(0, 4, work)

    def late_cells(p, bb):
        cells_late(
            p, bb, shift_ref[p, 0], halos[p], cur_ref, cot_ref, sum_c, act_c, pre_c, gc_ref, acc)

    def late_positions(p, bb):
        positions_late(
            p, bb, shift_ref[p, 0], halos[p], pre_halos[p], prev_ref, e, masks, sum_p, gp_ref)

    def late(i):
        for bb in (2 * i, 2 * i + 1):
            late_cells(0, bb)
            late_positions(0, bb)

    early(0)
    early(1)
    arrive(0)
    loop(0, 4, late)
    arrive(1)
    loop(0, 2, lambda i: [late_cells(1, 4 * i + k) for k in range(4)])

    turned = (pltpu.roll(acc[0], back[0], 1) + pltpu.roll(acc[1], back[1], 1)).T
    for u in range(9):
        ar0[9 * u : 9 * u + 9] = turned[16 * u : 16 * u + 9]
    ar0[81:128] = jnp.zeros((47, 128), F32)

    def share(ref, i):
        return ref.at[pl.ds(pl.multiple_of(i * 16, 16), 16)]

    def first(d):
        peer = (g1 + d) % 8
        return pltpu.make_async_remote_copy(
            src_ref=share(ar0, peer), dst_ref=ar1.at[g1], send_sem=s1.at[peer],
            recv_sem=r1.at[g1], device_id=member(peer, g2), device_id_type=MESH,
        )

    def second(d):
        peer = (g2 + d) % 16
        return pltpu.make_async_remote_copy(
            src_ref=ar2.at[g2], dst_ref=ar2.at[g2], send_sem=s2.at[peer],
            recv_sem=r2.at[g2], device_id=member(g1, peer), device_id_type=MESH,
        )

    def third(d):
        peer = (g1 + d) % 8
        return pltpu.make_async_remote_copy(
            src_ref=ar3.at[g1], dst_ref=ar3.at[g1], send_sem=s3.at[peer],
            recv_sem=r3.at[g1], device_id=member(peer, g2), device_id_type=MESH,
        )

    def got(buffer, sends, receives, source):
        pltpu.make_async_remote_copy(
            src_ref=buffer.at[source], dst_ref=buffer.at[source], send_sem=sends.at[source],
            recv_sem=receives.at[source], device_id=(row, 1 - col), device_id_type=MESH,
        ).wait_recv()

    for d in range(1, 8):
        first(d).start()
    loop(0, 1, lambda i: [late_positions(1, k) for k in range(3)])
    ar1[g1] = ar0[pl.ds(pl.multiple_of(g1 * 16, 16), 16)]
    for d in range(1, 8):
        first(d).wait_send()
        got(ar1, s1, r1, (g1 + d) % 8)
    ar2[g2] = jnp.sum(ar1[...], axis=0)
    for d in range(1, 16):
        second(d).start()
    loop(0, 1, lambda i: [late_positions(1, 3 + k) for k in range(3)])
    for d in range(1, 16):
        second(d).wait_send()
        got(ar2, s2, r2, (g2 + d) % 16)
    ar3[g1] = jnp.sum(ar2[...], axis=0)
    for d in range(1, 8):
        third(d).start()
    loop(0, 1, lambda i: [late_positions(1, 6 + k) for k in range(2)])
    for d in range(1, 8):
        third(d).wait_send()
        got(ar3, s3, r3, (g1 + d) % 8)
    gw_ref[...] = ar3[...].reshape(128, 128)[:81] * norm

    for p in range(2):
        for k in range(2):

            @pl.when(row > 0)
            def _():
                along(p, 0, k).wait_send()

            @pl.when(row < last)
            def _():
                along(p, 1, k).wait_send()


def spread_matrix():
    e = np.zeros((128, 256), np.float32)
    for u in range(9):
        for v in range(9):
            e[9 * u + v, 16 * u + v] = 1.0 / 32.0
    return e


def local(current, previous, shift, weight, cotangent):
    pairs, channels, rows, cols = current.shape
    prev = previous.transpose(0, 2, 3, 1)
    cur = current.transpose(0, 2, 3, 1)
    cot = cotangent.transpose(0, 2, 3, 1)
    e = jnp.asarray(spread_matrix(), BF)
    eye = jnp.asarray(np.eye(81, 128), BF)
    total = pairs * rows * lax.axis_size("row") * cols * lax.axis_size("col")
    vmem = pl.BlockSpec(memory_space=pltpu.VMEM)
    dma = pltpu.SemaphoreType.DMA
    v = pltpu.VMEM
    gc, gp, gw = pl.pallas_call(
        functools.partial(kernel, 1.0 / math.sqrt(total)),
        in_specs=[pl.BlockSpec(memory_space=pltpu.SMEM)] + [vmem] * 6,
        out_specs=[vmem] * 3,
        out_shape=[
            jax.ShapeDtypeStruct((2, 8, 128, 256), BF),
            jax.ShapeDtypeStruct((2, 8, 128, 256), BF),
            jax.ShapeDtypeStruct((81, 128), F32),
        ],
        scratch_shapes=[
            v((2, 8, 16, 256), BF), v((2, 8, 16, 256), BF),
            v((2, 4, 16, 128), BF), v((2, 4, 16, 128), BF),
            v((16, WIDE, 256), BF), v((16, WIDE, 256), BF),
            v((8, WIDE, 128), BF), v((8, WIDE, 128), BF),
            v((8, WIDE, 128), F32),
            v((2, 2, 8, WIDE, 256), BF),
            v((2, 2, 4, WIDE, 128), BF), v((2, 2, 4, WIDE, 128), BF),
            v((16, WIDE, 256), BF), v((16, WIDE, 256), BF),
            v((8, WIDE, 128), BF), v((8, WIDE, 128), BF),
            v((2, 8, 128, 256), F32),
            v((2, 8, 128, 128), F32), v((2, 8, 128, 128), F32),
            v((2, 8, 128, 256), F32),
            v((2, 128, 256), F32),
            v((128, 128), F32), v((8, 16, 128), F32), v((16, 16, 128), F32), v((8, 16, 128), F32),
            dma((2, 2)), dma((2, 2)), dma((2, 2, 2)), dma((2, 2, 2)),
            dma((8,)), dma((8,)), dma((16,)), dma((16,)), dma((8,)), dma((8,)),
        ],
        compiler_params=pltpu.CompilerParams(
            collective_id=0, has_side_effects=True, vmem_limit_bytes=56 << 20
        ),
        cost_estimate=pl.CostEstimate(
            flops=3_000_000_000, bytes_accessed=8 << 20, transcendentals=1_500_000
        ),
    )(shift, prev, cur, cot, weight.T, e, eye)
    return gc.transpose(0, 3, 1, 2), gp.transpose(0, 3, 1, 2), gw.T


def solution(mesh):
    grid = P(None, None, "row", "col")
    return jax.shard_map(
        local,
        mesh=mesh,
        in_specs=(grid, grid, P(), P(), grid),
        out_specs=(grid, grid, P()),
        check_vma=False,
    )
```

```python
import functools
import math

import jax
import jax.numpy as jnp
import numpy as np
from jax import lax
from jax.experimental import pallas as pl
from jax.experimental.pallas import tpu as pltpu
from jax.sharding import PartitionSpec as P

BF = jnp.bfloat16
F32 = jnp.float32
MESH = pl.DeviceIdType.MESH
NT = (((1,), (1,)), ((), ()))
TN = (((0,), (0,)), ((), ()))
NN = (((1,), (0,)), ((), ()))
WIDE = 144


def dot(a, b, dims=NN):
    return lax.dot_general(a, b, dims, preferred_element_type=F32)


def iota(shape, axis):
    return lax.broadcasted_iota(jnp.int32, shape, axis)


def skew(x, shift):
    return pltpu.roll(x, shift % 256, 1, stride=1, stride_axis=0)


def flip8(x):
    idx = 7 - iota((8, 128), 0)
    parts = [
        jnp.take_along_axis(x[:, at : at + 128], idx, axis=0) for at in range(0, x.shape[1], 128)
    ]
    return parts[0] if len(parts) == 1 else jnp.concatenate(parts, axis=1)


def activation(vol_dot):
    half = vol_dot * (1.0 / 32.0)
    q = 1.0 + jnp.tanh(half)
    act = half * q
    return act, q + act * (2.0 - q)


def cell_block(p, bb, rows_of, cur_ref):
    at = pl.multiple_of(bb * 16, 16)
    cur = cur_ref[p, :, pl.ds(at, 16), :].reshape(128, 256)
    rows = [rows_of(i, at) for i in range(8)]
    win = jnp.concatenate([r[0:16] for r in rows] + [r[8:24] for r in rows], axis=0)
    return win, dot(cur, win, NT)


def split_product(grads, win):
    zero = jnp.zeros((8, 128), F32)
    full = [
        jnp.concatenate([zero, g] if i % 2 else [g, zero], axis=1) for i, g in enumerate(grads)
    ]
    return dot(jnp.concatenate(full, axis=0).astype(BF), win)


def cells_early(p, bb, dy, own, cur_ref, cot_ref, wk, sum_c, act_c, pre_c):
    win, vol = cell_block(p, bb, lambda i, at: own[i, pl.ds(at, 32), :], cur_ref)
    at = pl.multiple_of(bb * 16, 16)
    pre = dot(cot_ref[p, :, pl.ds(at, 16), :].reshape(128, 128), wk)
    grads, acts, rest = [], [], []
    for i in range(16):
        y, odd = divmod(i, 2)
        rows = slice(8 * i, 8 * i + 8)
        act, slope = activation(vol[rows, 128 * odd : 128 * odd + 128])
        piece = skew(pre[rows], 16 * y)
        grads.append(piece[:, :128] * slope)
        rest.append(piece[:, 128:])
        acts.append(flip8(act))
    act_c[p, bb] = jnp.concatenate(acts, axis=0)
    pre_c[p, bb] = jnp.concatenate(rest, axis=0)
    sum_c[p, bb] = split_product(grads, win)


def cells_late(p, bb, dy, halo, cur_ref, cot_ref, sum_c, act_c, pre_c, out_ref, acc_ref):
    def rows_of(i, at):
        return halo[i, pl.ds(at, 32), :]

    win, vol = cell_block(p, bb, rows_of, cur_ref)
    at = pl.multiple_of(bb * 16, 16)
    cot = cot_ref[p, :, pl.ds(at, 16), :].reshape(128, 128).astype(F32)
    cot_rev = jnp.concatenate([flip8(cot[8 * i : 8 * i + 8]) for i in range(16)], axis=0)
    act_own, pre = act_c[p, bb], pre_c[p, bb]
    grads, acts = [], []
    for i in range(16):
        y, odd = divmod(i, 2)
        rows = slice(8 * i, 8 * i + 8)
        act, slope = activation(vol[rows, 128 * odd : 128 * odd + 128])
        grads.append(pre[rows] * slope)
        act = jnp.concatenate([act_own[rows], flip8(act)], axis=1)
        acts.append(skew(act, 249 - 16 * y))
    act = jnp.concatenate(acts, axis=0).astype(BF)
    acc_ref[p] += dot(cot_rev.astype(BF), act, TN)
    out = sum_c[p, bb] + split_product(grads, win)
    out_ref[p, :, pl.ds(at, 16), :] = out.astype(BF).reshape(8, 16, 256)


def position_block(p, bb, rows_of, pres_of, half_of, prev_ref, spread, masks):
    at = pl.multiple_of(bb * 16, 16)
    prev = prev_ref[p, :, pl.ds(at, 16), :].reshape(128, 256)
    win = jnp.concatenate([rows_of(i, at)[:24] for i in range(8)], axis=0)
    vol = dot(win, prev, NT)
    pre = dot(jnp.concatenate([pres_of(i, at)[:24] for i in range(8)], axis=0), spread)
    grads = []
    for i in range(8):
        for g in range(3):
            rows = slice(24 * i + 8 * g, 24 * i + 8 * g + 8)
            piece = pre[rows]
            if g != 1:
                piece = piece * masks[g // 2]
            piece = skew(piece, 16 * i + 8 * (g - 1))
            grads.append(half_of(i, piece) * activation(vol[rows])[1])
    return dot(jnp.concatenate(grads, axis=0).astype(BF), win, TN)


def positions_early(p, bb, dy, own, own_cot, prev_ref, wk, masks, sum_p):
    sum_p[p, bb] = position_block(
        p, bb, lambda i, at: own[8 + i, pl.ds(at, 32), :],
        lambda i, at: own_cot[i, pl.ds(at, 32), :], lambda i, x: x[:, :128],
        prev_ref, wk, masks,
    )


def positions_late(p, bb, dy, halo, pre_halo, prev_ref, e, masks, sum_p, out_ref):
    out = sum_p[p, bb] + position_block(
        p, bb, lambda i, at: halo[8 + i, pl.ds(at, 32), :],
        lambda i, at: pre_halo[i, pl.ds(at, 32), :],
        lambda i, x: jnp.where(i < 4 + dy, x[:, 128:], x[:, :128]),
        prev_ref, e, masks,
    )
    at = pl.multiple_of(bb * 16, 16)
    out_ref[p, :, pl.ds(at, 16), :] = out.astype(BF).reshape(8, 16, 256)


def kernel(
    norm, shift_ref, prev_in, cur_in, cot_in, w_ref, e_ref, eye_ref,
    gc_ref, gp_ref, gw_ref,
    prev_ref, cur_ref, cot_ref, flat0, flat1, msg_r, rim_s, rim_r,
    edge_s, edge_r0, edge_r1, edge_cot_s, edge_cot_r, own0, own1, own_cot0, own_cot1, own_pre,
    msg, tri_s, tri_r, halo0, halo1, pre_halo0, pre_halo1,
    sum_c, act_c, pre_c, sum_p, acc, ar0, ar1, ar2, ar3,
    side_ss, side_rs, row_ss, row_rs, s1, r1, s2, r2, s3, r3,
):
    row, col = lax.axis_index("row"), lax.axis_index("col")
    last = lax.axis_size("row") - 1
    left = col == 0
    owns, own_cots = (own0, own1), (own_cot0, own_cot1)
    halos, pre_halos = (halo0, halo1), (pre_halo0, pre_halo1)
    g1, g2 = (row % 4) * 2 + col, row // 4

    def member(a, b):
        return (b * 4 + a // 2, a % 2)

    barrier = pltpu.get_barrier_semaphore()

    def greet(target):
        pl.semaphore_signal(barrier, inc=1, device_id=target, device_id_type=MESH)

    for d in range(1, 8):
        greet(member((g1 + d) % 8, g2))
    for d in range(1, 16):
        greet(member(g1, (g2 + d) % 16))
    greet(((row + 1) % (last + 1), col))
    greet(((row + last) % (last + 1), col))

    def side(p, k):
        src, dst = (
            (edge_s.at[p], (edge_r0, edge_r1)[p]), (edge_cot_s.at[p], edge_cot_r.at[p])
        )[k]
        return pltpu.make_async_remote_copy(
            src_ref=src, dst_ref=dst, send_sem=side_ss.at[p, k],
            recv_sem=side_rs.at[p, k], device_id=(row, 1 - col), device_id_type=MESH,
        )

    def along(p, way, k):
        s, r = ((msg, msg_r), (rim_s, rim_r), (tri_s, tri_r))[k]
        src, dst = s.at[p, way], r.at[p, way]
        target = jnp.where(row == last, row, row + 1) if way else jnp.where(row == 0, row, row - 1)
        return pltpu.make_async_remote_copy(
            src_ref=src, dst_ref=dst, send_sem=row_ss.at[p, way, k],
            recv_sem=row_rs.at[p, way, k], device_id=(target, col), device_id_type=MESH,
        )

    def pack(p):
        dy = shift_ref[p, 0]

        def chunk(i, carry):
            at = pl.ds(pl.multiple_of(i * 16, 16), 16)
            pos = prev_in[p, at].astype(F32)
            cell = pltpu.roll(cur_in[p, at].astype(F32), (4 + dy) % 8, 1)
            low = iota((16, 8, 128), 1) < 4 + dy
            msg[p, 0, at] = jnp.where(low, pos, cell).astype(BF)
            msg[p, 1, at] = jnp.where(low, cell, pos).astype(BF)
            return carry

        lax.fori_loop(0, 16, chunk, 0)

    def send(p, k):
        @pl.when(row > 0)
        def _():
            along(p, 0, k).start()

        @pl.when(row < last)
        def _():
            along(p, 1, k).start()

    ident = jnp.where(iota((128, 128), 0) == iota((128, 128), 1), 1.0, 0.0).astype(BF)

    def spread_rows(flat, x):
        flat[0 : x.shape[0] * 8] = x.reshape(x.shape[0] * 8, 128)

    def picked(flat, y, channels):
        return flat[pl.ds(y, channels, stride=8), :].astype(BF)

    def turn(p):
        for source, target, flat in (
            (prev_in, prev_ref, flat0), (cur_in, cur_ref, flat1), (cot_in, cot_ref, flat0)
        ):
            channels = source.shape[1]
            spread_rows(flat, source[p].astype(F32))
            for y in range(8):
                target[p, y] = dot(ident, picked(flat, y, channels), NT).astype(BF)

    start = jnp.where(left, 112, 0)

    def edges(p):
        for y in range(8):
            pick = []
            for ref in (prev_ref, cur_ref):
                tile = ref[p, y, pl.ds(pl.multiple_of(start, 16), 16), :].astype(F32)
                pick.append(jnp.where(left, tile[8:], tile[:8]))
            edge_s[p, y] = jnp.concatenate(pick, axis=0).astype(BF)
        for y in range(0, 8, 2):
            pick = []
            for yy in (y, y + 1):
                tile = cot_ref[p, yy, pl.ds(pl.multiple_of(start, 16), 16), :].astype(F32)
                pick.append(jnp.where(left, tile[8:], tile[:8]))
            edge_cot_s[p, y // 2] = jnp.concatenate(pick, axis=0).astype(BF)
        for k in range(2):
            side(p, k).start()

    pack(0)
    pl.semaphore_wait(barrier, 24)
    send(0, 0)
    turn(0)
    edges(0)
    pack(1)
    turn(1)
    edges(1)

    w81 = w_ref[...]
    e = e_ref[...]
    w9 = dot(w81, eye_ref[...], TN).astype(BF)
    wk = dot(w9, e)
    turns = [(16 * (shift_ref[p, 0] + 12)) % 256 for p in range(2)]
    back = [(16 * (4 - shift_ref[p, 0])) % 256 for p in range(2)]
    wks = [pltpu.roll(wk, turns[p], 1).astype(BF) for p in range(2)]
    sub, lane = iota((8, 256), 0), iota((8, 256), 1) % 16
    masks = (jnp.where(lane >= 8 - sub, 1.0, 0.0), jnp.where(lane < 8 - sub, 1.0, 0.0))
    far = jnp.where(left, 136, 0)
    tri_lane = iota((WIDE, 128), 1)
    acc[...] = jnp.zeros_like(acc)

    def aligner(offset):
        take = iota((WIDE, 128), 1) + 8 == iota((WIDE, 128), 0) + offset
        out = [jnp.where(take, 1.0, 0.0).astype(BF)]
        at, in_at = iota((WIDE, 16), 0) + offset, iota((WIDE, 16), 1)
        for slots in (0, 8):
            ok = (in_at >= slots) & (in_at < slots + 8) & (in_at - slots + far == at)
            out.append(jnp.where(ok, 1.0, 0.0).astype(BF))
        return out

    def join(p):
        dy, dx = shift_ref[p, 0], shift_ref[p, 1]
        own, own_cot, edge_r = owns[p], own_cots[p], (edge_r0, edge_r1)[p]
        take_p, rim_p, _ = aligner(4 + dx)
        take_c, rim_c0, rim_c1 = aligner(4 - dx)
        for k in range(2):
            side(p, k).wait()
        for y in range(8):
            edge = edge_r[y]
            own[y] = (dot(take_p, prev_ref[p, y]) + dot(rim_p, edge)).astype(BF)
            own[8 + y] = (dot(take_c, cur_ref[p, y]) + dot(rim_c1, edge)).astype(BF)
            rim = dot(rim_c1 if y % 2 else rim_c0, edge_cot_r[p, y // 2])
            aligned = (dot(take_c, cot_ref[p, y]) + rim).astype(BF)
            own_cot[y] = aligned
            own_pre[y] = dot(aligned, w9)

        def tile(s, up):
            is_prev = (s < 4 + dy) if up else (s >= 4 + dy)
            at = jnp.where(is_prev, s, jnp.where(s < 4 + dy, s + 4 - dy, s - 4 - dy))
            both = edge_r[at].astype(F32)
            return jnp.where(is_prev, both[:8], both[8:])

        for k in range(4):
            for way in range(2):
                pair = [tile(2 * k, way == 0), tile(2 * k + 1, way == 0)]
                rim_s[p, way, k] = jnp.concatenate(pair, axis=0).astype(BF)

        def cell_row(t):
            return own_pre[jnp.where(t < 4 + dy, t + 4 - dy, t - 4 - dy)]

        for s in range(4):
            near, away = cell_row(s), cell_row(7 - s)
            tri_s[p, 1, s] = jnp.where(
                tri_lane >= 9 * (8 - s), near, pltpu.roll(away, 128 - 9 * (s + 1), 1)
            ).astype(BF)
            tri_s[p, 0, s] = jnp.where(
                tri_lane < 9 * (8 - s), near, pltpu.roll(away, 9 * (8 - s), 1)
            ).astype(BF)
        send(p, 1)
        send(p, 2)

    join(0)
    send(1, 0)
    join(1)

    def arrive(p):
        dy, dx = shift_ref[p, 0], shift_ref[p, 1]
        halo = halos[p]
        take_p, *rim_p = aligner(4 + dx)
        take_c, *rim_c = aligner(4 - dx)

        @pl.when(row > 0)
        def _():
            for k in range(3):
                along(p, 1, k).wait_recv()

        @pl.when(row == 0)
        def _():
            msg_r[p, 1] = jnp.zeros((256, 8, 128), BF)
            rim_r[p, 1] = jnp.zeros((4, 16, 256), BF)
            tri_r[p, 1] = jnp.zeros((4, WIDE, 128), BF)

        @pl.when(row < last)
        def _():
            for k in range(3):
                along(p, 0, k).wait_recv()

        @pl.when(row == last)
        def _():
            msg_r[p, 0] = jnp.zeros((256, 8, 128), BF)
            rim_r[p, 0] = jnp.zeros((4, 16, 256), BF)
            tri_r[p, 0] = jnp.zeros((4, WIDE, 128), BF)

        def sort(i, carry):
            at = pl.ds(pl.multiple_of(i * 16, 16), 16)
            to = pl.ds(pl.multiple_of(i * 128, 128), 128)
            up, down = msg_r[p, 0, at].astype(F32), msg_r[p, 1, at].astype(F32)
            low = iota((16, 8, 128), 1) < 4 + dy
            flat0[to] = jnp.where(low, up, down).reshape(128, 128)
            flat1[to] = jnp.where(low, down, up).reshape(128, 128)
            return carry

        lax.fori_loop(0, 16, sort, 0)
        for k in range(4):
            up, down = rim_r[p, 0, k].astype(F32), rim_r[p, 1, k].astype(F32)
            low = 2 * k + iota((16, 256), 0) // 8 < 4 + dy
            edge_p = jnp.where(low, up, down).astype(BF)
            edge_c = jnp.where(low, down, up).astype(BF)
            for h in range(2):
                s = 2 * k + h
                x = dot(take_p, picked(flat0, s, 256), NT) + dot(rim_p[h], edge_p)
                halo[s] = x.astype(BF)
                x = dot(take_c, picked(flat1, s, 256), NT) + dot(rim_c[h], edge_c)
                halo[8 + s] = x.astype(BF)
        for s in range(4):
            up, down = tri_r[p, 0, s].astype(F32), tri_r[p, 1, s].astype(F32)
            pre_halos[p][s] = jnp.where(s < 4 + dy, down, up).astype(BF)
            down = pltpu.roll(down, 9 * (s + 1), 1)
            up = pltpu.roll(up, 128 - 9 * (8 - s), 1)
            pre_halos[p][7 - s] = jnp.where(7 - s < 4 + dy, down, up).astype(BF)

    def loop(lo, hi, work):
        def body(bb, carry):
            work(bb)
            return carry

        lax.fori_loop(lo, hi, body, 0)

    def early(p):
        dy = shift_ref[p, 0]

        def work(i):
            for bb in (2 * i, 2 * i + 1):
                cells_early(
                    p, bb, dy, owns[p], cur_ref, cot_ref, wks[p], sum_c, act_c, pre_c)
                positions_early(
                    p, bb, dy, owns[p], own_cots[p], prev_ref, wks[p], masks, sum_p)

        loop(0, 4, work)

    def late_cells(p, bb):
        cells_late(
            p, bb, shift_ref[p, 0], halos[p], cur_ref, cot_ref, sum_c, act_c, pre_c, gc_ref, acc)

    def late_positions(p, bb):
        positions_late(
            p, bb, shift_ref[p, 0], halos[p], pre_halos[p], prev_ref, e, masks, sum_p, gp_ref)

    def late(i):
        for bb in (2 * i, 2 * i + 1):
            late_cells(0, bb)
            late_positions(0, bb)

    early(0)
    early(1)
    arrive(0)
    loop(0, 4, late)
    arrive(1)
    loop(0, 2, lambda i: [late_cells(1, 4 * i + k) for k in range(4)])

    turned = (pltpu.roll(acc[0], back[0], 1) + pltpu.roll(acc[1], back[1], 1)).T
    for u in range(9):
        ar0[9 * u : 9 * u + 9] = turned[16 * u : 16 * u + 9]
    ar0[81:128] = jnp.zeros((47, 128), F32)

    def share(ref, i):
        return ref.at[pl.ds(pl.multiple_of(i * 16, 16), 16)]

    def first(d):
        peer = (g1 + d) % 8
        return pltpu.make_async_remote_copy(
            src_ref=share(ar0, peer), dst_ref=ar1.at[g1], send_sem=s1.at[peer],
            recv_sem=r1.at[g1], device_id=member(peer, g2), device_id_type=MESH,
        )

    def second(d):
        peer = (g2 + d) % 16
        return pltpu.make_async_remote_copy(
            src_ref=ar2.at[g2], dst_ref=ar2.at[g2], send_sem=s2.at[peer],
            recv_sem=r2.at[g2], device_id=member(g1, peer), device_id_type=MESH,
        )

    def third(d):
        peer = (g1 + d) % 8
        return pltpu.make_async_remote_copy(
            src_ref=ar3.at[g1], dst_ref=ar3.at[g1], send_sem=s3.at[peer],
            recv_sem=r3.at[g1], device_id=member(peer, g2), device_id_type=MESH,
        )

    def got(buffer, sends, receives, source):
        pltpu.make_async_remote_copy(
            src_ref=buffer.at[source], dst_ref=buffer.at[source], send_sem=sends.at[source],
            recv_sem=receives.at[source], device_id=(row, 1 - col), device_id_type=MESH,
        ).wait_recv()

    for d in range(1, 8):
        first(d).start()
    loop(0, 1, lambda i: [late_positions(1, k) for k in range(3)])
    ar1[g1] = ar0[pl.ds(pl.multiple_of(g1 * 16, 16), 16)]
    for d in range(1, 8):
        first(d).wait_send()
        got(ar1, s1, r1, (g1 + d) % 8)
    ar2[g2] = jnp.sum(ar1[...], axis=0)
    for d in range(1, 16):
        second(d).start()
    loop(0, 1, lambda i: [late_positions(1, 3 + k) for k in range(3)])
    for d in range(1, 16):
        second(d).wait_send()
        got(ar2, s2, r2, (g2 + d) % 16)
    ar3[g1] = jnp.sum(ar2[...], axis=0)
    for d in range(1, 8):
        third(d).start()
    loop(0, 1, lambda i: [late_positions(1, 6 + k) for k in range(2)])
    for d in range(1, 8):
        third(d).wait_send()
        got(ar3, s3, r3, (g1 + d) % 8)
    gw_ref[...] = ar3[...].reshape(128, 128)[:81] * norm

    for p in range(2):
        for k in range(3):

            @pl.when(row > 0)
            def _():
                along(p, 0, k).wait_send()

            @pl.when(row < last)
            def _():
                along(p, 1, k).wait_send()


def spread_matrix():
    e = np.zeros((128, 256), np.float32)
    for u in range(9):
        for v in range(9):
            e[9 * u + v, 16 * u + v] = 1.0 / 32.0
    return e


def local(current, previous, shift, weight, cotangent):
    pairs, channels, rows, cols = current.shape
    e = jnp.asarray(spread_matrix(), BF)
    eye = jnp.asarray(np.eye(81, 128), BF)
    total = pairs * rows * lax.axis_size("row") * cols * lax.axis_size("col")
    vmem = pl.BlockSpec(memory_space=pltpu.VMEM)
    dma = pltpu.SemaphoreType.DMA
    v = pltpu.VMEM
    gc, gp, gw = pl.pallas_call(
        functools.partial(kernel, 1.0 / math.sqrt(total)),
        in_specs=[pl.BlockSpec(memory_space=pltpu.SMEM)] + [vmem] * 6,
        out_specs=[vmem] * 3,
        out_shape=[
            jax.ShapeDtypeStruct((2, 8, 128, 256), BF),
            jax.ShapeDtypeStruct((2, 8, 128, 256), BF),
            jax.ShapeDtypeStruct((81, 128), F32),
        ],
        scratch_shapes=[
            v((2, 8, 128, 256), BF), v((2, 8, 128, 256), BF), v((2, 8, 128, 128), BF),
            v((2048, 128), F32), v((2048, 128), F32),
            v((2, 2, 256, 8, 128), BF), v((2, 2, 4, 16, 256), BF), v((2, 2, 4, 16, 256), BF),
            v((2, 8, 16, 256), BF), v((8, 16, 256), BF), v((8, 16, 256), BF),
            v((2, 4, 16, 128), BF), v((2, 4, 16, 128), BF),
            v((16, WIDE, 256), BF), v((16, WIDE, 256), BF),
            v((8, WIDE, 128), BF), v((8, WIDE, 128), BF),
            v((8, WIDE, 128), F32),
            v((2, 2, 256, 8, 128), BF),
            v((2, 2, 4, WIDE, 128), BF), v((2, 2, 4, WIDE, 128), BF),
            v((16, WIDE, 256), BF), v((16, WIDE, 256), BF),
            v((8, WIDE, 128), BF), v((8, WIDE, 128), BF),
            v((2, 8, 128, 256), F32),
            v((2, 8, 128, 128), F32), v((2, 8, 128, 128), F32),
            v((2, 8, 128, 256), F32),
            v((2, 128, 256), F32),
            v((128, 128), F32), v((8, 16, 128), F32), v((16, 16, 128), F32), v((8, 16, 128), F32),
            dma((2, 2)), dma((2, 2)), dma((2, 2, 3)), dma((2, 2, 3)),
            dma((8,)), dma((8,)), dma((16,)), dma((16,)), dma((8,)), dma((8,)),
        ],
        compiler_params=pltpu.CompilerParams(
            collective_id=0, has_side_effects=True, vmem_limit_bytes=56 << 20
        ),
        cost_estimate=pl.CostEstimate(
            flops=3_000_000_000, bytes_accessed=8 << 20, transcendentals=1_500_000
        ),
    )(shift, previous, current, cotangent, weight.T, e, eye)
    return gc.transpose(0, 3, 1, 2), gp.transpose(0, 3, 1, 2), gw.T


def solution(mesh):
    grid = P(None, None, "row", "col")
    return jax.shard_map(
        local,
        mesh=mesh,
        in_specs=(grid, grid, P(), P(), grid),
        out_specs=(grid, grid, P()),
        check_vma=False,
    )
```

```python
import functools
import math

import jax
import jax.numpy as jnp
import numpy as np
from jax import lax
from jax.experimental import pallas as pl
from jax.experimental.pallas import tpu as pltpu
from jax.sharding import PartitionSpec as P

BF = jnp.bfloat16
F32 = jnp.float32
MESH = pl.DeviceIdType.MESH
NT = (((1,), (1,)), ((), ()))
TN = (((0,), (0,)), ((), ()))
NN = (((1,), (0,)), ((), ()))
WIDE = 144


def dot(a, b, dims=NN):
    return lax.dot_general(a, b, dims, preferred_element_type=F32)


def iota(shape, axis):
    return lax.broadcasted_iota(jnp.int32, shape, axis)


def skew(x, shift):
    return pltpu.roll(x, shift % 256, 1, stride=1, stride_axis=0)


def flip8(x):
    idx = 7 - iota((8, 128), 0)
    parts = [
        jnp.take_along_axis(x[:, at : at + 128], idx, axis=0) for at in range(0, x.shape[1], 128)
    ]
    return parts[0] if len(parts) == 1 else jnp.concatenate(parts, axis=1)


def activation(vol_dot):
    half = vol_dot * (1.0 / 32.0)
    q = 1.0 + jnp.tanh(half)
    act = half * q
    return act, q + act * (2.0 - q)


def cell_block(p, bb, rows_of, cur_ref):
    at = pl.multiple_of(bb * 16, 16)
    cur = cur_ref[p, :, pl.ds(at, 16), :].reshape(128, 256)
    rows = [rows_of(i, at) for i in range(8)]
    win = jnp.concatenate([r[0:16] for r in rows] + [r[8:24] for r in rows], axis=0)
    return win, dot(cur, win, NT)


def split_grads(grads):
    zero = jnp.zeros((8, 128), F32)
    full = [
        jnp.concatenate([zero, g] if i % 2 else [g, zero], axis=1) for i, g in enumerate(grads)
    ]
    return jnp.concatenate(full, axis=0).astype(BF)


def cells_early(p, bb, own, cur_ref, cot_ref, wk, sum_c, act_c, pre_c, sum_q):
    win, vol = cell_block(p, bb, lambda i, at: own[i, pl.ds(at, 32), :], cur_ref)
    at = pl.multiple_of(bb * 16, 16)
    pre = dot(cot_ref[p, :, pl.ds(at, 16), :].reshape(128, 128), wk)
    grads, acts, rest = [], [], []
    for i in range(16):
        y, odd = divmod(i, 2)
        rows = slice(8 * i, 8 * i + 8)
        act, slope = activation(vol[rows, 128 * odd : 128 * odd + 128])
        piece = skew(pre[rows], 16 * y)
        grads.append(piece[:, :128] * slope)
        rest.append(piece[:, 128:])
        acts.append(flip8(act))
    act_c[p, bb] = jnp.concatenate(acts, axis=0)
    pre_c[p, bb] = jnp.concatenate(rest, axis=0)
    grad = split_grads(grads)
    sum_c[p, bb] = dot(grad, win)
    cur = cur_ref[p, :, pl.ds(at, 16), :].reshape(128, 256)
    back = dot(grad, cur, TN)
    for i in range(8):
        even, odd = back[16 * i : 16 * i + 16], back[128 + 16 * i : 128 + 16 * i + 16]
        sum_q[p, i, pl.ds(at, 8), :] += even[:8]
        sum_q[p, i, pl.ds(at + 8, 8), :] = even[8:] + odd[:8]
        sum_q[p, i, pl.ds(at + 16, 8), :] = odd[8:]


def cells_late(p, bb, dy, halo, cur_ref, cot_ref, sum_c, act_c, pre_c, out_ref, acc_ref):
    def rows_of(i, at):
        return halo[i, pl.ds(at, 32), :]

    win, vol = cell_block(p, bb, rows_of, cur_ref)
    at = pl.multiple_of(bb * 16, 16)
    cot = cot_ref[p, :, pl.ds(at, 16), :].reshape(128, 128).astype(F32)
    cot_rev = jnp.concatenate([flip8(cot[8 * i : 8 * i + 8]) for i in range(16)], axis=0)
    act_own, pre = act_c[p, bb], pre_c[p, bb]
    grads, acts = [], []
    for i in range(16):
        y, odd = divmod(i, 2)
        rows = slice(8 * i, 8 * i + 8)
        act, slope = activation(vol[rows, 128 * odd : 128 * odd + 128])
        grads.append(pre[rows] * slope)
        act = jnp.concatenate([act_own[rows], flip8(act)], axis=1)
        acts.append(skew(act, 249 - 16 * y))
    act = jnp.concatenate(acts, axis=0).astype(BF)
    acc_ref[p] += dot(cot_rev.astype(BF), act, TN)
    out = sum_c[p, bb] + dot(split_grads(grads), win)
    out_ref[p, :, pl.ds(at, 16), :] = out.astype(BF).reshape(8, 16, 256)


def rim_positions(p, left, rim_cur, rim_cot, prev_ref, wk, masks, rim_sum):
    at = pl.multiple_of(jnp.where(left, 112, 0), 16)
    prev = prev_ref[p, :, pl.ds(at, 16), :].reshape(128, 256)
    win = rim_cur[p].reshape(64, 256).astype(BF)
    vol = dot(win, prev, NT)
    pre = dot(rim_cot[p].reshape(64, 128).astype(BF), wk)
    mask = jnp.where(left, masks[1], masks[0])
    grads = []
    for i in range(8):
        rows = slice(8 * i, 8 * i + 8)
        piece = pre[rows] * mask
        piece = jnp.where(left, skew(piece, 16 * i + 8), skew(piece, 16 * i - 8))[:, :128]
        grads.append(piece * activation(vol[rows])[1])
    rim_sum[p] = dot(jnp.concatenate(grads, axis=0).astype(BF), win, TN)


def positions_late(
    p, bb, dy, dx, left, halo, pre_halo, prev_ref, e, masks, sum_q, rim_sum, out_ref
):
    at = pl.multiple_of(bb * 16, 16)
    prev = prev_ref[p, :, pl.ds(at, 16), :].reshape(128, 256)
    win = jnp.concatenate([halo[8 + i, pl.ds(at, 32), :][:24] for i in range(8)], axis=0)
    vol = dot(win, prev, NT)
    pre = dot(
        jnp.concatenate([pre_halo[i, pl.ds(at, 32), :][:24] for i in range(8)], axis=0), e
    )
    grads = []
    for i in range(8):
        for g in range(3):
            rows = slice(24 * i + 8 * g, 24 * i + 8 * g + 8)
            piece = pre[rows]
            if g != 1:
                piece = piece * masks[g // 2]
            piece = skew(piece, 16 * i + 8 * (g - 1))
            piece = jnp.where(i < 4 + dy, piece[:, 128:], piece[:, :128])
            grads.append(piece * activation(vol[rows])[1])
    out = dot(jnp.concatenate(grads, axis=0).astype(BF), win, TN)
    own = pltpu.roll(sum_q[p, :, pl.ds(at, 24), :], (20 + dx) % 24, 1)[:, :16].reshape(128, 256)
    rim = jnp.where(bb == jnp.where(left, 7, 0), 1.0, 0.0) * rim_sum[p]
    out_ref[p, :, pl.ds(at, 16), :] = (out + own + rim).astype(BF).reshape(8, 16, 256)


def kernel(
    norm, shift_ref, prev_in, cur_in, cot_in, w_ref, e_ref, eye_ref,
    gc_ref, gp_ref, gw_ref,
    prev_ref, cur_ref, cot_ref, flat0, flat1, msg_r, rim_s, rim_r,
    edge_s, edge_r0, edge_r1, edge_cot_s, edge_cot_r, own0, own1, cot_x, own_pre, rim_cur, rim_cot,
    msg, tri_s, tri_r, halo0, halo1, pre_halo0, pre_halo1,
    sum_c, act_c, pre_c, sum_q, rim_sum, acc, ar0, ar1, ar2, ar3,
    side_ss, side_rs, row_ss, row_rs, s1, r1, s2, r2, s3, r3,
):
    row, col = lax.axis_index("row"), lax.axis_index("col")
    last = lax.axis_size("row") - 1
    left = col == 0
    owns = (own0, own1)
    halos, pre_halos = (halo0, halo1), (pre_halo0, pre_halo1)
    g1, g2 = (row % 4) * 2 + col, row // 4

    def member(a, b):
        return (b * 4 + a // 2, a % 2)

    barrier = pltpu.get_barrier_semaphore()

    def greet(target):
        pl.semaphore_signal(barrier, inc=1, device_id=target, device_id_type=MESH)

    for d in range(1, 8):
        greet(member((g1 + d) % 8, g2))
    for d in range(1, 16):
        greet(member(g1, (g2 + d) % 16))
    greet(((row + 1) % (last + 1), col))
    greet(((row + last) % (last + 1), col))

    def side(p, k):
        src, dst = (
            (edge_s.at[p], (edge_r0, edge_r1)[p]), (edge_cot_s.at[p], edge_cot_r.at[p])
        )[k]
        return pltpu.make_async_remote_copy(
            src_ref=src, dst_ref=dst, send_sem=side_ss.at[p, k],
            recv_sem=side_rs.at[p, k], device_id=(row, 1 - col), device_id_type=MESH,
        )

    def along(p, way, k):
        s, r = ((msg, msg_r), (rim_s, rim_r), (tri_s, tri_r))[k]
        src, dst = s.at[p, way], r.at[p, way]
        target = jnp.where(row == last, row, row + 1) if way else jnp.where(row == 0, row, row - 1)
        return pltpu.make_async_remote_copy(
            src_ref=src, dst_ref=dst, send_sem=row_ss.at[p, way, k],
            recv_sem=row_rs.at[p, way, k], device_id=(target, col), device_id_type=MESH,
        )

    def pack(p):
        dy = shift_ref[p, 0]

        def chunk(i, carry):
            at = pl.ds(pl.multiple_of(i * 16, 16), 16)
            pos = prev_in[p, at].astype(F32)
            cell = pltpu.roll(cur_in[p, at].astype(F32), (4 + dy) % 8, 1)
            low = iota((16, 8, 128), 1) < 4 + dy
            msg[p, 0, at] = jnp.where(low, pos, cell).astype(BF)
            msg[p, 1, at] = jnp.where(low, cell, pos).astype(BF)
            return carry

        lax.fori_loop(0, 16, chunk, 0)

    def send(p, k):
        @pl.when(row > 0)
        def _():
            along(p, 0, k).start()

        @pl.when(row < last)
        def _():
            along(p, 1, k).start()

    ident = jnp.where(iota((128, 128), 0) == iota((128, 128), 1), 1.0, 0.0).astype(BF)

    def spread_rows(flat, x):
        flat[0 : x.shape[0] * 8] = x.reshape(x.shape[0] * 8, 128)

    def picked(flat, y, channels):
        return flat[pl.ds(y, channels, stride=8), :].astype(BF)

    def aligner(offset):
        take = iota((WIDE, 128), 1) + 8 == iota((WIDE, 128), 0) + offset
        return jnp.where(take, 1.0, 0.0).astype(BF)

    def rim_aligner(rows, first, offset, slots):
        far = jnp.where(left, 136, 0)
        at, in_at = iota((rows, 16), 0) + offset, iota((rows, 16), 1)
        at = at + (first if rows == 8 else jnp.where(iota((rows, 16), 0) < 16, 0, 112))
        ok = (in_at >= slots) & (in_at < slots + 8) & (in_at - slots + far == at)
        return jnp.where(ok, 1.0, 0.0).astype(BF)

    def turn(p):
        dx = shift_ref[p, 1]
        both_p = jnp.concatenate([ident, aligner(4 + dx)], axis=0)
        both_c = jnp.concatenate([ident, aligner(4 - dx)], axis=0)
        spread_rows(flat0, prev_in[p].astype(F32))
        for y in range(8):
            x = dot(both_p, picked(flat0, y, 256), NT).astype(BF)
            prev_ref[p, y] = x[:128]
            owns[p][y] = x[128:]
        spread_rows(flat1, cur_in[p].astype(F32))
        for y in range(8):
            cur_ref[p, y] = dot(ident, picked(flat1, y, 256), NT).astype(BF)
        spread_rows(flat0, cot_in[p].astype(F32))
        for y in range(8):
            x = dot(both_c, picked(flat0, y, 128), NT)
            cot_ref[p, y] = x[:128].astype(BF)
            cot_x[p, y] = x[128:]

    start = jnp.where(left, 112, 0)

    def edges(p):
        for y in range(8):
            pick = []
            for ref in (prev_ref, cur_ref):
                tile = ref[p, y, pl.ds(pl.multiple_of(start, 16), 16), :].astype(F32)
                pick.append(jnp.where(left, tile[8:], tile[:8]))
            edge_s[p, y] = jnp.concatenate(pick, axis=0).astype(BF)
        for y in range(0, 8, 2):
            pick = []
            for yy in (y, y + 1):
                tile = cot_ref[p, yy, pl.ds(pl.multiple_of(start, 16), 16), :].astype(F32)
                pick.append(jnp.where(left, tile[8:], tile[:8]))
            edge_cot_s[p, y // 2] = jnp.concatenate(pick, axis=0).astype(BF)
        for k in range(2):
            side(p, k).start()

    pack(0)
    pl.semaphore_wait(barrier, 24)
    send(0, 0)
    turn(0)
    edges(0)
    pack(1)
    turn(1)
    edges(1)

    w81 = w_ref[...]
    e = e_ref[...]
    w9 = dot(w81, eye_ref[...], TN).astype(BF)
    wk = dot(w9, e)
    turns = [(16 * (shift_ref[p, 0] + 12)) % 256 for p in range(2)]
    back = [(16 * (4 - shift_ref[p, 0])) % 256 for p in range(2)]
    wks = [pltpu.roll(wk, turns[p], 1).astype(BF) for p in range(2)]
    sub, lane = iota((8, 256), 0), iota((8, 256), 1) % 16
    masks = (jnp.where(lane >= 8 - sub, 1.0, 0.0), jnp.where(lane < 8 - sub, 1.0, 0.0))
    tri_lane = iota((WIDE, 128), 1)
    acc[...] = jnp.zeros_like(acc)
    sum_q[:, :, 0:8] = jnp.zeros((2, 8, 8, 256), F32)

    def join(p):
        dy, dx = shift_ref[p, 0], shift_ref[p, 1]
        own, edge_r = owns[p], (edge_r0, edge_r1)[p]
        first = jnp.where(left, 128, 0)
        rim_p = rim_aligner(32, 0, 4 + dx, 0)
        rim_c = [rim_aligner(32, 0, 4 - dx, slots) for slots in (0, 8)]
        rim_8 = [rim_aligner(8, first, 4 - dx, slots) for slots in (0, 8)]
        for k in range(2):
            side(p, k).wait()
        for y in range(8):
            edge, edge_cot = edge_r[y], edge_cot_r[p, y // 2]
            rim = dot(rim_p, edge)
            own[y, 0:16] = (own[y, 0:16].astype(F32) + rim[:16]).astype(BF)
            own[y, 128:144] = (own[y, 128:144].astype(F32) + rim[16:]).astype(BF)
            rim_cur[p, y] = dot(rim_8[1], edge)
            rim_cot[p, y] = dot(rim_8[y % 2], edge_cot)
            rim = dot(rim_c[y % 2], edge_cot)
            x = cot_x[p, y]
            x = jnp.concatenate([x[:16] + rim[:16], x[16:128], x[128:] + rim[16:]], axis=0)
            own_pre[y] = dot(x.astype(BF), w9)

        def tile(s, up):
            is_prev = (s < 4 + dy) if up else (s >= 4 + dy)
            at = jnp.where(is_prev, s, jnp.where(s < 4 + dy, s + 4 - dy, s - 4 - dy))
            both = edge_r[at].astype(F32)
            return jnp.where(is_prev, both[:8], both[8:])

        for k in range(4):
            for way in range(2):
                pair = [tile(2 * k, way == 0), tile(2 * k + 1, way == 0)]
                rim_s[p, way, k] = jnp.concatenate(pair, axis=0).astype(BF)

        def cell_row(t):
            return own_pre[jnp.where(t < 4 + dy, t + 4 - dy, t - 4 - dy)]

        for s in range(4):
            near, away = cell_row(s), cell_row(7 - s)
            tri_s[p, 1, s] = jnp.where(
                tri_lane >= 9 * (8 - s), near, pltpu.roll(away, 128 - 9 * (s + 1), 1)
            ).astype(BF)
            tri_s[p, 0, s] = jnp.where(
                tri_lane < 9 * (8 - s), near, pltpu.roll(away, 9 * (8 - s), 1)
            ).astype(BF)
        send(p, 1)
        send(p, 2)

    join(0)
    send(1, 0)
    join(1)

    def arrive(p):
        dy, dx = shift_ref[p, 0], shift_ref[p, 1]
        halo = halos[p]
        take_p, take_c = aligner(4 + dx), aligner(4 - dx)
        rim_p = [rim_aligner(32, 0, 4 + dx, slots) for slots in (0, 8)]
        rim_c = [rim_aligner(32, 0, 4 - dx, slots) for slots in (0, 8)]

        @pl.when(row > 0)
        def _():
            for k in range(3):
                along(p, 1, k).wait_recv()

        @pl.when(row == 0)
        def _():
            msg_r[p, 1] = jnp.zeros((256, 8, 128), BF)
            rim_r[p, 1] = jnp.zeros((4, 16, 256), BF)
            tri_r[p, 1] = jnp.zeros((4, WIDE, 128), BF)

        @pl.when(row < last)
        def _():
            for k in range(3):
                along(p, 0, k).wait_recv()

        @pl.when(row == last)
        def _():
            msg_r[p, 0] = jnp.zeros((256, 8, 128), BF)
            rim_r[p, 0] = jnp.zeros((4, 16, 256), BF)
            tri_r[p, 0] = jnp.zeros((4, WIDE, 128), BF)

        def sort(i, carry):
            at = pl.ds(pl.multiple_of(i * 16, 16), 16)
            to = pl.ds(pl.multiple_of(i * 128, 128), 128)
            up, down = msg_r[p, 0, at].astype(F32), msg_r[p, 1, at].astype(F32)
            low = iota((16, 8, 128), 1) < 4 + dy
            flat0[to] = jnp.where(low, up, down).reshape(128, 128)
            flat1[to] = jnp.where(low, down, up).reshape(128, 128)
            return carry

        lax.fori_loop(0, 16, sort, 0)
        for k in range(4):
            up, down = rim_r[p, 0, k].astype(F32), rim_r[p, 1, k].astype(F32)
            low = 2 * k + iota((16, 256), 0) // 8 < 4 + dy
            edge_p = jnp.where(low, up, down).astype(BF)
            edge_c = jnp.where(low, down, up).astype(BF)
            for h in range(2):
                s = 2 * k + h
                for to, take, flat, rims, edge in (
                    (s, take_p, flat0, rim_p, edge_p), (8 + s, take_c, flat1, rim_c, edge_c)
                ):
                    x, rim = dot(take, picked(flat, s, 256), NT), dot(rims[h], edge)
                    halo[to, 0:16] = (x[:16] + rim[:16]).astype(BF)
                    halo[to, 16:128] = x[16:128].astype(BF)
                    halo[to, 128:144] = (x[128:] + rim[16:]).astype(BF)
        for s in range(4):
            up, down = tri_r[p, 0, s].astype(F32), tri_r[p, 1, s].astype(F32)
            pre_halos[p][s] = jnp.where(s < 4 + dy, down, up).astype(BF)
            down = pltpu.roll(down, 9 * (s + 1), 1)
            up = pltpu.roll(up, 128 - 9 * (8 - s), 1)
            pre_halos[p][7 - s] = jnp.where(7 - s < 4 + dy, down, up).astype(BF)

    def loop(lo, hi, work):
        def body(bb, carry):
            work(bb)
            return carry

        lax.fori_loop(lo, hi, body, 0)

    def early(p):
        def work(i):
            for bb in (2 * i, 2 * i + 1):
                cells_early(
                    p, bb, owns[p], cur_ref, cot_ref, wks[p], sum_c, act_c, pre_c, sum_q)

        loop(0, 4, work)
        rim_positions(p, left, rim_cur, rim_cot, prev_ref, wks[p], masks, rim_sum)

    def late_cells(p, bb):
        cells_late(
            p, bb, shift_ref[p, 0], halos[p], cur_ref, cot_ref, sum_c, act_c, pre_c, gc_ref, acc)

    def late_positions(p, bb):
        positions_late(
            p, bb, shift_ref[p, 0], shift_ref[p, 1], left, halos[p], pre_halos[p], prev_ref, e,
            masks, sum_q, rim_sum, gp_ref)

    def late(i):
        for bb in (2 * i, 2 * i + 1):
            late_cells(0, bb)
            late_positions(0, bb)

    early(0)
    early(1)
    arrive(0)
    loop(0, 4, late)
    arrive(1)
    loop(0, 2, lambda i: [late_cells(1, 4 * i + k) for k in range(4)])

    turned = (pltpu.roll(acc[0], back[0], 1) + pltpu.roll(acc[1], back[1], 1)).T
    for u in range(9):
        ar0[9 * u : 9 * u + 9] = turned[16 * u : 16 * u + 9]
    ar0[81:128] = jnp.zeros((47, 128), F32)

    def share(ref, i):
        return ref.at[pl.ds(pl.multiple_of(i * 16, 16), 16)]

    def first(d):
        peer = (g1 + d) % 8
        return pltpu.make_async_remote_copy(
            src_ref=share(ar0, peer), dst_ref=ar1.at[g1], send_sem=s1.at[peer],
            recv_sem=r1.at[g1], device_id=member(peer, g2), device_id_type=MESH,
        )

    def second(d):
        peer = (g2 + d) % 16
        return pltpu.make_async_remote_copy(
            src_ref=ar2.at[g2], dst_ref=ar2.at[g2], send_sem=s2.at[peer],
            recv_sem=r2.at[g2], device_id=member(g1, peer), device_id_type=MESH,
        )

    def third(d):
        peer = (g1 + d) % 8
        return pltpu.make_async_remote_copy(
            src_ref=ar3.at[g1], dst_ref=ar3.at[g1], send_sem=s3.at[peer],
            recv_sem=r3.at[g1], device_id=member(peer, g2), device_id_type=MESH,
        )

    def got(buffer, sends, receives, source):
        pltpu.make_async_remote_copy(
            src_ref=buffer.at[source], dst_ref=buffer.at[source], send_sem=sends.at[source],
            recv_sem=receives.at[source], device_id=(row, 1 - col), device_id_type=MESH,
        ).wait_recv()

    for d in range(1, 8):
        first(d).start()
    loop(0, 1, lambda i: [late_positions(1, k) for k in range(3)])
    ar1[g1] = ar0[pl.ds(pl.multiple_of(g1 * 16, 16), 16)]
    for d in range(1, 8):
        first(d).wait_send()
        got(ar1, s1, r1, (g1 + d) % 8)
    ar2[g2] = jnp.sum(ar1[...], axis=0)
    for d in range(1, 16):
        second(d).start()
    loop(0, 1, lambda i: [late_positions(1, 3 + k) for k in range(3)])
    for d in range(1, 16):
        second(d).wait_send()
        got(ar2, s2, r2, (g2 + d) % 16)
    ar3[g1] = jnp.sum(ar2[...], axis=0)
    for d in range(1, 8):
        third(d).start()
    loop(0, 1, lambda i: [late_positions(1, 6 + k) for k in range(2)])
    for d in range(1, 8):
        third(d).wait_send()
        got(ar3, s3, r3, (g1 + d) % 8)
    gw_ref[...] = ar3[...].reshape(128, 128)[:81] * norm

    for p in range(2):
        for k in range(3):

            @pl.when(row > 0)
            def _():
                along(p, 0, k).wait_send()

            @pl.when(row < last)
            def _():
                along(p, 1, k).wait_send()


def spread_matrix():
    e = np.zeros((128, 256), np.float32)
    for u in range(9):
        for v in range(9):
            e[9 * u + v, 16 * u + v] = 1.0 / 32.0
    return e


def local(current, previous, shift, weight, cotangent):
    pairs, channels, rows, cols = current.shape
    e = jnp.asarray(spread_matrix(), BF)
    eye = jnp.asarray(np.eye(81, 128), BF)
    total = pairs * rows * lax.axis_size("row") * cols * lax.axis_size("col")
    vmem = pl.BlockSpec(memory_space=pltpu.VMEM)
    dma = pltpu.SemaphoreType.DMA
    v = pltpu.VMEM
    gc, gp, gw = pl.pallas_call(
        functools.partial(kernel, 1.0 / math.sqrt(total)),
        in_specs=[pl.BlockSpec(memory_space=pltpu.SMEM)] + [vmem] * 6,
        out_specs=[vmem] * 3,
        out_shape=[
            jax.ShapeDtypeStruct((2, 8, 128, 256), BF),
            jax.ShapeDtypeStruct((2, 8, 128, 256), BF),
            jax.ShapeDtypeStruct((81, 128), F32),
        ],
        scratch_shapes=[
            v((2, 8, 128, 256), BF), v((2, 8, 128, 256), BF), v((2, 8, 128, 128), BF),
            v((2048, 128), F32), v((2048, 128), F32),
            v((2, 2, 256, 8, 128), BF), v((2, 2, 4, 16, 256), BF), v((2, 2, 4, 16, 256), BF),
            v((2, 8, 16, 256), BF), v((8, 16, 256), BF), v((8, 16, 256), BF),
            v((2, 4, 16, 128), BF), v((2, 4, 16, 128), BF),
            v((8, WIDE, 256), BF), v((8, WIDE, 256), BF),
            v((2, 8, WIDE, 128), F32), v((8, WIDE, 128), F32),
            v((2, 8, 8, 256), F32), v((2, 8, 8, 128), F32),
            v((2, 2, 256, 8, 128), BF),
            v((2, 2, 4, WIDE, 128), BF), v((2, 2, 4, WIDE, 128), BF),
            v((16, WIDE, 256), BF), v((16, WIDE, 256), BF),
            v((8, WIDE, 128), BF), v((8, WIDE, 128), BF),
            v((2, 8, 128, 256), F32),
            v((2, 8, 128, 128), F32), v((2, 8, 128, 128), F32),
            v((2, 8, WIDE, 256), F32), v((2, 128, 256), F32),
            v((2, 128, 256), F32),
            v((128, 128), F32), v((8, 16, 128), F32), v((16, 16, 128), F32), v((8, 16, 128), F32),
            dma((2, 2)), dma((2, 2)), dma((2, 2, 3)), dma((2, 2, 3)),
            dma((8,)), dma((8,)), dma((16,)), dma((16,)), dma((8,)), dma((8,)),
        ],
        compiler_params=pltpu.CompilerParams(
            collective_id=0, has_side_effects=True, vmem_limit_bytes=56 << 20
        ),
        cost_estimate=pl.CostEstimate(
            flops=3_000_000_000, bytes_accessed=8 << 20, transcendentals=1_500_000
        ),
    )(shift, previous, current, cotangent, weight.T, e, eye)
    return gc.transpose(0, 3, 1, 2), gp.transpose(0, 3, 1, 2), gw.T


def solution(mesh):
    grid = P(None, None, "row", "col")
    return jax.shard_map(
        local,
        mesh=mesh,
        in_specs=(grid, grid, P(), P(), grid),
        out_specs=(grid, grid, P()),
        check_vma=False,
    )
```

```python
import functools
import math

import jax
import jax.numpy as jnp
import numpy as np
from jax import lax
from jax.experimental import pallas as pl
from jax.experimental.pallas import tpu as pltpu
from jax.sharding import PartitionSpec as P

BF = jnp.bfloat16
F32 = jnp.float32
MESH = pl.DeviceIdType.MESH
NT = (((1,), (1,)), ((), ()))
TN = (((0,), (0,)), ((), ()))
NN = (((1,), (0,)), ((), ()))
WIDE = 144


def dot(a, b, dims=NN):
    return lax.dot_general(a, b, dims, preferred_element_type=F32)


def iota(shape, axis):
    return lax.broadcasted_iota(jnp.int32, shape, axis)


def skew(x, shift):
    return pltpu.roll(x, shift % 256, 1, stride=1, stride_axis=0)


def flip8(x):
    idx = 7 - iota((8, 128), 0)
    parts = [
        jnp.take_along_axis(x[:, at : at + 128], idx, axis=0) for at in range(0, x.shape[1], 128)
    ]
    return parts[0] if len(parts) == 1 else jnp.concatenate(parts, axis=1)


def activation(vol_dot):
    half = vol_dot * (1.0 / 32.0)
    q = 1.0 + jnp.tanh(half)
    act = half * q
    return act, q + act * (2.0 - q)


def cell_block(p, bb, rows_of, cur_ref):
    at = pl.multiple_of(bb * 16, 16)
    cur = cur_ref[p, :, pl.ds(at, 16), :].reshape(128, 256)
    rows = [rows_of(i, at) for i in range(8)]
    win = jnp.concatenate([r[0:16] for r in rows] + [r[8:24] for r in rows], axis=0)
    return win, dot(cur, win, NT)


def split_grads(grads):
    zero = jnp.zeros((8, 128), F32)
    full = [
        jnp.concatenate([zero, g] if i % 2 else [g, zero], axis=1) for i, g in enumerate(grads)
    ]
    return jnp.concatenate(full, axis=0).astype(BF)


def cells_early(p, bb, own, cur_ref, cot_ref, wk, sum_c, act_c, pre_c, sum_q):
    win, vol = cell_block(p, bb, lambda i, at: own[i, pl.ds(at, 32), :], cur_ref)
    at = pl.multiple_of(bb * 16, 16)
    pre = dot(cot_ref[p, :, pl.ds(at, 16), :].reshape(128, 128), wk)
    grads, acts, rest = [], [], []
    for i in range(16):
        y, odd = divmod(i, 2)
        rows = slice(8 * i, 8 * i + 8)
        act, slope = activation(vol[rows, 128 * odd : 128 * odd + 128])
        piece = skew(pre[rows], 16 * y)
        grads.append(piece[:, :128] * slope)
        rest.append(piece[:, 128:])
        acts.append(flip8(act))
    act_c[p, bb] = jnp.concatenate(acts, axis=0)
    pre_c[p, bb] = jnp.concatenate(rest, axis=0)
    grad = split_grads(grads)
    sum_c[p, bb] = dot(grad, win)
    cur = cur_ref[p, :, pl.ds(at, 16), :].reshape(128, 256)
    back = dot(grad, cur, TN)
    for i in range(8):
        even, odd = back[16 * i : 16 * i + 16], back[128 + 16 * i : 128 + 16 * i + 16]
        sum_q[p, i, pl.ds(at, 8), :] += even[:8]
        sum_q[p, i, pl.ds(at + 8, 8), :] = even[8:] + odd[:8]
        sum_q[p, i, pl.ds(at + 16, 8), :] = odd[8:]


def cells_late(p, bb, dy, halo, cur_ref, cot_ref, sum_c, act_c, pre_c, out_ref, acc_ref):
    def rows_of(i, at):
        return halo[i, pl.ds(at, 32), :]

    win, vol = cell_block(p, bb, rows_of, cur_ref)
    at = pl.multiple_of(bb * 16, 16)
    cot = cot_ref[p, :, pl.ds(at, 16), :].reshape(128, 128).astype(F32)
    cot_rev = jnp.concatenate([flip8(cot[8 * i : 8 * i + 8]) for i in range(16)], axis=0)
    act_own, pre = act_c[p, bb], pre_c[p, bb]
    grads, acts = [], []
    for i in range(16):
        y, odd = divmod(i, 2)
        rows = slice(8 * i, 8 * i + 8)
        act, slope = activation(vol[rows, 128 * odd : 128 * odd + 128])
        grads.append(pre[rows] * slope)
        act = jnp.concatenate([act_own[rows], flip8(act)], axis=1)
        acts.append(skew(act, 249 - 16 * y))
    act = jnp.concatenate(acts, axis=0).astype(BF)
    acc_ref[p] += dot(cot_rev.astype(BF), act, TN)
    out = sum_c[p, bb] + dot(split_grads(grads), win)
    out_ref[p, :, pl.ds(at, 16), :] = out.astype(BF).reshape(8, 16, 256)


def rim_positions(p, left, rim_cur, rim_cot, prev_ref, wk, masks, rim_sum):
    at = pl.multiple_of(jnp.where(left, 112, 0), 16)
    prev = prev_ref[p, :, pl.ds(at, 16), :].reshape(128, 256)
    win = rim_cur[p].reshape(64, 256).astype(BF)
    vol = dot(win, prev, NT)
    pre = dot(rim_cot[p].reshape(64, 128).astype(BF), wk)
    mask = jnp.where(left, masks[1], masks[0])
    grads = []
    for i in range(8):
        rows = slice(8 * i, 8 * i + 8)
        piece = pre[rows] * mask
        piece = jnp.where(left, skew(piece, 16 * i + 8), skew(piece, 16 * i - 8))[:, :128]
        grads.append(piece * activation(vol[rows])[1])
    rim_sum[p] = dot(jnp.concatenate(grads, axis=0).astype(BF), win, TN)


def positions_late(
    p, bb, dx, left, halo, pre_halo, prev_ref, e_fold, masks, sum_q, rim_sum, out_ref
):
    at = pl.multiple_of(bb * 16, 16)
    prev = prev_ref[p, :, pl.ds(at, 16), :].reshape(128, 256)
    win = jnp.concatenate([halo[8 + i, pl.ds(at, 32), :][:24] for i in range(8)], axis=0)
    vol = dot(win, prev, NT)
    pre = dot(
        jnp.concatenate([pre_halo[i, pl.ds(at, 32), :][:24] for i in range(8)], axis=0), e_fold
    )
    grads = []
    for i in range(8):
        for g in range(3):
            rows = slice(24 * i + 8 * g, 24 * i + 8 * g + 8)
            piece = pre[rows]
            if g != 1:
                piece = piece * masks[g // 2][:, :128]
            shift = (16 * i + 8 * (g - 1)) % 128
            piece = pltpu.roll(piece, shift, 1, stride=1, stride_axis=0)
            grads.append(piece * activation(vol[rows])[1])
    out = dot(jnp.concatenate(grads, axis=0).astype(BF), win, TN)
    own = pltpu.roll(sum_q[p, :, pl.ds(at, 24), :], (20 + dx) % 24, 1)[:, :16].reshape(128, 256)
    rim = jnp.where(bb == jnp.where(left, 7, 0), 1.0, 0.0) * rim_sum[p]
    out_ref[p, :, pl.ds(at, 16), :] = (out + own + rim).astype(BF).reshape(8, 16, 256)


def kernel(
    norm, shift_ref, prev_hbm, cur_hbm, cot_hbm, w_ref, e_ref, eye_ref,
    gc_hbm, gp_hbm, gw_ref,
    prev_in, cur_in, cot_in, gc_ref, gp_ref,
    prev_ref, cur_ref, cot_ref, flat0, flat1, msg_r, rim_s, rim_r,
    edge_s, edge_r0, edge_r1, edge_cot_s, edge_cot_r, own0, own1, cot_x, own_pre, rim_cur, rim_cot,
    msg, tri_s, tri_r, halo0, halo1, pre_halo0, pre_halo1,
    sum_c, act_c, pre_c, sum_q, rim_sum, acc, ar0, ar1, ar2, ar3, ar4,
    side_ss, side_rs, row_ss, row_rs, s1, r1, s2, r2, s3, r3, s4, r4, load_sem, store_sem,
):
    row, col = lax.axis_index("row"), lax.axis_index("col")
    last = lax.axis_size("row") - 1
    left = col == 0
    owns = (own0, own1)
    halos, pre_halos = (halo0, halo1), (pre_halo0, pre_halo1)
    g1, g2, g3 = (row % 4) * 2 + col, (row // 4) % 4, row // 16

    def member(a, b, c):
        return ((c * 4 + b) * 4 + a // 2, a % 2)

    loads, stores = [], []
    for p in range(2):
        for source, target in ((prev_hbm, prev_in), (cur_hbm, cur_in), (cot_hbm, cot_in)):
            at = load_sem.at[len(loads)]
            loads.append(pltpu.make_async_copy(source.at[p], target.at[p], at))
        for source, target in ((gc_ref, gc_hbm), (gp_ref, gp_hbm)):
            at = store_sem.at[len(stores)]
            stores.append(pltpu.make_async_copy(source.at[p], target.at[p], at))
    for copy in loads:
        copy.start()

    barrier = pltpu.get_barrier_semaphore()

    def greet(target):
        pl.semaphore_signal(barrier, inc=1, device_id=target, device_id_type=MESH)

    for d in range(1, 8):
        greet(member((g1 + d) % 8, g2, g3))
    for d in range(1, 4):
        greet(member(g1, (g2 + d) % 4, g3))
        greet(member(g1, g2, (g3 + d) % 4))
    greet(((row + 1) % (last + 1), col))
    greet(((row + last) % (last + 1), col))

    def side(p, k):
        src, dst = (
            (edge_s.at[p], (edge_r0, edge_r1)[p]), (edge_cot_s.at[p], edge_cot_r.at[p])
        )[k]
        return pltpu.make_async_remote_copy(
            src_ref=src, dst_ref=dst, send_sem=side_ss.at[p, k],
            recv_sem=side_rs.at[p, k], device_id=(row, 1 - col), device_id_type=MESH,
        )

    def along(p, way, k):
        s, r = ((msg, msg_r), (rim_s, rim_r), (tri_s, tri_r))[k]
        src, dst = s.at[p, way], r.at[p, way]
        target = jnp.where(row == last, row, row + 1) if way else jnp.where(row == 0, row, row - 1)
        return pltpu.make_async_remote_copy(
            src_ref=src, dst_ref=dst, send_sem=row_ss.at[p, way, k],
            recv_sem=row_rs.at[p, way, k], device_id=(target, col), device_id_type=MESH,
        )

    def pack(p):
        dy = shift_ref[p, 0]

        def chunk(i, carry):
            at = pl.ds(pl.multiple_of(i * 16, 16), 16)
            pos = prev_in[p, at].astype(F32)
            cell = pltpu.roll(cur_in[p, at].astype(F32), (4 + dy) % 8, 1)
            low = iota((16, 8, 128), 1) < 4 + dy
            msg[p, 0, at] = jnp.where(low, pos, cell).astype(BF)
            msg[p, 1, at] = jnp.where(low, cell, pos).astype(BF)
            return carry

        lax.fori_loop(0, 16, chunk, 0)

    def send(p, k):
        @pl.when(row > 0)
        def _():
            along(p, 0, k).start()

        @pl.when(row < last)
        def _():
            along(p, 1, k).start()

    ident = jnp.where(iota((128, 128), 0) == iota((128, 128), 1), 1.0, 0.0).astype(BF)

    def spread_rows(flat, x):
        flat[0 : x.shape[0] * 8] = x.reshape(x.shape[0] * 8, 128)

    def picked(flat, y, channels):
        return flat[pl.ds(y, channels, stride=8), :].astype(BF)

    def aligner(offset):
        take = iota((WIDE, 128), 1) + 8 == iota((WIDE, 128), 0) + offset
        return jnp.where(take, 1.0, 0.0).astype(BF)

    def rim_place(tile, offset):
        tile = pltpu.roll(tile, offset % 8, tile.ndim - 2)
        at = iota(tile.shape, tile.ndim - 2)
        keep = jnp.where(left, at, -1 - at) >= jnp.where(left, offset, -offset)
        return jnp.where(keep, tile, 0.0)

    def rim_add(x, rim):
        zero = jnp.zeros_like(rim)
        low, high = jnp.where(left, zero, rim), jnp.where(left, rim, zero)
        return jnp.concatenate([x[:8] + low, x[8:128], x[128:136] + high, x[136:]], axis=0)

    def turn_prev(p):
        both = jnp.concatenate([ident, aligner(4 + shift_ref[p, 1])], axis=0)
        spread_rows(flat0, prev_in[p].astype(F32))
        for y in range(8):
            x = dot(both, picked(flat0, y, 256), NT).astype(BF)
            prev_ref[p, y] = x[:128]
            owns[p][y] = x[128:]

    def turn_cells(p):
        both = jnp.concatenate([ident, aligner(4 - shift_ref[p, 1])], axis=0)
        spread_rows(flat1, cur_in[p].astype(F32))
        for y in range(8):
            cur_ref[p, y] = dot(ident, picked(flat1, y, 256), NT).astype(BF)
        spread_rows(flat0, cot_in[p].astype(F32))
        for y in range(8):
            x = dot(both, picked(flat0, y, 128), NT)
            cot_ref[p, y] = x[:128].astype(BF)
            cot_x[p, y] = x[128:]

    start = jnp.where(left, 112, 0)

    def edges(p):
        for y in range(8):
            pick = []
            for ref in (prev_ref, cur_ref):
                tile = ref[p, y, pl.ds(pl.multiple_of(start, 16), 16), :].astype(F32)
                pick.append(jnp.where(left, tile[8:], tile[:8]))
            edge_s[p, y] = jnp.concatenate(pick, axis=0).astype(BF)
        for y in range(0, 8, 2):
            pick = []
            for yy in (y, y + 1):
                tile = cot_ref[p, yy, pl.ds(pl.multiple_of(start, 16), 16), :].astype(F32)
                pick.append(jnp.where(left, tile[8:], tile[:8]))
            edge_cot_s[p, y // 2] = jnp.concatenate(pick, axis=0).astype(BF)
        for k in range(2):
            side(p, k).start()

    for copy in loads[:2]:
        copy.wait()
    pack(0)
    pl.semaphore_wait(barrier, 15)
    send(0, 0)
    for copy in loads[2:]:
        copy.wait()
    turn_prev(0)
    turn_cells(0)
    edges(0)
    pack(1)
    turn_prev(1)
    turn_cells(1)
    edges(1)

    w81 = w_ref[...]
    e = e_ref[...]
    w9 = dot(w81, eye_ref[...], TN).astype(BF)
    wk = dot(w9, e)
    e_fold = (e[:, :128].astype(F32) + e[:, 128:].astype(F32)).astype(BF)
    turns = [(16 * (shift_ref[p, 0] + 12)) % 256 for p in range(2)]
    back = [(16 * (4 - shift_ref[p, 0])) % 256 for p in range(2)]
    wks = [pltpu.roll(wk, turns[p], 1).astype(BF) for p in range(2)]
    sub, lane = iota((8, 256), 0), iota((8, 256), 1) % 16
    masks = (jnp.where(lane >= 8 - sub, 1.0, 0.0), jnp.where(lane < 8 - sub, 1.0, 0.0))
    tri_lane = iota((WIDE, 128), 1)
    acc[...] = jnp.zeros_like(acc)
    sum_q[:, :, 0:8] = jnp.zeros((2, 8, 8, 256), F32)

    def join(p):
        dy, dx = shift_ref[p, 0], shift_ref[p, 1]
        own, edge_r = owns[p], (edge_r0, edge_r1)[p]
        for k in range(2):
            side(p, k).wait()
        for y in range(8):
            edge = edge_r[y].astype(F32)
            rim = rim_place(edge[:8], 4 - dx)
            zero = jnp.zeros_like(rim)
            for at, piece in ((0, jnp.where(left, zero, rim)), (128, jnp.where(left, rim, zero))):
                tile = own[y, at : at + 16].astype(F32) + jnp.concatenate([piece, zero], axis=0)
                own[y, at : at + 16] = tile.astype(BF)
            rim_cur[p, y] = rim_place(edge[8:], 4 + dx)
            at = 8 * (y % 2)
            rim = rim_place(edge_cot_r[p, y // 2].astype(F32)[at : at + 8], 4 + dx)
            rim_cot[p, y] = rim
            own_pre[y] = dot(rim_add(cot_x[p, y], rim).astype(BF), w9)

        def tile(s, up):
            is_prev = (s < 4 + dy) if up else (s >= 4 + dy)
            at = jnp.where(is_prev, s, jnp.where(s < 4 + dy, s + 4 - dy, s - 4 - dy))
            both = edge_r[at].astype(F32)
            return jnp.where(is_prev, both[:8], both[8:])

        for k in range(4):
            for way in range(2):
                pair = [tile(2 * k, way == 0), tile(2 * k + 1, way == 0)]
                rim_s[p, way, k] = jnp.concatenate(pair, axis=0).astype(BF)

        def cell_row(t):
            return own_pre[jnp.where(t < 4 + dy, t + 4 - dy, t - 4 - dy)]

        for s in range(4):
            near, away = cell_row(s), cell_row(7 - s)
            tri_s[p, 1, s] = jnp.where(
                tri_lane >= 9 * (8 - s), near, pltpu.roll(away, 128 - 9 * (s + 1), 1)
            ).astype(BF)
            tri_s[p, 0, s] = jnp.where(
                tri_lane < 9 * (8 - s), near, pltpu.roll(away, 9 * (8 - s), 1)
            ).astype(BF)
        send(p, 1)
        send(p, 2)

    join(0)
    send(1, 0)
    join(1)

    def arrive(p):
        dy, dx = shift_ref[p, 0], shift_ref[p, 1]
        halo = halos[p]
        take_p, take_c = aligner(4 + dx), aligner(4 - dx)

        def receive(k, buffer):
            for way, edge_row in ((1, 0), (0, last)):

                @pl.when(row != edge_row)
                def _():
                    along(p, way, k).wait_recv()

                @pl.when(row == edge_row)
                def _():
                    part = buffer.at[p, way]
                    part[...] = jnp.zeros(part.shape, BF)

        for k, buffer in enumerate((msg_r, rim_r, tri_r)):
            receive(k, buffer)

        def sort(i, carry):
            at = pl.ds(pl.multiple_of(i * 16, 16), 16)
            to = pl.ds(pl.multiple_of(i * 128, 128), 128)
            up, down = msg_r[p, 0, at].astype(F32), msg_r[p, 1, at].astype(F32)
            low = iota((16, 8, 128), 1) < 4 + dy
            flat0[to] = jnp.where(low, up, down).reshape(128, 128)
            flat1[to] = jnp.where(low, down, up).reshape(128, 128)
            return carry

        lax.fori_loop(0, 16, sort, 0)
        for s in range(8):
            at = 8 * (s % 2)
            up = rim_r[p, 0, s // 2].astype(F32)[at : at + 8]
            down = rim_r[p, 1, s // 2].astype(F32)[at : at + 8]
            low = s < 4 + dy
            x = dot(take_p, picked(flat0, s, 256), NT)
            rim = rim_place(jnp.where(low, up, down), 4 - dx)
            halo[s] = rim_add(x, rim).astype(BF)
            x = dot(take_c, picked(flat1, s, 256), NT)
            rim = rim_place(jnp.where(low, down, up), 4 + dx)
            halo[8 + s] = rim_add(x, rim).astype(BF)
        for s in range(4):
            up, down = tri_r[p, 0, s].astype(F32), tri_r[p, 1, s].astype(F32)
            near = tri_lane >= 9 * (8 - s)
            x = jnp.where(near == (s < 4 + dy), jnp.where(s < 4 + dy, down, up), 0.0)
            pre_halos[p][s] = x.astype(BF)
            down = pltpu.roll(down, 9 * (s + 1), 1)
            up = pltpu.roll(up, 128 - 9 * (8 - s), 1)
            near = tri_lane >= 9 * (s + 1)
            x = jnp.where(near == (7 - s < 4 + dy), jnp.where(7 - s < 4 + dy, down, up), 0.0)
            pre_halos[p][7 - s] = jnp.where(tri_lane < 81, x, 0.0).astype(BF)

    def loop(lo, hi, work):
        def body(bb, carry):
            work(bb)
            return carry

        lax.fori_loop(lo, hi, body, 0)

    def early(p):
        def work(i):
            for bb in (2 * i, 2 * i + 1):
                cells_early(
                    p, bb, owns[p], cur_ref, cot_ref, wks[p], sum_c, act_c, pre_c, sum_q)

        loop(0, 4, work)
        rim_positions(p, left, rim_cur, rim_cot, prev_ref, wks[p], masks, rim_sum)

    def late_cells(p, bb):
        cells_late(
            p, bb, shift_ref[p, 0], halos[p], cur_ref, cot_ref, sum_c, act_c, pre_c, gc_ref, acc)

    def late_positions(p, bb):
        positions_late(
            p, bb, shift_ref[p, 1], left, halos[p], pre_halos[p], prev_ref, e_fold, masks,
            sum_q, rim_sum, gp_ref)

    def late(i):
        for bb in (2 * i, 2 * i + 1):
            late_cells(0, bb)
            late_positions(0, bb)

    early(0)
    early(1)
    arrive(0)
    loop(0, 4, late)
    stores[0].start()
    stores[1].start()
    arrive(1)
    loop(0, 2, lambda i: [late_cells(1, 4 * i + k) for k in range(4)])

    stores[2].start()

    turned = (pltpu.roll(acc[0], back[0], 1) + pltpu.roll(acc[1], back[1], 1)).T
    for u in range(9):
        ar0[9 * u : 9 * u + 9] = turned[16 * u : 16 * u + 9]
    ar0[81:128] = jnp.zeros((47, 128), F32)

    def share(ref, i):
        return ref.at[pl.ds(pl.multiple_of(i * 16, 16), 16)]

    def first(d):
        peer = (g1 + d) % 8
        return pltpu.make_async_remote_copy(
            src_ref=share(ar0, peer), dst_ref=ar1.at[g1], send_sem=s1.at[peer],
            recv_sem=r1.at[g1], device_id=member(peer, g2, g3), device_id_type=MESH,
        )

    def second(d):
        peer = (g2 + d) % 4
        return pltpu.make_async_remote_copy(
            src_ref=ar2.at[g2], dst_ref=ar2.at[g2], send_sem=s2.at[peer],
            recv_sem=r2.at[g2], device_id=member(g1, peer, g3), device_id_type=MESH,
        )

    def third(d):
        peer = (g3 + d) % 4
        return pltpu.make_async_remote_copy(
            src_ref=ar3.at[g3], dst_ref=ar3.at[g3], send_sem=s3.at[peer],
            recv_sem=r3.at[g3], device_id=member(g1, g2, peer), device_id_type=MESH,
        )

    def fourth(d):
        peer = (g1 + d) % 8
        return pltpu.make_async_remote_copy(
            src_ref=ar4.at[g1], dst_ref=ar4.at[g1], send_sem=s4.at[peer],
            recv_sem=r4.at[g1], device_id=member(peer, g2, g3), device_id_type=MESH,
        )

    def got(buffer, sends, receives, source):
        pltpu.make_async_remote_copy(
            src_ref=buffer.at[source], dst_ref=buffer.at[source], send_sem=sends.at[source],
            recv_sem=receives.at[source], device_id=(row, 1 - col), device_id_type=MESH,
        ).wait_recv()

    def some_positions(lo, hi):
        loop(0, 1, lambda i: [late_positions(1, k) for k in range(lo, hi)])

    for d in range(1, 8):
        first(d).start()
    some_positions(0, 2)
    ar1[g1] = ar0[pl.ds(pl.multiple_of(g1 * 16, 16), 16)]
    for d in range(1, 8):
        first(d).wait_send()
        got(ar1, s1, r1, (g1 + d) % 8)
    ar2[g2] = jnp.sum(ar1[...], axis=0)
    for d in range(1, 4):
        second(d).start()
    some_positions(2, 4)
    for d in range(1, 4):
        second(d).wait_send()
        got(ar2, s2, r2, (g2 + d) % 4)
    ar3[g3] = jnp.sum(ar2[...], axis=0)
    for d in range(1, 4):
        third(d).start()
    some_positions(4, 6)
    for d in range(1, 4):
        third(d).wait_send()
        got(ar3, s3, r3, (g3 + d) % 4)
    ar4[g1] = jnp.sum(ar3[...], axis=0)
    for d in range(1, 8):
        fourth(d).start()
    some_positions(6, 8)
    stores[3].start()
    for d in range(1, 8):
        fourth(d).wait_send()
        got(ar4, s4, r4, (g1 + d) % 8)
    gw_ref[...] = ar4[...].reshape(128, 128)[:81] * norm
    for copy in stores:
        copy.wait()

    for p in range(2):
        for k in range(3):

            @pl.when(row > 0)
            def _():
                along(p, 0, k).wait_send()

            @pl.when(row < last)
            def _():
                along(p, 1, k).wait_send()


def spread_matrix():
    e = np.zeros((128, 256), np.float32)
    for u in range(9):
        for v in range(9):
            e[9 * u + v, 16 * u + v] = 1.0 / 32.0
    return e


def local(current, previous, shift, weight, cotangent):
    pairs, channels, rows, cols = current.shape
    e = jnp.asarray(spread_matrix(), BF)
    eye = jnp.asarray(np.eye(81, 128), BF)
    total = pairs * rows * lax.axis_size("row") * cols * lax.axis_size("col")
    vmem = pl.BlockSpec(memory_space=pltpu.VMEM)
    hbm = pl.BlockSpec(memory_space=pl.ANY)
    dma = pltpu.SemaphoreType.DMA
    v = pltpu.VMEM
    gc, gp, gw = pl.pallas_call(
        functools.partial(kernel, 1.0 / math.sqrt(total)),
        in_specs=[pl.BlockSpec(memory_space=pltpu.SMEM)] + [hbm] * 3 + [vmem] * 3,
        out_specs=[hbm, hbm, vmem],
        out_shape=[
            jax.ShapeDtypeStruct((2, 8, 128, 256), BF),
            jax.ShapeDtypeStruct((2, 8, 128, 256), BF),
            jax.ShapeDtypeStruct((81, 128), F32),
        ],
        scratch_shapes=[
            v((2, 256, 8, 128), BF), v((2, 256, 8, 128), BF), v((2, 128, 8, 128), BF),
            v((2, 8, 128, 256), BF), v((2, 8, 128, 256), BF),
            v((2, 8, 128, 256), BF), v((2, 8, 128, 256), BF), v((2, 8, 128, 128), BF),
            v((2048, 128), F32), v((2048, 128), F32),
            v((2, 2, 256, 8, 128), BF), v((2, 2, 4, 16, 256), BF), v((2, 2, 4, 16, 256), BF),
            v((2, 8, 16, 256), BF), v((8, 16, 256), BF), v((8, 16, 256), BF),
            v((2, 4, 16, 128), BF), v((2, 4, 16, 128), BF),
            v((8, WIDE, 256), BF), v((8, WIDE, 256), BF),
            v((2, 8, WIDE, 128), F32), v((8, WIDE, 128), F32),
            v((2, 8, 8, 256), F32), v((2, 8, 8, 128), F32),
            v((2, 2, 256, 8, 128), BF),
            v((2, 2, 4, WIDE, 128), BF), v((2, 2, 4, WIDE, 128), BF),
            v((16, WIDE, 256), BF), v((16, WIDE, 256), BF),
            v((8, WIDE, 128), BF), v((8, WIDE, 128), BF),
            v((2, 8, 128, 256), F32),
            v((2, 8, 128, 128), F32), v((2, 8, 128, 128), F32),
            v((2, 8, WIDE, 256), F32), v((2, 128, 256), F32),
            v((2, 128, 256), F32),
            v((128, 128), F32), v((8, 16, 128), F32), v((4, 16, 128), F32), v((4, 16, 128), F32),
            v((8, 16, 128), F32),
            dma((2, 2)), dma((2, 2)), dma((2, 2, 3)), dma((2, 2, 3)),
            dma((8,)), dma((8,)), dma((4,)), dma((4,)), dma((4,)), dma((4,)), dma((8,)), dma((8,)),
            dma((6,)), dma((4,)),
        ],
        compiler_params=pltpu.CompilerParams(
            collective_id=0, has_side_effects=True, vmem_limit_bytes=56 << 20
        ),
        cost_estimate=pl.CostEstimate(
            flops=3_000_000_000, bytes_accessed=8 << 20, transcendentals=1_500_000
        ),
    )(shift, previous, current, cotangent, weight.T, e, eye)
    return gc.transpose(0, 3, 1, 2), gp.transpose(0, 3, 1, 2), gw.T


def solution(mesh):
    grid = P(None, None, "row", "col")
    return jax.shard_map(
        local,
        mesh=mesh,
        in_specs=(grid, grid, P(), P(), grid),
        out_specs=(grid, grid, P()),
        check_vma=False,
    )
```

```python
import functools
import math

import jax
import jax.numpy as jnp
import numpy as np
from jax import lax
from jax.experimental import pallas as pl
from jax.experimental.pallas import tpu as pltpu
from jax.sharding import PartitionSpec as P

BF = jnp.bfloat16
F32 = jnp.float32
MESH = pl.DeviceIdType.MESH
NT = (((1,), (1,)), ((), ()))
TN = (((0,), (0,)), ((), ()))
NN = (((1,), (0,)), ((), ()))
WIDE = 144


def dot(a, b, dims=NN):
    return lax.dot_general(a, b, dims, preferred_element_type=F32)


def iota(shape, axis):
    return lax.broadcasted_iota(jnp.int32, shape, axis)


def skew(x, shift):
    return pltpu.roll(x, shift % 256, 1, stride=1, stride_axis=0)


def flip8(x):
    idx = 7 - iota((8, 128), 0)
    parts = [
        jnp.take_along_axis(x[:, at : at + 128], idx, axis=0) for at in range(0, x.shape[1], 128)
    ]
    return parts[0] if len(parts) == 1 else jnp.concatenate(parts, axis=1)


def activation(vol_dot):
    half = vol_dot * (1.0 / 32.0)
    q = 1.0 + jnp.tanh(half)
    act = half * q
    return act, q + act * (2.0 - q)


def cell_block(p, bb, rows_of, cur_ref):
    at = pl.multiple_of(bb * 16, 16)
    cur = cur_ref[p, :, pl.ds(at, 16), :].reshape(128, 256)
    rows = [rows_of(i, at) for i in range(8)]
    win = jnp.concatenate([r[0:16] for r in rows] + [r[8:24] for r in rows], axis=0)
    return win, dot(cur, win, NT)


def split_grads(grads):
    zero = jnp.zeros((8, 128), F32)
    full = [
        jnp.concatenate([zero, g] if i % 2 else [g, zero], axis=1) for i, g in enumerate(grads)
    ]
    return jnp.concatenate(full, axis=0).astype(BF)


def cells_early(p, bb, own, cur_ref, cot_ref, wk, sum_c, act_c, pre_c, sum_q):
    win, vol = cell_block(p, bb, lambda i, at: own[i, pl.ds(at, 32), :], cur_ref)
    at = pl.multiple_of(bb * 16, 16)
    pre = dot(cot_ref[p, :, pl.ds(at, 16), :].reshape(128, 128), wk)
    grads, acts, rest = [], [], []
    for i in range(16):
        y, odd = divmod(i, 2)
        rows = slice(8 * i, 8 * i + 8)
        act, slope = activation(vol[rows, 128 * odd : 128 * odd + 128])
        piece = skew(pre[rows], 16 * y)
        grads.append(piece[:, :128] * slope)
        rest.append(piece[:, 128:])
        acts.append(flip8(act))
    act_c[p, bb] = jnp.concatenate(acts, axis=0)
    pre_c[p, bb] = jnp.concatenate(rest, axis=0)
    grad = split_grads(grads)
    sum_c[p, bb] = dot(grad, win)
    cur = cur_ref[p, :, pl.ds(at, 16), :].reshape(128, 256)
    back = dot(grad, cur, TN)
    for i in range(8):
        even, odd = back[16 * i : 16 * i + 16], back[128 + 16 * i : 128 + 16 * i + 16]
        sum_q[p, i, pl.ds(at, 8), :] += even[:8]
        sum_q[p, i, pl.ds(at + 8, 8), :] = even[8:] + odd[:8]
        sum_q[p, i, pl.ds(at + 16, 8), :] = odd[8:]


def cells_late(p, bb, dy, halo, cur_ref, cot_ref, sum_c, act_c, pre_c, out_ref, acc_ref):
    def rows_of(i, at):
        return halo[i, pl.ds(at, 32), :]

    win, vol = cell_block(p, bb, rows_of, cur_ref)
    at = pl.multiple_of(bb * 16, 16)
    cot = cot_ref[p, :, pl.ds(at, 16), :].reshape(128, 128).astype(F32)
    cot_rev = jnp.concatenate([flip8(cot[8 * i : 8 * i + 8]) for i in range(16)], axis=0)
    act_own, pre = act_c[p, bb], pre_c[p, bb]
    grads, acts = [], []
    for i in range(16):
        y, odd = divmod(i, 2)
        rows = slice(8 * i, 8 * i + 8)
        act, slope = activation(vol[rows, 128 * odd : 128 * odd + 128])
        grads.append(pre[rows] * slope)
        act = jnp.concatenate([act_own[rows], flip8(act)], axis=1)
        acts.append(skew(act, 249 - 16 * y))
    act = jnp.concatenate(acts, axis=0).astype(BF)
    acc_ref[p] += dot(cot_rev.astype(BF), act, TN)
    out = sum_c[p, bb] + dot(split_grads(grads), win)
    out_ref[p, :, pl.ds(at, 16), :] = out.astype(BF).reshape(8, 16, 256)


def rim_positions(p, left, rim_cur, rim_cot, prev_ref, wk, masks, rim_sum):
    at = pl.multiple_of(jnp.where(left, 112, 0), 16)
    prev = prev_ref[p, :, pl.ds(at, 16), :].reshape(128, 256)
    win = rim_cur[p].reshape(64, 256).astype(BF)
    vol = dot(win, prev, NT)
    pre = dot(rim_cot[p].reshape(64, 128).astype(BF), wk)
    mask = jnp.where(left, masks[1], masks[0])
    grads = []
    for i in range(8):
        rows = slice(8 * i, 8 * i + 8)
        piece = pre[rows] * mask
        piece = jnp.where(left, skew(piece, 16 * i + 8), skew(piece, 16 * i - 8))[:, :128]
        grads.append(piece * activation(vol[rows])[1])
    rim_sum[p] = dot(jnp.concatenate(grads, axis=0).astype(BF), win, TN)


def positions_late(
    p, bb, dx, left, halo, pre_halo, prev_ref, e_fold, masks, sum_q, rim_sum, out_ref
):
    at = pl.multiple_of(bb * 16, 16)
    prev = prev_ref[p, :, pl.ds(at, 16), :].reshape(128, 256)
    win = jnp.concatenate([halo[8 + i, pl.ds(at, 32), :][:24] for i in range(8)], axis=0)
    vol = dot(win, prev, NT)
    pre = dot(
        jnp.concatenate([pre_halo[i, pl.ds(at, 32), :][:24] for i in range(8)], axis=0), e_fold
    )
    grads = []
    for i in range(8):
        for g in range(3):
            rows = slice(24 * i + 8 * g, 24 * i + 8 * g + 8)
            piece = pre[rows]
            if g != 1:
                piece = piece * masks[g // 2][:, :128]
            shift = (16 * i + 8 * (g - 1)) % 128
            piece = pltpu.roll(piece, shift, 1, stride=1, stride_axis=0)
            grads.append(piece * activation(vol[rows])[1])
    out = dot(jnp.concatenate(grads, axis=0).astype(BF), win, TN)
    own = pltpu.roll(sum_q[p, :, pl.ds(at, 24), :], (20 + dx) % 24, 1)[:, :16].reshape(128, 256)
    rim = jnp.where(bb == jnp.where(left, 7, 0), 1.0, 0.0) * rim_sum[p]
    out_ref[p, :, pl.ds(at, 16), :] = (out + own + rim).astype(BF).reshape(8, 16, 256)


def kernel(
    norm, shift_ref, prev_hbm, cur_hbm, cot_hbm, w_ref, e_ref, eye_ref,
    gc_hbm, gp_hbm, gw_ref,
    prev_in, cur_in, cot_in, gc_ref, gp_ref,
    prev_ref, cur_ref, cot_ref, flat0, flat1, msg_r, rim_s, rim_r,
    edge_s, edge_r0, edge_r1, edge_cot_s, edge_cot_r, own0, own1, cot_x, own_pre, rim_cur, rim_cot,
    msg, tri_s, tri_r, halo0, halo1, pre_halo0, pre_halo1,
    sum_c, act_c, pre_c, sum_q, rim_sum, acc, ar0, ar1, ar2, ar3,
    side_ss, side_rs, row_ss, row_rs, s1, r1, s2, r2, s3, r3, load_sem, store_sem,
):
    row, col = lax.axis_index("row"), lax.axis_index("col")
    last = lax.axis_size("row") - 1
    left = col == 0
    owns = (own0, own1)
    halos, pre_halos = (halo0, halo1), (pre_halo0, pre_halo1)
    g1, g2 = (row % 4) * 2 + col, row // 4

    def member(a, b):
        return (b * 4 + a // 2, a % 2)

    loads, stores = [], []
    for p in range(2):
        for source, target in ((prev_hbm, prev_in), (cur_hbm, cur_in), (cot_hbm, cot_in)):
            at = load_sem.at[len(loads)]
            loads.append(pltpu.make_async_copy(source.at[p], target.at[p], at))
        for source, target in ((gc_ref, gc_hbm), (gp_ref, gp_hbm)):
            at = store_sem.at[len(stores)]
            stores.append(pltpu.make_async_copy(source.at[p], target.at[p], at))
    for copy in loads:
        copy.start()

    barrier = pltpu.get_barrier_semaphore()

    def greet(target):
        pl.semaphore_signal(barrier, inc=1, device_id=target, device_id_type=MESH)

    for d in range(1, 8):
        greet(member((g1 + d) % 8, g2))
    for d in range(1, 16):
        greet(member(g1, (g2 + d) % 16))
    greet(((row + 1) % (last + 1), col))
    greet(((row + last) % (last + 1), col))

    def side(p, k):
        src, dst = (
            (edge_s.at[p], (edge_r0, edge_r1)[p]), (edge_cot_s.at[p], edge_cot_r.at[p])
        )[k]
        return pltpu.make_async_remote_copy(
            src_ref=src, dst_ref=dst, send_sem=side_ss.at[p, k],
            recv_sem=side_rs.at[p, k], device_id=(row, 1 - col), device_id_type=MESH,
        )

    def along(p, way, k):
        s, r = ((msg, msg_r), (rim_s, rim_r), (tri_s, tri_r))[k]
        src, dst = s.at[p, way], r.at[p, way]
        target = jnp.where(row == last, row, row + 1) if way else jnp.where(row == 0, row, row - 1)
        return pltpu.make_async_remote_copy(
            src_ref=src, dst_ref=dst, send_sem=row_ss.at[p, way, k],
            recv_sem=row_rs.at[p, way, k], device_id=(target, col), device_id_type=MESH,
        )

    def pack(p):
        dy = shift_ref[p, 0]

        def chunk(i, carry):
            at = pl.ds(pl.multiple_of(i * 16, 16), 16)
            pos = prev_in[p, at].astype(F32)
            cell = pltpu.roll(cur_in[p, at].astype(F32), (4 + dy) % 8, 1)
            low = iota((16, 8, 128), 1) < 4 + dy
            msg[p, 0, at] = jnp.where(low, pos, cell).astype(BF)
            msg[p, 1, at] = jnp.where(low, cell, pos).astype(BF)
            return carry

        lax.fori_loop(0, 16, chunk, 0)

    def send(p, k):
        @pl.when(row > 0)
        def _():
            along(p, 0, k).start()

        @pl.when(row < last)
        def _():
            along(p, 1, k).start()

    ident = jnp.where(iota((128, 128), 0) == iota((128, 128), 1), 1.0, 0.0).astype(BF)

    def spread_rows(flat, x):
        flat[0 : x.shape[0] * 8] = x.reshape(x.shape[0] * 8, 128)

    def picked(flat, y, channels):
        return flat[pl.ds(y, channels, stride=8), :].astype(BF)

    def aligner(offset):
        take = iota((WIDE, 128), 1) + 8 == iota((WIDE, 128), 0) + offset
        return jnp.where(take, 1.0, 0.0).astype(BF)

    def rim_place(tile, offset):
        tile = pltpu.roll(tile, offset % 8, tile.ndim - 2)
        at = iota(tile.shape, tile.ndim - 2)
        keep = jnp.where(left, at, -1 - at) >= jnp.where(left, offset, -offset)
        return jnp.where(keep, tile, 0.0)

    def rim_add(x, rim):
        zero = jnp.zeros_like(rim)
        low, high = jnp.where(left, zero, rim), jnp.where(left, rim, zero)
        return jnp.concatenate([x[:8] + low, x[8:128], x[128:136] + high, x[136:]], axis=0)

    def turn_prev(p):
        both = jnp.concatenate([ident, aligner(4 + shift_ref[p, 1])], axis=0)
        spread_rows(flat0, prev_in[p].astype(F32))
        for y in range(8):
            x = dot(both, picked(flat0, y, 256), NT).astype(BF)
            prev_ref[p, y] = x[:128]
            owns[p][y] = x[128:]

    def turn_cells(p):
        both = jnp.concatenate([ident, aligner(4 - shift_ref[p, 1])], axis=0)
        spread_rows(flat1, cur_in[p].astype(F32))
        for y in range(8):
            cur_ref[p, y] = dot(ident, picked(flat1, y, 256), NT).astype(BF)
        spread_rows(flat0, cot_in[p].astype(F32))
        for y in range(8):
            x = dot(both, picked(flat0, y, 128), NT)
            cot_ref[p, y] = x[:128].astype(BF)
            cot_x[p, y] = x[128:]

    start = jnp.where(left, 112, 0)

    def edges(p):
        for y in range(8):
            pick = []
            for ref in (prev_ref, cur_ref):
                tile = ref[p, y, pl.ds(pl.multiple_of(start, 16), 16), :].astype(F32)
                pick.append(jnp.where(left, tile[8:], tile[:8]))
            edge_s[p, y] = jnp.concatenate(pick, axis=0).astype(BF)
        for y in range(0, 8, 2):
            pick = []
            for yy in (y, y + 1):
                tile = cot_ref[p, yy, pl.ds(pl.multiple_of(start, 16), 16), :].astype(F32)
                pick.append(jnp.where(left, tile[8:], tile[:8]))
            edge_cot_s[p, y // 2] = jnp.concatenate(pick, axis=0).astype(BF)
        for k in range(2):
            side(p, k).start()

    for copy in loads[:2]:
        copy.wait()
    pack(0)
    pl.semaphore_wait(barrier, 24)
    send(0, 0)
    for copy in loads[2:]:
        copy.wait()
    turn_prev(0)
    turn_cells(0)
    edges(0)
    pack(1)
    turn_prev(1)

    w81 = w_ref[...]
    e = e_ref[...]
    w9 = dot(w81, eye_ref[...], TN).astype(BF)
    wk = dot(w9, e)
    e_fold = (e[:, :128].astype(F32) + e[:, 128:].astype(F32)).astype(BF)
    turns = [(16 * (shift_ref[p, 0] + 12)) % 256 for p in range(2)]
    back = [(16 * (4 - shift_ref[p, 0])) % 256 for p in range(2)]
    wks = [pltpu.roll(wk, turns[p], 1).astype(BF) for p in range(2)]
    sub, lane = iota((8, 256), 0), iota((8, 256), 1) % 16
    masks = (jnp.where(lane >= 8 - sub, 1.0, 0.0), jnp.where(lane < 8 - sub, 1.0, 0.0))
    tri_lane = iota((WIDE, 128), 1)
    acc[...] = jnp.zeros_like(acc)
    sum_q[:, :, 0:8] = jnp.zeros((2, 8, 8, 256), F32)

    def join(p):
        dy, dx = shift_ref[p, 0], shift_ref[p, 1]
        own, edge_r = owns[p], (edge_r0, edge_r1)[p]
        for k in range(2):
            side(p, k).wait()
        for y in range(8):
            edge = edge_r[y].astype(F32)
            rim = rim_place(edge[:8], 4 - dx)
            zero = jnp.zeros_like(rim)
            for at, piece in ((0, jnp.where(left, zero, rim)), (128, jnp.where(left, rim, zero))):
                tile = own[y, at : at + 16].astype(F32) + jnp.concatenate([piece, zero], axis=0)
                own[y, at : at + 16] = tile.astype(BF)
            rim_cur[p, y] = rim_place(edge[8:], 4 + dx)
            at = 8 * (y % 2)
            rim = rim_place(edge_cot_r[p, y // 2].astype(F32)[at : at + 8], 4 + dx)
            rim_cot[p, y] = rim
            own_pre[y] = dot(rim_add(cot_x[p, y], rim).astype(BF), w9)

        def tile(s, up):
            is_prev = (s < 4 + dy) if up else (s >= 4 + dy)
            at = jnp.where(is_prev, s, jnp.where(s < 4 + dy, s + 4 - dy, s - 4 - dy))
            both = edge_r[at].astype(F32)
            return jnp.where(is_prev, both[:8], both[8:])

        for k in range(4):
            for way in range(2):
                pair = [tile(2 * k, way == 0), tile(2 * k + 1, way == 0)]
                rim_s[p, way, k] = jnp.concatenate(pair, axis=0).astype(BF)

        def cell_row(t):
            return own_pre[jnp.where(t < 4 + dy, t + 4 - dy, t - 4 - dy)]

        for s in range(4):
            near, away = cell_row(s), cell_row(7 - s)
            tri_s[p, 1, s] = jnp.where(
                tri_lane >= 9 * (8 - s), near, pltpu.roll(away, 128 - 9 * (s + 1), 1)
            ).astype(BF)
            tri_s[p, 0, s] = jnp.where(
                tri_lane < 9 * (8 - s), near, pltpu.roll(away, 9 * (8 - s), 1)
            ).astype(BF)
        send(p, 1)
        send(p, 2)

    join(0)
    send(1, 0)
    turn_cells(1)
    edges(1)

    def arrive(p):
        dy, dx = shift_ref[p, 0], shift_ref[p, 1]
        halo = halos[p]
        take_p, take_c = aligner(4 + dx), aligner(4 - dx)

        def receive(k, buffer):
            for way, edge_row in ((1, 0), (0, last)):

                @pl.when(row != edge_row)
                def _():
                    along(p, way, k).wait_recv()

                @pl.when(row == edge_row)
                def _():
                    part = buffer.at[p, way]
                    part[...] = jnp.zeros(part.shape, BF)

        for k, buffer in enumerate((msg_r, rim_r, tri_r)):
            receive(k, buffer)

        def sort(i, carry):
            at = pl.ds(pl.multiple_of(i * 16, 16), 16)
            to = pl.ds(pl.multiple_of(i * 128, 128), 128)
            up, down = msg_r[p, 0, at].astype(F32), msg_r[p, 1, at].astype(F32)
            low = iota((16, 8, 128), 1) < 4 + dy
            flat0[to] = jnp.where(low, up, down).reshape(128, 128)
            flat1[to] = jnp.where(low, down, up).reshape(128, 128)
            return carry

        lax.fori_loop(0, 16, sort, 0)
        for s in range(8):
            at = 8 * (s % 2)
            up = rim_r[p, 0, s // 2].astype(F32)[at : at + 8]
            down = rim_r[p, 1, s // 2].astype(F32)[at : at + 8]
            low = s < 4 + dy
            x = dot(take_p, picked(flat0, s, 256), NT)
            rim = rim_place(jnp.where(low, up, down), 4 - dx)
            halo[s] = rim_add(x, rim).astype(BF)
            x = dot(take_c, picked(flat1, s, 256), NT)
            rim = rim_place(jnp.where(low, down, up), 4 + dx)
            halo[8 + s] = rim_add(x, rim).astype(BF)
        for s in range(4):
            up, down = tri_r[p, 0, s].astype(F32), tri_r[p, 1, s].astype(F32)
            near = tri_lane >= 9 * (8 - s)
            x = jnp.where(near == (s < 4 + dy), jnp.where(s < 4 + dy, down, up), 0.0)
            pre_halos[p][s] = x.astype(BF)
            down = pltpu.roll(down, 9 * (s + 1), 1)
            up = pltpu.roll(up, 128 - 9 * (8 - s), 1)
            near = tri_lane >= 9 * (s + 1)
            x = jnp.where(near == (7 - s < 4 + dy), jnp.where(7 - s < 4 + dy, down, up), 0.0)
            pre_halos[p][7 - s] = jnp.where(tri_lane < 81, x, 0.0).astype(BF)

    def loop(lo, hi, work):
        def body(bb, carry):
            work(bb)
            return carry

        lax.fori_loop(lo, hi, body, 0)

    def early(p):
        def work(i):
            for bb in (2 * i, 2 * i + 1):
                cells_early(
                    p, bb, owns[p], cur_ref, cot_ref, wks[p], sum_c, act_c, pre_c, sum_q)

        loop(0, 4, work)
        rim_positions(p, left, rim_cur, rim_cot, prev_ref, wks[p], masks, rim_sum)

    def late_cells(p, bb):
        cells_late(
            p, bb, shift_ref[p, 0], halos[p], cur_ref, cot_ref, sum_c, act_c, pre_c, gc_ref, acc)

    def late_positions(p, bb):
        positions_late(
            p, bb, shift_ref[p, 1], left, halos[p], pre_halos[p], prev_ref, e_fold, masks,
            sum_q, rim_sum, gp_ref)

    early(0)
    join(1)
    early(1)
    arrive(0)
    loop(0, 2, lambda i: [late_cells(0, 4 * i + k) for k in range(4)])
    stores[0].start()
    arrive(1)
    loop(0, 2, lambda i: [late_cells(1, 4 * i + k) for k in range(4)])

    stores[2].start()

    turned = (pltpu.roll(acc[0], back[0], 1) + pltpu.roll(acc[1], back[1], 1)).T
    for u in range(9):
        ar0[9 * u : 9 * u + 9] = turned[16 * u : 16 * u + 9]
    ar0[81:128] = jnp.zeros((47, 128), F32)

    def share(ref, i):
        return ref.at[pl.ds(pl.multiple_of(i * 16, 16), 16)]

    def first(d):
        peer = (g1 + d) % 8
        return pltpu.make_async_remote_copy(
            src_ref=share(ar0, peer), dst_ref=ar1.at[g1], send_sem=s1.at[peer],
            recv_sem=r1.at[g1], device_id=member(peer, g2), device_id_type=MESH,
        )

    def second(d):
        peer = (g2 + d) % 16
        return pltpu.make_async_remote_copy(
            src_ref=ar2.at[g2], dst_ref=ar2.at[g2], send_sem=s2.at[peer],
            recv_sem=r2.at[g2], device_id=member(g1, peer), device_id_type=MESH,
        )

    def third(d):
        peer = (g1 + d) % 8
        return pltpu.make_async_remote_copy(
            src_ref=ar3.at[g1], dst_ref=ar3.at[g1], send_sem=s3.at[peer],
            recv_sem=r3.at[g1], device_id=member(peer, g2), device_id_type=MESH,
        )

    def got(buffer, sends, receives, source):
        pltpu.make_async_remote_copy(
            src_ref=buffer.at[source], dst_ref=buffer.at[source], send_sem=sends.at[source],
            recv_sem=receives.at[source], device_id=(row, 1 - col), device_id_type=MESH,
        ).wait_recv()

    def some_positions(p, lo, hi):
        loop(lo // 2, hi // 2, lambda i: [late_positions(p, 2 * i + k) for k in range(2)])

    for d in range(1, 8):
        first(d).start()
    some_positions(0, 0, 8)
    stores[1].start()
    ar1[g1] = ar0[pl.ds(pl.multiple_of(g1 * 16, 16), 16)]
    for d in range(1, 8):
        got(ar1, s1, r1, (g1 + d) % 8)
    ar2[g2] = jnp.sum(ar1[...], axis=0)
    for d in range(1, 16):
        second(d).start()
    some_positions(1, 0, 4)
    for d in range(1, 16):
        got(ar2, s2, r2, (g2 + d) % 16)
    ar3[g1] = jnp.sum(ar2[...], axis=0)
    for d in range(1, 8):
        third(d).start()
    some_positions(1, 4, 8)
    stores[3].start()
    for d in range(1, 8):
        got(ar3, s3, r3, (g1 + d) % 8)
    gw_ref[...] = ar3[...].reshape(128, 128)[:81] * norm
    for d in range(1, 8):
        first(d).wait_send()
        third(d).wait_send()
    for d in range(1, 16):
        second(d).wait_send()
    for copy in stores:
        copy.wait()

    for p in range(2):
        for k in range(3):

            @pl.when(row > 0)
            def _():
                along(p, 0, k).wait_send()

            @pl.when(row < last)
            def _():
                along(p, 1, k).wait_send()


def spread_matrix():
    e = np.zeros((128, 256), np.float32)
    for u in range(9):
        for v in range(9):
            e[9 * u + v, 16 * u + v] = 1.0 / 32.0
    return e


def local(current, previous, shift, weight, cotangent):
    pairs, channels, rows, cols = current.shape
    e = jnp.asarray(spread_matrix(), BF)
    eye = jnp.asarray(np.eye(81, 128), BF)
    total = pairs * rows * lax.axis_size("row") * cols * lax.axis_size("col")
    vmem = pl.BlockSpec(memory_space=pltpu.VMEM)
    hbm = pl.BlockSpec(memory_space=pl.ANY)
    dma = pltpu.SemaphoreType.DMA
    v = pltpu.VMEM
    gc, gp, gw = pl.pallas_call(
        functools.partial(kernel, 1.0 / math.sqrt(total)),
        in_specs=[pl.BlockSpec(memory_space=pltpu.SMEM)] + [hbm] * 3 + [vmem] * 3,
        out_specs=[hbm, hbm, vmem],
        out_shape=[
            jax.ShapeDtypeStruct((2, 8, 128, 256), BF),
            jax.ShapeDtypeStruct((2, 8, 128, 256), BF),
            jax.ShapeDtypeStruct((81, 128), F32),
        ],
        scratch_shapes=[
            v((2, 256, 8, 128), BF), v((2, 256, 8, 128), BF), v((2, 128, 8, 128), BF),
            v((2, 8, 128, 256), BF), v((2, 8, 128, 256), BF),
            v((2, 8, 128, 256), BF), v((2, 8, 128, 256), BF), v((2, 8, 128, 128), BF),
            v((2048, 128), F32), v((2048, 128), F32),
            v((2, 2, 256, 8, 128), BF), v((2, 2, 4, 16, 256), BF), v((2, 2, 4, 16, 256), BF),
            v((2, 8, 16, 256), BF), v((8, 16, 256), BF), v((8, 16, 256), BF),
            v((2, 4, 16, 128), BF), v((2, 4, 16, 128), BF),
            v((8, WIDE, 256), BF), v((8, WIDE, 256), BF),
            v((2, 8, WIDE, 128), F32), v((8, WIDE, 128), F32),
            v((2, 8, 8, 256), F32), v((2, 8, 8, 128), F32),
            v((2, 2, 256, 8, 128), BF),
            v((2, 2, 4, WIDE, 128), BF), v((2, 2, 4, WIDE, 128), BF),
            v((16, WIDE, 256), BF), v((16, WIDE, 256), BF),
            v((8, WIDE, 128), BF), v((8, WIDE, 128), BF),
            v((2, 8, 128, 256), F32),
            v((2, 8, 128, 128), F32), v((2, 8, 128, 128), F32),
            v((2, 8, WIDE, 256), F32), v((2, 128, 256), F32),
            v((2, 128, 256), F32),
            v((128, 128), F32), v((8, 16, 128), F32), v((16, 16, 128), F32), v((8, 16, 128), F32),
            dma((2, 2)), dma((2, 2)), dma((2, 2, 3)), dma((2, 2, 3)),
            dma((8,)), dma((8,)), dma((16,)), dma((16,)), dma((8,)), dma((8,)),
            dma((6,)), dma((4,)),
        ],
        compiler_params=pltpu.CompilerParams(
            collective_id=0, has_side_effects=True, vmem_limit_bytes=56 << 20
        ),
        cost_estimate=pl.CostEstimate(
            flops=3_000_000_000, bytes_accessed=8 << 20, transcendentals=1_500_000
        ),
    )(shift, previous, current, cotangent, weight.T, e, eye)
    return gc.transpose(0, 3, 1, 2), gp.transpose(0, 3, 1, 2), gw.T


def solution(mesh):
    grid = P(None, None, "row", "col")
    return jax.shard_map(
        local,
        mesh=mesh,
        in_specs=(grid, grid, P(), P(), grid),
        out_specs=(grid, grid, P()),
        check_vma=False,
    )
```

```python
import functools
import math

import jax
import jax.numpy as jnp
import numpy as np
from jax import lax
from jax.experimental import pallas as pl
from jax.experimental.pallas import tpu as pltpu
from jax.sharding import PartitionSpec as P

BF = jnp.bfloat16
F32 = jnp.float32
MESH = pl.DeviceIdType.MESH
NT = (((1,), (1,)), ((), ()))
TN = (((0,), (0,)), ((), ()))
NN = (((1,), (0,)), ((), ()))
WIDE = 144


def dot(a, b, dims=NN):
    return lax.dot_general(a, b, dims, preferred_element_type=F32)


def iota(shape, axis):
    return lax.broadcasted_iota(jnp.int32, shape, axis)


def skew(x, shift):
    return pltpu.roll(x, shift % 256, 1, stride=1, stride_axis=0)


def flip8(x):
    idx = 7 - iota((8, 128), 0)
    parts = [
        jnp.take_along_axis(x[:, at : at + 128], idx, axis=0) for at in range(0, x.shape[1], 128)
    ]
    return parts[0] if len(parts) == 1 else jnp.concatenate(parts, axis=1)


def activation(vol_dot):
    half = vol_dot * (1.0 / 32.0)
    q = 1.0 + jnp.tanh(half)
    act = half * q
    return act, q + act * (2.0 - q)


def cell_block(p, bb, rows_of, both):
    at = pl.multiple_of(bb * 16, 16)
    cur = both[p, 8:16, pl.ds(at, 16), :].reshape(128, 256)
    rows = [rows_of(i, at) for i in range(8)]
    win = jnp.concatenate([r[0:16] for r in rows] + [r[8:24] for r in rows], axis=0)
    return win, dot(cur, win, NT)


def split_grads(grads):
    zero = jnp.zeros((8, 128), F32)
    full = [
        jnp.concatenate([zero, g] if i % 2 else [g, zero], axis=1) for i, g in enumerate(grads)
    ]
    return jnp.concatenate(full, axis=0).astype(BF)


def cells_early(p, bb, own, both, cot_ref, wk, sum_c, act_c, pre_c, sum_q):
    win, vol = cell_block(p, bb, lambda i, at: own[i, pl.ds(at, 32), :], both)
    at = pl.multiple_of(bb * 16, 16)
    pre = dot(cot_ref[p, :, pl.ds(at, 16), :].reshape(128, 128), wk)
    grads, acts, rest = [], [], []
    for i in range(16):
        y, odd = divmod(i, 2)
        rows = slice(8 * i, 8 * i + 8)
        act, slope = activation(vol[rows, 128 * odd : 128 * odd + 128])
        piece = skew(pre[rows], 16 * y)
        grads.append(piece[:, :128] * slope)
        rest.append(piece[:, 128:])
        acts.append(flip8(act))
    act_c[p, bb] = jnp.concatenate(acts, axis=0)
    pre_c[p, bb] = jnp.concatenate(rest, axis=0)
    grad = split_grads(grads)
    sum_c[p, bb] = dot(grad, win)
    cur = both[p, 8:16, pl.ds(at, 16), :].reshape(128, 256)
    back = dot(grad, cur, TN)
    for i in range(8):
        even, odd = back[16 * i : 16 * i + 16], back[128 + 16 * i : 128 + 16 * i + 16]
        sum_q[p, i, pl.ds(at, 8), :] += even[:8]
        sum_q[p, i, pl.ds(at + 8, 8), :] = even[8:] + odd[:8]
        sum_q[p, i, pl.ds(at + 16, 8), :] = odd[8:]


def cells_late(p, bb, dy, halo, both, cot_ref, sum_c, act_c, pre_c, out_ref, acc_ref):
    def rows_of(i, at):
        return halo[i, pl.ds(at, 32), :]

    win, vol = cell_block(p, bb, rows_of, both)
    at = pl.multiple_of(bb * 16, 16)
    cot = cot_ref[p, :, pl.ds(at, 16), :].reshape(128, 128).astype(F32)
    cot_rev = jnp.concatenate([flip8(cot[8 * i : 8 * i + 8]) for i in range(16)], axis=0)
    act_own, pre = act_c[p, bb], pre_c[p, bb]
    grads, acts = [], []
    for i in range(16):
        y, odd = divmod(i, 2)
        rows = slice(8 * i, 8 * i + 8)
        act, slope = activation(vol[rows, 128 * odd : 128 * odd + 128])
        grads.append(pre[rows] * slope)
        act = jnp.concatenate([act_own[rows], flip8(act)], axis=1)
        acts.append(skew(act, 249 - 16 * y))
    act = jnp.concatenate(acts, axis=0).astype(BF)
    acc_ref[p] += dot(cot_rev.astype(BF), act, TN)
    out = sum_c[p, bb] + dot(split_grads(grads), win)
    out_ref[p, :, pl.ds(at, 16), :] = out.astype(BF).reshape(8, 16, 256)


def rim_positions(p, left, rim_cur, rim_cot, both, wk, masks, rim_sum):
    at = pl.multiple_of(jnp.where(left, 112, 0), 16)
    prev = both[p, 0:8, pl.ds(at, 16), :].reshape(128, 256)
    win = rim_cur[p].reshape(64, 256).astype(BF)
    vol = dot(win, prev, NT)
    pre = dot(rim_cot[p].reshape(64, 128).astype(BF), wk)
    mask = jnp.where(left, masks[1], masks[0])
    grads = []
    for i in range(8):
        rows = slice(8 * i, 8 * i + 8)
        piece = pre[rows] * mask
        piece = jnp.where(left, skew(piece, 16 * i + 8), skew(piece, 16 * i - 8))[:, :128]
        grads.append(piece * activation(vol[rows])[1])
    rim_sum[p] = dot(jnp.concatenate(grads, axis=0).astype(BF), win, TN)


def positions_late(
    p, bb, dx, left, halo, pre_halo, both, e_fold, masks, sum_q, rim_sum, out_ref
):
    at = pl.multiple_of(bb * 16, 16)
    prev = both[p, 0:8, pl.ds(at, 16), :].reshape(128, 256)
    win = jnp.concatenate([halo[8 + i, pl.ds(at, 32), :][:24] for i in range(8)], axis=0)
    vol = dot(win, prev, NT)
    pre = dot(
        jnp.concatenate([pre_halo[i, pl.ds(at, 32), :][:24] for i in range(8)], axis=0), e_fold
    )
    grads = []
    for i in range(8):
        for g in range(3):
            rows = slice(24 * i + 8 * g, 24 * i + 8 * g + 8)
            piece = pre[rows]
            if g != 1:
                piece = piece * masks[g // 2][:, :128]
            shift = (16 * i + 8 * (g - 1)) % 128
            piece = pltpu.roll(piece, shift, 1, stride=1, stride_axis=0)
            grads.append(piece * activation(vol[rows])[1])
    out = dot(jnp.concatenate(grads, axis=0).astype(BF), win, TN)
    own = pltpu.roll(sum_q[p, :, pl.ds(at, 24), :], (20 + dx) % 24, 1)[:, :16].reshape(128, 256)
    rim = jnp.where(bb == jnp.where(left, 7, 0), 1.0, 0.0) * rim_sum[p]
    out_ref[p, :, pl.ds(at, 16), :] = (out + own + rim).astype(BF).reshape(8, 16, 256)


def kernel(
    norm, shift_ref, prev_hbm, cur_hbm, cot_hbm, w_ref, e_ref, eye_ref,
    gc_hbm, gp_hbm, gw_ref,
    both, cot_ref, gc_ref, gp_ref, msg_r0, msg_r1, rim_s, rim_r,
    edge_s, edge_r0, edge_r1, edge_cot_s, edge_cot_r, own0, own1, own_pre, rim_cur, rim_cot,
    msg, tri_s, tri_r, halo0, halo1, pre_halo0, pre_halo1,
    sum_c, act_c, pre_c, sum_q, rim_sum, acc, ar0, ar1, ar2, ar3, ar4,
    side_ss, side_rs, row_ss, row_rs, s1, r1, s2, r2, s3, r3, s4, r4, load_sem, store_sem,
):
    row, col = lax.axis_index("row"), lax.axis_index("col")
    last = lax.axis_size("row") - 1
    left = col == 0
    owns = (own0, own1)
    halos, pre_halos = (halo0, halo1), (pre_halo0, pre_halo1)
    g1, g2, g3 = (row % 4) * 2 + col, (row // 4) % 4, row // 16

    def member(a, b, c):
        return ((c * 4 + b) * 4 + a // 2, a % 2)

    loads, stores = [], []
    for p in range(2):
        for source, target in (
            (prev_hbm, both.at[p, 0:8]), (cur_hbm, both.at[p, 8:16]), (cot_hbm, cot_ref.at[p])
        ):
            at = load_sem.at[len(loads)]
            loads.append(pltpu.make_async_copy(source.at[p], target, at))
        for source, target in ((gc_ref, gc_hbm), (gp_ref, gp_hbm)):
            at = store_sem.at[len(stores)]
            stores.append(pltpu.make_async_copy(source.at[p], target.at[p], at))
    for copy in loads:
        copy.start()

    barrier = pltpu.get_barrier_semaphore()

    def greet(target):
        pl.semaphore_signal(barrier, inc=1, device_id=target, device_id_type=MESH)

    for d in range(1, 8):
        greet(member((g1 + d) % 8, g2, g3))
    for d in range(1, 4):
        greet(member(g1, (g2 + d) % 4, g3))
        greet(member(g1, g2, (g3 + d) % 4))
    greet(((row + 1) % (last + 1), col))
    greet(((row + last) % (last + 1), col))

    def side(p, k):
        src, dst = (
            (edge_s.at[p], (edge_r0, edge_r1)[p]), (edge_cot_s.at[p], edge_cot_r.at[p])
        )[k]
        return pltpu.make_async_remote_copy(
            src_ref=src, dst_ref=dst, send_sem=side_ss.at[p, k],
            recv_sem=side_rs.at[p, k], device_id=(row, 1 - col), device_id_type=MESH,
        )

    def along(p, way, k):
        src, dst = (
            (msg.at[p, way], (msg_r0, msg_r1)[p].at[way]), (rim_s.at[p, way], rim_r.at[p, way]),
            (tri_s.at[p, way], tri_r.at[p, way]),
        )[k]
        target = jnp.where(row == last, row, row + 1) if way else jnp.where(row == 0, row, row - 1)
        return pltpu.make_async_remote_copy(
            src_ref=src, dst_ref=dst, send_sem=row_ss.at[p, way, k],
            recv_sem=row_rs.at[p, way, k], device_id=(target, col), device_id_type=MESH,
        )

    def pack(p):
        dy = shift_ref[p, 0]

        def copy(s, carry):
            msg[p, 0, s] = both[p, jnp.where(s < 4 + dy, s, 4 + s - dy)]
            msg[p, 1, s] = both[p, jnp.where(s < 4 + dy, 12 + s - dy, s)]
            return carry

        lax.fori_loop(0, 8, copy, 0)

    def send(p, k):
        @pl.when(row > 0)
        def _():
            along(p, 0, k).start()

        @pl.when(row < last)
        def _():
            along(p, 1, k).start()

    def aligner(offset):
        take = iota((WIDE, 128), 1) + 8 == iota((WIDE, 128), 0) + offset
        return jnp.where(take, 1.0, 0.0).astype(BF)

    def rim_place(tile, offset):
        tile = pltpu.roll(tile, offset % 8, tile.ndim - 2)
        at = iota(tile.shape, tile.ndim - 2)
        keep = jnp.where(left, at, -1 - at) >= jnp.where(left, offset, -offset)
        return jnp.where(keep, tile, 0.0)

    def rim_add(x, rim):
        zero = jnp.zeros_like(rim)
        low, high = jnp.where(left, zero, rim), jnp.where(left, rim, zero)
        return jnp.concatenate([x[:8] + low, x[8:128], x[128:136] + high, x[136:]], axis=0)

    start = jnp.where(left, 112, 0)

    def edges(p):
        for y in range(8):
            pick = []
            for ref_row in (y, 8 + y):
                tile = both[p, ref_row, pl.ds(pl.multiple_of(start, 16), 16), :].astype(F32)
                pick.append(jnp.where(left, tile[8:], tile[:8]))
            edge_s[p, y] = jnp.concatenate(pick, axis=0).astype(BF)
        for y in range(0, 8, 2):
            pick = []
            for yy in (y, y + 1):
                tile = cot_ref[p, yy, pl.ds(pl.multiple_of(start, 16), 16), :].astype(F32)
                pick.append(jnp.where(left, tile[8:], tile[:8]))
            edge_cot_s[p, y // 2] = jnp.concatenate(pick, axis=0).astype(BF)

    for copy in loads:
        copy.wait()
    edges(0)
    pack(0)
    pl.semaphore_wait(barrier, 15)
    for k in range(2):
        side(0, k).start()
    send(0, 0)
    edges(1)
    for k in range(2):
        side(1, k).start()
    pack(1)

    w81 = w_ref[...]
    e = e_ref[...]
    w9 = dot(w81, eye_ref[...], TN).astype(BF)
    wk = dot(w9, e)
    e_fold = (e[:, :128].astype(F32) + e[:, 128:].astype(F32)).astype(BF)
    turns = [(16 * (shift_ref[p, 0] + 12)) % 256 for p in range(2)]
    back = [(16 * (4 - shift_ref[p, 0])) % 256 for p in range(2)]
    wks = [pltpu.roll(wk, turns[p], 1).astype(BF) for p in range(2)]
    sub, lane = iota((8, 256), 0), iota((8, 256), 1) % 16
    masks = (jnp.where(lane >= 8 - sub, 1.0, 0.0), jnp.where(lane < 8 - sub, 1.0, 0.0))
    tri_lane = iota((WIDE, 128), 1)
    acc[...] = jnp.zeros_like(acc)
    sum_q[:, :, 0:8] = jnp.zeros((2, 8, 8, 256), F32)

    def join(p):
        dy, dx = shift_ref[p, 0], shift_ref[p, 1]
        own, edge_r = owns[p], (edge_r0, edge_r1)[p]
        take_p, take_c = aligner(4 + dx), aligner(4 - dx)
        for k in range(2):
            side(p, k).wait()
        for y in range(8):
            edge = edge_r[y].astype(F32)
            own[y] = rim_add(dot(take_p, both[p, y]), rim_place(edge[:8], 4 - dx)).astype(BF)
            rim_cur[p, y] = rim_place(edge[8:], 4 + dx)
            at = 8 * (y % 2)
            rim = rim_place(edge_cot_r[p, y // 2].astype(F32)[at : at + 8], 4 + dx)
            rim_cot[p, y] = rim
            own_pre[y] = dot(rim_add(dot(take_c, cot_ref[p, y]), rim).astype(BF), w9)

        def tile(s, up):
            is_prev = (s < 4 + dy) if up else (s >= 4 + dy)
            at = jnp.where(is_prev, s, jnp.where(s < 4 + dy, s + 4 - dy, s - 4 - dy))
            both = edge_r[at].astype(F32)
            return jnp.where(is_prev, both[:8], both[8:])

        for k in range(4):
            for way in range(2):
                pair = [tile(2 * k, way == 0), tile(2 * k + 1, way == 0)]
                rim_s[p, way, k] = jnp.concatenate(pair, axis=0).astype(BF)

        def cell_row(t):
            return own_pre[jnp.where(t < 4 + dy, t + 4 - dy, t - 4 - dy)]

        for s in range(4):
            near, away = cell_row(s), cell_row(7 - s)
            tri_s[p, 1, s] = jnp.where(
                tri_lane >= 9 * (8 - s), near, pltpu.roll(away, 128 - 9 * (s + 1), 1)
            ).astype(BF)
            tri_s[p, 0, s] = jnp.where(
                tri_lane < 9 * (8 - s), near, pltpu.roll(away, 9 * (8 - s), 1)
            ).astype(BF)
        send(p, 1)
        send(p, 2)

    join(0)
    send(1, 0)
    join(1)

    def arrive(p):
        dy, dx = shift_ref[p, 0], shift_ref[p, 1]
        halo = halos[p]
        take_p, take_c = aligner(4 + dx), aligner(4 - dx)

        def receive(k, buffer):
            for way, edge_row in ((1, 0), (0, last)):

                @pl.when(row != edge_row)
                def _():
                    along(p, way, k).wait_recv()

                @pl.when(row == edge_row)
                def _():
                    part = buffer[way]
                    part[...] = jnp.zeros(part.shape, BF)

        msg_r = (msg_r0, msg_r1)[p]
        receive(0, msg_r.at)
        receive(1, rim_r.at[p].at)
        receive(2, tri_r.at[p].at)
        for s in range(8):
            at = 8 * (s % 2)
            up = rim_r[p, 0, s // 2].astype(F32)[at : at + 8]
            down = rim_r[p, 1, s // 2].astype(F32)[at : at + 8]
            low = s < 4 + dy
            x = dot(take_p, msg_r[jnp.where(low, 0, 1), s])
            rim = rim_place(jnp.where(low, up, down), 4 - dx)
            halo[s] = rim_add(x, rim).astype(BF)
            x = dot(take_c, msg_r[jnp.where(low, 1, 0), s])
            rim = rim_place(jnp.where(low, down, up), 4 + dx)
            halo[8 + s] = rim_add(x, rim).astype(BF)
        for s in range(4):
            up, down = tri_r[p, 0, s].astype(F32), tri_r[p, 1, s].astype(F32)
            near = tri_lane >= 9 * (8 - s)
            x = jnp.where(near == (s < 4 + dy), jnp.where(s < 4 + dy, down, up), 0.0)
            pre_halos[p][s] = x.astype(BF)
            down = pltpu.roll(down, 9 * (s + 1), 1)
            up = pltpu.roll(up, 128 - 9 * (8 - s), 1)
            near = tri_lane >= 9 * (s + 1)
            x = jnp.where(near == (7 - s < 4 + dy), jnp.where(7 - s < 4 + dy, down, up), 0.0)
            pre_halos[p][7 - s] = jnp.where(tri_lane < 81, x, 0.0).astype(BF)

    def loop(lo, hi, work):
        def body(bb, carry):
            work(bb)
            return carry

        lax.fori_loop(lo, hi, body, 0)

    def early(p):
        def work(i):
            for bb in (2 * i, 2 * i + 1):
                cells_early(
                    p, bb, owns[p], both, cot_ref, wks[p], sum_c, act_c, pre_c, sum_q)

        loop(0, 4, work)
        rim_positions(p, left, rim_cur, rim_cot, both, wks[p], masks, rim_sum)

    def late_cells(p, bb):
        cells_late(
            p, bb, shift_ref[p, 0], halos[p], both, cot_ref, sum_c, act_c, pre_c, gc_ref, acc)

    def late_positions(p, bb):
        positions_late(
            p, bb, shift_ref[p, 1], left, halos[p], pre_halos[p], both, e_fold, masks,
            sum_q, rim_sum, gp_ref)

    def late(i):
        for bb in (2 * i, 2 * i + 1):
            late_cells(0, bb)
            late_positions(0, bb)

    early(0)
    early(1)
    arrive(0)
    loop(0, 4, late)
    stores[0].start()
    stores[1].start()
    arrive(1)
    loop(0, 2, lambda i: [late_cells(1, 4 * i + k) for k in range(4)])

    stores[2].start()

    turned = (pltpu.roll(acc[0], back[0], 1) + pltpu.roll(acc[1], back[1], 1)).T
    for u in range(9):
        ar0[9 * u : 9 * u + 9] = turned[16 * u : 16 * u + 9]
    ar0[81:128] = jnp.zeros((47, 128), F32)

    def share(ref, i):
        return ref.at[pl.ds(pl.multiple_of(i * 16, 16), 16)]

    def first(d):
        peer = (g1 + d) % 8
        return pltpu.make_async_remote_copy(
            src_ref=share(ar0, peer), dst_ref=ar1.at[g1], send_sem=s1.at[peer],
            recv_sem=r1.at[g1], device_id=member(peer, g2, g3), device_id_type=MESH,
        )

    def second(d):
        peer = (g2 + d) % 4
        return pltpu.make_async_remote_copy(
            src_ref=ar2.at[g2], dst_ref=ar2.at[g2], send_sem=s2.at[peer],
            recv_sem=r2.at[g2], device_id=member(g1, peer, g3), device_id_type=MESH,
        )

    def third(d):
        peer = (g3 + d) % 4
        return pltpu.make_async_remote_copy(
            src_ref=ar3.at[g3], dst_ref=ar3.at[g3], send_sem=s3.at[peer],
            recv_sem=r3.at[g3], device_id=member(g1, g2, peer), device_id_type=MESH,
        )

    def fourth(d):
        peer = (g1 + d) % 8
        return pltpu.make_async_remote_copy(
            src_ref=ar4.at[g1], dst_ref=ar4.at[g1], send_sem=s4.at[peer],
            recv_sem=r4.at[g1], device_id=member(peer, g2, g3), device_id_type=MESH,
        )

    def got(buffer, sends, receives, source):
        pltpu.make_async_remote_copy(
            src_ref=buffer.at[source], dst_ref=buffer.at[source], send_sem=sends.at[source],
            recv_sem=receives.at[source], device_id=(row, 1 - col), device_id_type=MESH,
        ).wait_recv()

    def some_positions(lo, hi):
        loop(0, 1, lambda i: [late_positions(1, k) for k in range(lo, hi)])

    for d in range(1, 8):
        first(d).start()
    some_positions(0, 2)
    ar1[g1] = ar0[pl.ds(pl.multiple_of(g1 * 16, 16), 16)]
    for d in range(1, 8):
        first(d).wait_send()
        got(ar1, s1, r1, (g1 + d) % 8)
    ar2[g2] = jnp.sum(ar1[...], axis=0)
    for d in range(1, 4):
        second(d).start()
    some_positions(2, 4)
    for d in range(1, 4):
        second(d).wait_send()
        got(ar2, s2, r2, (g2 + d) % 4)
    ar3[g3] = jnp.sum(ar2[...], axis=0)
    for d in range(1, 4):
        third(d).start()
    some_positions(4, 6)
    for d in range(1, 4):
        third(d).wait_send()
        got(ar3, s3, r3, (g3 + d) % 4)
    ar4[g1] = jnp.sum(ar3[...], axis=0)
    for d in range(1, 8):
        fourth(d).start()
    some_positions(6, 8)
    stores[3].start()
    for d in range(1, 8):
        fourth(d).wait_send()
        got(ar4, s4, r4, (g1 + d) % 8)
    gw_ref[...] = ar4[...].reshape(128, 128)[:81] * norm
    for copy in stores:
        copy.wait()

    for p in range(2):
        for k in range(3):

            @pl.when(row > 0)
            def _():
                along(p, 0, k).wait_send()

            @pl.when(row < last)
            def _():
                along(p, 1, k).wait_send()


def spread_matrix():
    e = np.zeros((128, 256), np.float32)
    for u in range(9):
        for v in range(9):
            e[9 * u + v, 16 * u + v] = 1.0 / 32.0
    return e


def local(current, previous, shift, weight, cotangent):
    pairs, channels, rows, cols = current.shape
    prev = previous.transpose(0, 2, 3, 1)
    cur = current.transpose(0, 2, 3, 1)
    cot = cotangent.transpose(0, 2, 3, 1)
    e = jnp.asarray(spread_matrix(), BF)
    eye = jnp.asarray(np.eye(81, 128), BF)
    total = pairs * rows * lax.axis_size("row") * cols * lax.axis_size("col")
    vmem = pl.BlockSpec(memory_space=pltpu.VMEM)
    hbm = pl.BlockSpec(memory_space=pl.ANY)
    dma = pltpu.SemaphoreType.DMA
    v = pltpu.VMEM
    gc, gp, gw = pl.pallas_call(
        functools.partial(kernel, 1.0 / math.sqrt(total)),
        in_specs=[pl.BlockSpec(memory_space=pltpu.SMEM)] + [hbm] * 3 + [vmem] * 3,
        out_specs=[hbm, hbm, vmem],
        out_shape=[
            jax.ShapeDtypeStruct((2, 8, 128, 256), BF),
            jax.ShapeDtypeStruct((2, 8, 128, 256), BF),
            jax.ShapeDtypeStruct((81, 128), F32),
        ],
        scratch_shapes=[
            v((2, 16, 128, 256), BF), v((2, 8, 128, 128), BF),
            v((2, 8, 128, 256), BF), v((2, 8, 128, 256), BF),
            v((2, 8, 128, 256), BF), v((2, 8, 128, 256), BF),
            v((2, 2, 4, 16, 256), BF), v((2, 2, 4, 16, 256), BF),
            v((2, 8, 16, 256), BF), v((8, 16, 256), BF), v((8, 16, 256), BF),
            v((2, 4, 16, 128), BF), v((2, 4, 16, 128), BF),
            v((8, WIDE, 256), BF), v((8, WIDE, 256), BF),
            v((8, WIDE, 128), F32),
            v((2, 8, 8, 256), F32), v((2, 8, 8, 128), F32),
            v((2, 2, 8, 128, 256), BF),
            v((2, 2, 4, WIDE, 128), BF), v((2, 2, 4, WIDE, 128), BF),
            v((16, WIDE, 256), BF), v((16, WIDE, 256), BF),
            v((8, WIDE, 128), BF), v((8, WIDE, 128), BF),
            v((2, 8, 128, 256), F32),
            v((2, 8, 128, 128), F32), v((2, 8, 128, 128), F32),
            v((2, 8, WIDE, 256), F32), v((2, 128, 256), F32),
            v((2, 128, 256), F32),
            v((128, 128), F32), v((8, 16, 128), F32), v((4, 16, 128), F32), v((4, 16, 128), F32),
            v((8, 16, 128), F32),
            dma((2, 2)), dma((2, 2)), dma((2, 2, 3)), dma((2, 2, 3)),
            dma((8,)), dma((8,)), dma((4,)), dma((4,)), dma((4,)), dma((4,)), dma((8,)), dma((8,)),
            dma((6,)), dma((4,)),
        ],
        compiler_params=pltpu.CompilerParams(
            collective_id=0, has_side_effects=True, vmem_limit_bytes=56 << 20
        ),
        cost_estimate=pl.CostEstimate(
            flops=3_000_000_000, bytes_accessed=8 << 20, transcendentals=1_500_000
        ),
    )(shift, prev, cur, cot, weight.T, e, eye)
    return gc.transpose(0, 3, 1, 2), gp.transpose(0, 3, 1, 2), gw.T


def solution(mesh):
    grid = P(None, None, "row", "col")
    return jax.shard_map(
        local,
        mesh=mesh,
        in_specs=(grid, grid, P(), P(), grid),
        out_specs=(grid, grid, P()),
        check_vma=False,
    )
```

```python
import functools
import math

import jax
import jax.numpy as jnp
import numpy as np
from jax import lax
from jax.experimental import pallas as pl
from jax.experimental.pallas import tpu as pltpu
from jax.sharding import PartitionSpec as P

BF = jnp.bfloat16
F32 = jnp.float32
MESH = pl.DeviceIdType.MESH
NT = (((1,), (1,)), ((), ()))
TN = (((0,), (0,)), ((), ()))
NN = (((1,), (0,)), ((), ()))
WIDE = 144


def dot(a, b, dims=NN):
    return lax.dot_general(a, b, dims, preferred_element_type=F32)


def iota(shape, axis):
    return lax.broadcasted_iota(jnp.int32, shape, axis)


def skew(x, shift):
    return pltpu.roll(x, shift % 256, 1, stride=1, stride_axis=0)


def activation(vol_dot):
    half = vol_dot * (1.0 / 32.0)
    q = 1.0 + jnp.tanh(half)
    act = half * q
    return act, q + act * (2.0 - q)


def cell_block(p, bb, rows_of, cur_ref, rev_ref):
    at = pl.multiple_of(bb * 16, 16)
    cur = cur_ref[p, :, pl.ds(at, 16), :].reshape(128, 256)
    rows = [rows_of(i, at) for i in range(8)]
    win = jnp.concatenate([r[0:16] for r in rows] + [r[8:24] for r in rows], axis=0)
    rev = rev_ref[p, :, pl.ds(at, 16), :].reshape(128, 256)
    return win, dot(jnp.concatenate([cur, rev], axis=0), win, NT)


def split_grads(grads):
    zero = jnp.zeros((8, 128), F32)
    full = [
        jnp.concatenate([zero, g] if i % 2 else [g, zero], axis=1) for i, g in enumerate(grads)
    ]
    return jnp.concatenate(full, axis=0).astype(BF)


def cells_early(p, bb, own, cur_ref, rev_ref, cot_ref, wk, sum_c, act_c, pre_c, sum_q):
    win, vol = cell_block(p, bb, lambda i, at: own[i, pl.ds(at, 32), :], cur_ref, rev_ref)
    at = pl.multiple_of(bb * 16, 16)
    pre = dot(cot_ref[p, :, pl.ds(at, 16), :].reshape(128, 128), wk)
    grads, acts, rest = [], [], []
    for i in range(16):
        y, odd = divmod(i, 2)
        rows = slice(8 * i, 8 * i + 8)
        lanes = slice(128 * odd, 128 * odd + 128)
        slope = activation(vol[rows, lanes])[1]
        piece = skew(pre[rows], 16 * y)
        grads.append(piece[:, :128] * slope)
        rest.append(piece[:, 128:])
        acts.append(activation(vol[128 + 8 * i : 136 + 8 * i, lanes])[0])
    act_c[p, bb] = jnp.concatenate(acts, axis=0)
    pre_c[p, bb] = jnp.concatenate(rest, axis=0)
    grad = split_grads(grads)
    sum_c[p, bb] = dot(grad, win)
    cur = cur_ref[p, :, pl.ds(at, 16), :].reshape(128, 256)
    back = dot(grad, cur, TN)
    for i in range(8):
        even, odd = back[16 * i : 16 * i + 16], back[128 + 16 * i : 128 + 16 * i + 16]
        sum_q[p, i, pl.ds(at, 8), :] += even[:8]
        sum_q[p, i, pl.ds(at + 8, 8), :] = even[8:] + odd[:8]
        sum_q[p, i, pl.ds(at + 16, 8), :] = odd[8:]


def cells_late(p, bb, dy, halo, cur_ref, rev_ref, cot_rev_ref, sum_c, act_c, pre_c, out_ref, acc_ref):
    def rows_of(i, at):
        return halo[i, pl.ds(at, 32), :]

    win, vol = cell_block(p, bb, rows_of, cur_ref, rev_ref)
    at = pl.multiple_of(bb * 16, 16)
    cot_rev = cot_rev_ref[p, :, pl.ds(at, 16), :].reshape(128, 128)
    act_own, pre = act_c[p, bb], pre_c[p, bb]
    grads, acts = [], []
    for i in range(16):
        y, odd = divmod(i, 2)
        rows = slice(8 * i, 8 * i + 8)
        lanes = slice(128 * odd, 128 * odd + 128)
        grads.append(pre[rows] * activation(vol[rows, lanes])[1])
        act = activation(vol[128 + 8 * i : 136 + 8 * i, lanes])[0]
        act = jnp.concatenate([act_own[rows], act], axis=1)
        acts.append(skew(act, 249 - 16 * y))
    act = jnp.concatenate(acts, axis=0).astype(BF)
    acc_ref[p] += dot(cot_rev, act, TN)
    out = sum_c[p, bb] + dot(split_grads(grads), win)
    out_ref[p, :, pl.ds(at, 16), :] = out.astype(BF).reshape(8, 16, 256)


def rim_positions(p, left, rim_cur, rim_cot, prev_ref, wk, masks, rim_sum):
    at = pl.multiple_of(jnp.where(left, 112, 0), 16)
    prev = prev_ref[p, :, pl.ds(at, 16), :].reshape(128, 256)
    win = rim_cur[p].reshape(64, 256).astype(BF)
    vol = dot(win, prev, NT)
    pre = dot(rim_cot[p].reshape(64, 128).astype(BF), wk)
    mask = jnp.where(left, masks[1], masks[0])
    grads = []
    for i in range(8):
        rows = slice(8 * i, 8 * i + 8)
        piece = pre[rows] * mask
        piece = jnp.where(left, skew(piece, 16 * i + 8), skew(piece, 16 * i - 8))[:, :128]
        grads.append(piece * activation(vol[rows])[1])
    rim_sum[p] = dot(jnp.concatenate(grads, axis=0).astype(BF), win, TN)


def positions_late(
    p, bb, dx, left, halo, pre_halo, prev_ref, e_fold, masks, sum_q, rim_sum, out_ref
):
    at = pl.multiple_of(bb * 16, 16)
    prev = prev_ref[p, :, pl.ds(at, 16), :].reshape(128, 256)
    win = jnp.concatenate([halo[8 + i, pl.ds(at, 32), :][:24] for i in range(8)], axis=0)
    vol = dot(win, prev, NT)
    pre = dot(
        jnp.concatenate([pre_halo[i, pl.ds(at, 32), :][:24] for i in range(8)], axis=0), e_fold
    )
    grads = []
    for i in range(8):
        for g in range(3):
            rows = slice(24 * i + 8 * g, 24 * i + 8 * g + 8)
            piece = pre[rows]
            if g != 1:
                piece = piece * masks[g // 2][:, :128]
            shift = (16 * i + 8 * (g - 1)) % 128
            piece = pltpu.roll(piece, shift, 1, stride=1, stride_axis=0)
            grads.append(piece * activation(vol[rows])[1])
    out = dot(jnp.concatenate(grads, axis=0).astype(BF), win, TN)
    own = pltpu.roll(sum_q[p, :, pl.ds(at, 24), :], (20 + dx) % 24, 1)[:, :16].reshape(128, 256)
    rim = jnp.where(bb == jnp.where(left, 7, 0), 1.0, 0.0) * rim_sum[p]
    out_ref[p, :, pl.ds(at, 16), :] = (out + own + rim).astype(BF).reshape(8, 16, 256)


def kernel(
    norm, shift_ref, prev_hbm, cur_hbm, cot_hbm, w_ref, e_ref, eye_ref,
    gc_hbm, gp_hbm, gw_ref,
    prev_in, cur_in, cot_in, gc_ref, gp_ref,
    prev_ref, cur_ref, cot_ref, rev_ref, cot_rev, flat0, flat1, msg_r, rim_s, rim_r,
    edge_s, edge_r0, edge_r1, edge_cot_s, edge_cot_r, own0, own1, cot_x, own_pre, rim_cur, rim_cot,
    msg, tri_s, tri_r, halo0, halo1, pre_halo0, pre_halo1,
    sum_c, act_c, pre_c, sum_q, rim_sum, acc, ar0, ar1, ar2, ar3, ar4,
    side_ss, side_rs, row_ss, row_rs, s1, r1, s2, r2, s3, r3, s4, r4, load_sem, store_sem,
):
    row, col = lax.axis_index("row"), lax.axis_index("col")
    last = lax.axis_size("row") - 1
    left = col == 0
    owns = (own0, own1)
    halos, pre_halos = (halo0, halo1), (pre_halo0, pre_halo1)
    g1, g2, g3 = (row % 4) * 2 + col, (row // 4) % 4, row // 16

    def member(a, b, c):
        return ((c * 4 + b) * 4 + a // 2, a % 2)

    loads, stores = [], []
    for p in range(2):
        for source, target in ((prev_hbm, prev_in), (cur_hbm, cur_in), (cot_hbm, cot_in)):
            at = load_sem.at[len(loads)]
            loads.append(pltpu.make_async_copy(source.at[p], target.at[p], at))
        for source, target in ((gc_ref, gc_hbm), (gp_ref, gp_hbm)):
            at = store_sem.at[len(stores)]
            stores.append(pltpu.make_async_copy(source.at[p], target.at[p], at))
    for copy in loads:
        copy.start()

    barrier = pltpu.get_barrier_semaphore()

    def greet(target):
        pl.semaphore_signal(barrier, inc=1, device_id=target, device_id_type=MESH)

    for d in range(1, 8):
        greet(member((g1 + d) % 8, g2, g3))
    for d in range(1, 4):
        greet(member(g1, (g2 + d) % 4, g3))
        greet(member(g1, g2, (g3 + d) % 4))
    greet(((row + 1) % (last + 1), col))
    greet(((row + last) % (last + 1), col))

    def side(p, k):
        src, dst = (
            (edge_s.at[p], (edge_r0, edge_r1)[p]), (edge_cot_s.at[p], edge_cot_r.at[p])
        )[k]
        return pltpu.make_async_remote_copy(
            src_ref=src, dst_ref=dst, send_sem=side_ss.at[p, k],
            recv_sem=side_rs.at[p, k], device_id=(row, 1 - col), device_id_type=MESH,
        )

    def along(p, way, k):
        s, r = ((msg, msg_r), (rim_s, rim_r), (tri_s, tri_r))[k]
        src, dst = s.at[p, way], r.at[p, way]
        target = jnp.where(row == last, row, row + 1) if way else jnp.where(row == 0, row, row - 1)
        return pltpu.make_async_remote_copy(
            src_ref=src, dst_ref=dst, send_sem=row_ss.at[p, way, k],
            recv_sem=row_rs.at[p, way, k], device_id=(target, col), device_id_type=MESH,
        )

    def pack(p):
        dy = shift_ref[p, 0]

        def chunk(i, carry):
            at = pl.ds(pl.multiple_of(i * 16, 16), 16)
            pos = prev_in[p, at].astype(F32)
            cell = pltpu.roll(cur_in[p, at].astype(F32), (4 + dy) % 8, 1)
            low = iota((16, 8, 128), 1) < 4 + dy
            msg[p, 0, at] = jnp.where(low, pos, cell).astype(BF)
            msg[p, 1, at] = jnp.where(low, cell, pos).astype(BF)
            return carry

        lax.fori_loop(0, 16, chunk, 0)

    def send(p, k):
        @pl.when(row > 0)
        def _():
            along(p, 0, k).start()

        @pl.when(row < last)
        def _():
            along(p, 1, k).start()

    mirror = iota((128, 128), 0) // 8 * 8 + 7 - iota((128, 128), 0) % 8 == iota((128, 128), 1)
    mirror = jnp.where(mirror, 1.0, 0.0).astype(BF)
    ident = jnp.where(iota((128, 128), 0) == iota((128, 128), 1), 1.0, 0.0).astype(BF)

    def spread_rows(flat, x):
        flat[0 : x.shape[0] * 8] = x.reshape(x.shape[0] * 8, 128)

    def picked(flat, y, channels):
        return flat[pl.ds(y, channels, stride=8), :].astype(BF)

    def aligner(offset):
        take = iota((WIDE, 128), 1) + 8 == iota((WIDE, 128), 0) + offset
        return jnp.where(take, 1.0, 0.0).astype(BF)

    def rim_place(tile, offset):
        tile = pltpu.roll(tile, offset % 8, tile.ndim - 2)
        at = iota(tile.shape, tile.ndim - 2)
        keep = jnp.where(left, at, -1 - at) >= jnp.where(left, offset, -offset)
        return jnp.where(keep, tile, 0.0)

    def rim_add(x, rim):
        zero = jnp.zeros_like(rim)
        low, high = jnp.where(left, zero, rim), jnp.where(left, rim, zero)
        return jnp.concatenate([x[:8] + low, x[8:128], x[128:136] + high, x[136:]], axis=0)

    def turn_prev(p):
        both = jnp.concatenate([ident, aligner(4 + shift_ref[p, 1])], axis=0)
        spread_rows(flat0, prev_in[p].astype(F32))
        for y in range(8):
            x = dot(both, picked(flat0, y, 256), NT).astype(BF)
            prev_ref[p, y] = x[:128]
            owns[p][y] = x[128:]

    def turn_cells(p):
        two = jnp.concatenate([ident, mirror], axis=0)
        three = jnp.concatenate([ident, mirror, aligner(4 - shift_ref[p, 1])], axis=0)
        spread_rows(flat1, cur_in[p].astype(F32))
        for y in range(8):
            x = dot(two, picked(flat1, y, 256), NT).astype(BF)
            cur_ref[p, y] = x[:128]
            rev_ref[p, y] = x[128:]
        spread_rows(flat0, cot_in[p].astype(F32))
        for y in range(8):
            x = dot(three, picked(flat0, y, 128), NT)
            cot_ref[p, y] = x[:128].astype(BF)
            cot_rev[p, y] = x[128:256].astype(BF)
            cot_x[p, y] = x[256:]

    start = jnp.where(left, 112, 0)

    def edges(p):
        for y in range(8):
            pick = []
            for ref in (prev_ref, cur_ref):
                tile = ref[p, y, pl.ds(pl.multiple_of(start, 16), 16), :].astype(F32)
                pick.append(jnp.where(left, tile[8:], tile[:8]))
            edge_s[p, y] = jnp.concatenate(pick, axis=0).astype(BF)
        for y in range(0, 8, 2):
            pick = []
            for yy in (y, y + 1):
                tile = cot_ref[p, yy, pl.ds(pl.multiple_of(start, 16), 16), :].astype(F32)
                pick.append(jnp.where(left, tile[8:], tile[:8]))
            edge_cot_s[p, y // 2] = jnp.concatenate(pick, axis=0).astype(BF)
        for k in range(2):
            side(p, k).start()

    for copy in loads[:2]:
        copy.wait()
    pack(0)
    pl.semaphore_wait(barrier, 15)
    send(0, 0)
    for copy in loads[2:]:
        copy.wait()
    turn_prev(0)
    turn_cells(0)
    edges(0)
    pack(1)
    turn_prev(1)
    turn_cells(1)
    edges(1)

    w81 = w_ref[...]
    e = e_ref[...]
    w9 = dot(w81, eye_ref[...], TN).astype(BF)
    wk = dot(w9, e)
    e_fold = (e[:, :128].astype(F32) + e[:, 128:].astype(F32)).astype(BF)
    turns = [(16 * (shift_ref[p, 0] + 12)) % 256 for p in range(2)]
    back = [(16 * (4 - shift_ref[p, 0])) % 256 for p in range(2)]
    wks = [pltpu.roll(wk, turns[p], 1).astype(BF) for p in range(2)]
    sub, lane = iota((8, 256), 0), iota((8, 256), 1) % 16
    masks = (jnp.where(lane >= 8 - sub, 1.0, 0.0), jnp.where(lane < 8 - sub, 1.0, 0.0))
    tri_lane = iota((WIDE, 128), 1)
    acc[...] = jnp.zeros_like(acc)
    sum_q[:, :, 0:8] = jnp.zeros((2, 8, 8, 256), F32)

    def join(p):
        dy, dx = shift_ref[p, 0], shift_ref[p, 1]
        own, edge_r = owns[p], (edge_r0, edge_r1)[p]
        for k in range(2):
            side(p, k).wait()
        for y in range(8):
            edge = edge_r[y].astype(F32)
            rim = rim_place(edge[:8], 4 - dx)
            zero = jnp.zeros_like(rim)
            for at, piece in ((0, jnp.where(left, zero, rim)), (128, jnp.where(left, rim, zero))):
                tile = own[y, at : at + 16].astype(F32) + jnp.concatenate([piece, zero], axis=0)
                own[y, at : at + 16] = tile.astype(BF)
            rim_cur[p, y] = rim_place(edge[8:], 4 + dx)
            at = 8 * (y % 2)
            rim = rim_place(edge_cot_r[p, y // 2].astype(F32)[at : at + 8], 4 + dx)
            rim_cot[p, y] = rim
            own_pre[y] = dot(rim_add(cot_x[p, y], rim).astype(BF), w9)

        def tile(s, up):
            is_prev = (s < 4 + dy) if up else (s >= 4 + dy)
            at = jnp.where(is_prev, s, jnp.where(s < 4 + dy, s + 4 - dy, s - 4 - dy))
            both = edge_r[at].astype(F32)
            return jnp.where(is_prev, both[:8], both[8:])

        for k in range(4):
            for way in range(2):
                pair = [tile(2 * k, way == 0), tile(2 * k + 1, way == 0)]
                rim_s[p, way, k] = jnp.concatenate(pair, axis=0).astype(BF)

        def cell_row(t):
            return own_pre[jnp.where(t < 4 + dy, t + 4 - dy, t - 4 - dy)]

        for s in range(4):
            near, away = cell_row(s), cell_row(7 - s)
            tri_s[p, 1, s] = jnp.where(
                tri_lane >= 9 * (8 - s), near, pltpu.roll(away, 128 - 9 * (s + 1), 1)
            ).astype(BF)
            tri_s[p, 0, s] = jnp.where(
                tri_lane < 9 * (8 - s), near, pltpu.roll(away, 9 * (8 - s), 1)
            ).astype(BF)
        send(p, 1)
        send(p, 2)

    join(0)
    send(1, 0)
    join(1)

    def arrive(p):
        dy, dx = shift_ref[p, 0], shift_ref[p, 1]
        halo = halos[p]
        take_p, take_c = aligner(4 + dx), aligner(4 - dx)

        def receive(k, buffer):
            for way, edge_row in ((1, 0), (0, last)):

                @pl.when(row != edge_row)
                def _():
                    along(p, way, k).wait_recv()

                @pl.when(row == edge_row)
                def _():
                    part = buffer.at[p, way]
                    part[...] = jnp.zeros(part.shape, BF)

        for k, buffer in enumerate((msg_r, rim_r, tri_r)):
            receive(k, buffer)

        def sort(i, carry):
            at = pl.ds(pl.multiple_of(i * 16, 16), 16)
            to = pl.ds(pl.multiple_of(i * 128, 128), 128)
            up, down = msg_r[p, 0, at].astype(F32), msg_r[p, 1, at].astype(F32)
            low = iota((16, 8, 128), 1) < 4 + dy
            flat0[to] = jnp.where(low, up, down).reshape(128, 128)
            flat1[to] = jnp.where(low, down, up).reshape(128, 128)
            return carry

        lax.fori_loop(0, 16, sort, 0)
        for s in range(8):
            at = 8 * (s % 2)
            up = rim_r[p, 0, s // 2].astype(F32)[at : at + 8]
            down = rim_r[p, 1, s // 2].astype(F32)[at : at + 8]
            low = s < 4 + dy
            x = dot(take_p, picked(flat0, s, 256), NT)
            rim = rim_place(jnp.where(low, up, down), 4 - dx)
            halo[s] = rim_add(x, rim).astype(BF)
            x = dot(take_c, picked(flat1, s, 256), NT)
            rim = rim_place(jnp.where(low, down, up), 4 + dx)
            halo[8 + s] = rim_add(x, rim).astype(BF)
        for s in range(4):
            up, down = tri_r[p, 0, s].astype(F32), tri_r[p, 1, s].astype(F32)
            near = tri_lane >= 9 * (8 - s)
            x = jnp.where(near == (s < 4 + dy), jnp.where(s < 4 + dy, down, up), 0.0)
            pre_halos[p][s] = x.astype(BF)
            down = pltpu.roll(down, 9 * (s + 1), 1)
            up = pltpu.roll(up, 128 - 9 * (8 - s), 1)
            near = tri_lane >= 9 * (s + 1)
            x = jnp.where(near == (7 - s < 4 + dy), jnp.where(7 - s < 4 + dy, down, up), 0.0)
            pre_halos[p][7 - s] = jnp.where(tri_lane < 81, x, 0.0).astype(BF)

    def loop(lo, hi, work):
        def body(bb, carry):
            work(bb)
            return carry

        lax.fori_loop(lo, hi, body, 0)

    def early(p):
        def work(i):
            for bb in (2 * i, 2 * i + 1):
                cells_early(
                    p, bb, owns[p], cur_ref, rev_ref, cot_ref, wks[p], sum_c, act_c, pre_c, sum_q)

        loop(0, 4, work)
        rim_positions(p, left, rim_cur, rim_cot, prev_ref, wks[p], masks, rim_sum)

    def late_cells(p, bb):
        cells_late(
            p, bb, shift_ref[p, 0], halos[p], cur_ref, rev_ref, cot_rev, sum_c, act_c, pre_c,
            gc_ref, acc)

    def late_positions(p, bb):
        positions_late(
            p, bb, shift_ref[p, 1], left, halos[p], pre_halos[p], prev_ref, e_fold, masks,
            sum_q, rim_sum, gp_ref)

    def late(i):
        for bb in (2 * i, 2 * i + 1):
            late_cells(0, bb)
            late_positions(0, bb)

    early(0)
    early(1)
    arrive(0)
    loop(0, 4, late)
    stores[0].start()
    stores[1].start()
    arrive(1)
    loop(0, 2, lambda i: [late_cells(1, 4 * i + k) for k in range(4)])

    stores[2].start()

    turned = (pltpu.roll(acc[0], back[0], 1) + pltpu.roll(acc[1], back[1], 1)).T
    for u in range(9):
        ar0[9 * u : 9 * u + 9] = turned[16 * u : 16 * u + 9]
    ar0[81:128] = jnp.zeros((47, 128), F32)

    def share(ref, i):
        return ref.at[pl.ds(pl.multiple_of(i * 16, 16), 16)]

    def first(d):
        peer = (g1 + d) % 8
        return pltpu.make_async_remote_copy(
            src_ref=share(ar0, peer), dst_ref=ar1.at[g1], send_sem=s1.at[peer],
            recv_sem=r1.at[g1], device_id=member(peer, g2, g3), device_id_type=MESH,
        )

    def second(d):
        peer = (g2 + d) % 4
        return pltpu.make_async_remote_copy(
            src_ref=ar2.at[g2], dst_ref=ar2.at[g2], send_sem=s2.at[peer],
            recv_sem=r2.at[g2], device_id=member(g1, peer, g3), device_id_type=MESH,
        )

    def third(d):
        peer = (g3 + d) % 4
        return pltpu.make_async_remote_copy(
            src_ref=ar3.at[g3], dst_ref=ar3.at[g3], send_sem=s3.at[peer],
            recv_sem=r3.at[g3], device_id=member(g1, g2, peer), device_id_type=MESH,
        )

    def fourth(d):
        peer = (g1 + d) % 8
        return pltpu.make_async_remote_copy(
            src_ref=ar4.at[g1], dst_ref=ar4.at[g1], send_sem=s4.at[peer],
            recv_sem=r4.at[g1], device_id=member(peer, g2, g3), device_id_type=MESH,
        )

    def got(buffer, sends, receives, source):
        pltpu.make_async_remote_copy(
            src_ref=buffer.at[source], dst_ref=buffer.at[source], send_sem=sends.at[source],
            recv_sem=receives.at[source], device_id=(row, 1 - col), device_id_type=MESH,
        ).wait_recv()

    def some_positions(lo, hi):
        loop(0, 1, lambda i: [late_positions(1, k) for k in range(lo, hi)])

    for d in range(1, 8):
        first(d).start()
    some_positions(0, 2)
    ar1[g1] = ar0[pl.ds(pl.multiple_of(g1 * 16, 16), 16)]
    for d in range(1, 8):
        first(d).wait_send()
        got(ar1, s1, r1, (g1 + d) % 8)
    ar2[g2] = jnp.sum(ar1[...], axis=0)
    for d in range(1, 4):
        second(d).start()
    some_positions(2, 4)
    for d in range(1, 4):
        second(d).wait_send()
        got(ar2, s2, r2, (g2 + d) % 4)
    ar3[g3] = jnp.sum(ar2[...], axis=0)
    for d in range(1, 4):
        third(d).start()
    some_positions(4, 6)
    for d in range(1, 4):
        third(d).wait_send()
        got(ar3, s3, r3, (g3 + d) % 4)
    ar4[g1] = jnp.sum(ar3[...], axis=0)
    for d in range(1, 8):
        fourth(d).start()
    some_positions(6, 8)
    stores[3].start()
    for d in range(1, 8):
        fourth(d).wait_send()
        got(ar4, s4, r4, (g1 + d) % 8)
    gw_ref[...] = ar4[...].reshape(128, 128)[:81] * norm
    for copy in stores:
        copy.wait()

    for p in range(2):
        for k in range(3):

            @pl.when(row > 0)
            def _():
                along(p, 0, k).wait_send()

            @pl.when(row < last)
            def _():
                along(p, 1, k).wait_send()


def spread_matrix():
    e = np.zeros((128, 256), np.float32)
    for u in range(9):
        for v in range(9):
            e[9 * u + v, 16 * u + v] = 1.0 / 32.0
    return e


def local(current, previous, shift, weight, cotangent):
    pairs, channels, rows, cols = current.shape
    e = jnp.asarray(spread_matrix(), BF)
    eye = jnp.asarray(np.eye(81, 128), BF)
    total = pairs * rows * lax.axis_size("row") * cols * lax.axis_size("col")
    vmem = pl.BlockSpec(memory_space=pltpu.VMEM)
    hbm = pl.BlockSpec(memory_space=pl.ANY)
    dma = pltpu.SemaphoreType.DMA
    v = pltpu.VMEM
    gc, gp, gw = pl.pallas_call(
        functools.partial(kernel, 1.0 / math.sqrt(total)),
        in_specs=[pl.BlockSpec(memory_space=pltpu.SMEM)] + [hbm] * 3 + [vmem] * 3,
        out_specs=[hbm, hbm, vmem],
        out_shape=[
            jax.ShapeDtypeStruct((2, 8, 128, 256), BF),
            jax.ShapeDtypeStruct((2, 8, 128, 256), BF),
            jax.ShapeDtypeStruct((81, 128), F32),
        ],
        scratch_shapes=[
            v((2, 256, 8, 128), BF), v((2, 256, 8, 128), BF), v((2, 128, 8, 128), BF),
            v((2, 8, 128, 256), BF), v((2, 8, 128, 256), BF),
            v((2, 8, 128, 256), BF), v((2, 8, 128, 256), BF), v((2, 8, 128, 128), BF),
            v((2, 8, 128, 256), BF), v((2, 8, 128, 128), BF),
            v((2048, 128), F32), v((2048, 128), F32),
            v((2, 2, 256, 8, 128), BF), v((2, 2, 4, 16, 256), BF), v((2, 2, 4, 16, 256), BF),
            v((2, 8, 16, 256), BF), v((8, 16, 256), BF), v((8, 16, 256), BF),
            v((2, 4, 16, 128), BF), v((2, 4, 16, 128), BF),
            v((8, WIDE, 256), BF), v((8, WIDE, 256), BF),
            v((2, 8, WIDE, 128), F32), v((8, WIDE, 128), F32),
            v((2, 8, 8, 256), F32), v((2, 8, 8, 128), F32),
            v((2, 2, 256, 8, 128), BF),
            v((2, 2, 4, WIDE, 128), BF), v((2, 2, 4, WIDE, 128), BF),
            v((16, WIDE, 256), BF), v((16, WIDE, 256), BF),
            v((8, WIDE, 128), BF), v((8, WIDE, 128), BF),
            v((2, 8, 128, 256), F32),
            v((2, 8, 128, 128), F32), v((2, 8, 128, 128), F32),
            v((2, 8, WIDE, 256), F32), v((2, 128, 256), F32),
            v((2, 128, 256), F32),
            v((128, 128), F32), v((8, 16, 128), F32), v((4, 16, 128), F32), v((4, 16, 128), F32),
            v((8, 16, 128), F32),
            dma((2, 2)), dma((2, 2)), dma((2, 2, 3)), dma((2, 2, 3)),
            dma((8,)), dma((8,)), dma((4,)), dma((4,)), dma((4,)), dma((4,)), dma((8,)), dma((8,)),
            dma((6,)), dma((4,)),
        ],
        compiler_params=pltpu.CompilerParams(
            collective_id=0, has_side_effects=True, vmem_limit_bytes=56 << 20
        ),
        cost_estimate=pl.CostEstimate(
            flops=3_000_000_000, bytes_accessed=8 << 20, transcendentals=1_500_000
        ),
    )(shift, previous, current, cotangent, weight.T, e, eye)
    return gc.transpose(0, 3, 1, 2), gp.transpose(0, 3, 1, 2), gw.T


def solution(mesh):
    grid = P(None, None, "row", "col")
    return jax.shard_map(
        local,
        mesh=mesh,
        in_specs=(grid, grid, P(), P(), grid),
        out_specs=(grid, grid, P()),
        check_vma=False,
    )
```

```python
import functools
import math

import jax
import jax.numpy as jnp
import numpy as np
from jax import lax
from jax.experimental import pallas as pl
from jax.experimental.pallas import tpu as pltpu
from jax.sharding import PartitionSpec as P

BF = jnp.bfloat16
F32 = jnp.float32
MESH = pl.DeviceIdType.MESH
NT = (((1,), (1,)), ((), ()))
TN = (((0,), (0,)), ((), ()))
NN = (((1,), (0,)), ((), ()))
WIDE = 144


def dot(a, b, dims=NN):
    return lax.dot_general(a, b, dims, preferred_element_type=F32)


def iota(shape, axis):
    return lax.broadcasted_iota(jnp.int32, shape, axis)


def skew(x, shift):
    return pltpu.roll(x, shift % 256, 1, stride=1, stride_axis=0)


def activation(vol_dot):
    half = vol_dot * (1.0 / 32.0)
    q = 1.0 + jnp.tanh(half)
    act = half * q
    return act, q + act * (2.0 - q)


def cell_block(p, bb, rows_of, cur_ref, rev_ref):
    at = pl.multiple_of(bb * 16, 16)
    cur = cur_ref[p, :, pl.ds(at, 16), :].reshape(128, 256)
    rows = [rows_of(i, at) for i in range(8)]
    win = jnp.concatenate([r[0:16] for r in rows] + [r[8:24] for r in rows], axis=0)
    rev = rev_ref[p, :, pl.ds(at, 16), :].reshape(128, 256)
    return win, dot(jnp.concatenate([cur, rev], axis=0), win, NT)


def split_grads(grads):
    zero = jnp.zeros((8, 128), F32)
    full = [
        jnp.concatenate([zero, g] if i % 2 else [g, zero], axis=1) for i, g in enumerate(grads)
    ]
    return jnp.concatenate(full, axis=0).astype(BF)


def cells_early(p, bb, own, cur_ref, rev_ref, cot_ref, wk, sum_c, act_c, pre_c, sum_q):
    win, vol = cell_block(p, bb, lambda i, at: own[p, i, pl.ds(at, 32), :], cur_ref, rev_ref)
    at = pl.multiple_of(bb * 16, 16)
    pre = dot(cot_ref[p, :, pl.ds(at, 16), :].reshape(128, 128), wk)
    grads, acts, rest = [], [], []
    for i in range(16):
        y, odd = divmod(i, 2)
        rows = slice(8 * i, 8 * i + 8)
        lanes = slice(128 * odd, 128 * odd + 128)
        slope = activation(vol[rows, lanes])[1]
        piece = skew(pre[rows], 16 * y)
        grads.append(piece[:, :128] * slope)
        rest.append(piece[:, 128:])
        acts.append(activation(vol[128 + 8 * i : 136 + 8 * i, lanes])[0])
    act_c[p, bb] = jnp.concatenate(acts, axis=0)
    pre_c[p, bb] = jnp.concatenate(rest, axis=0)
    grad = split_grads(grads)
    sum_c[p, bb] = dot(grad, win)
    cur = cur_ref[p, :, pl.ds(at, 16), :].reshape(128, 256)
    back = dot(grad, cur, TN)
    for i in range(8):
        even, odd = back[16 * i : 16 * i + 16], back[128 + 16 * i : 128 + 16 * i + 16]
        sum_q[p, i, pl.ds(at, 8), :] += even[:8]
        sum_q[p, i, pl.ds(at + 8, 8), :] = even[8:] + odd[:8]
        sum_q[p, i, pl.ds(at + 16, 8), :] = odd[8:]


def cells_late(p, bb, dy, halo, cur_ref, rev_ref, cot_rev_ref, sum_c, act_c, pre_c, out_ref, acc_ref):
    def rows_of(i, at):
        return halo[i, pl.ds(at, 32), :]

    win, vol = cell_block(p, bb, rows_of, cur_ref, rev_ref)
    at = pl.multiple_of(bb * 16, 16)
    cot_rev = cot_rev_ref[p, :, pl.ds(at, 16), :].reshape(128, 128)
    act_own, pre = act_c[p, bb], pre_c[p, bb]
    grads, acts = [], []
    for i in range(16):
        y, odd = divmod(i, 2)
        rows = slice(8 * i, 8 * i + 8)
        lanes = slice(128 * odd, 128 * odd + 128)
        grads.append(pre[rows] * activation(vol[rows, lanes])[1])
        act = activation(vol[128 + 8 * i : 136 + 8 * i, lanes])[0]
        act = jnp.concatenate([act_own[rows], act], axis=1)
        acts.append(skew(act, 249 - 16 * y))
    act = jnp.concatenate(acts, axis=0).astype(BF)
    acc_ref[p] += dot(cot_rev, act, TN)
    out = sum_c[p, bb] + dot(split_grads(grads), win)
    out_ref[p, :, pl.ds(at, 16), :] = out.astype(BF).reshape(8, 16, 256)


def rim_positions(p, left, rim_cur, rim_cot, prev_ref, wk, masks, rim_sum):
    at = pl.multiple_of(jnp.where(left, 112, 0), 16)
    prev = prev_ref[p, :, pl.ds(at, 16), :].reshape(128, 256)
    win = rim_cur[p].reshape(64, 256).astype(BF)
    vol = dot(win, prev, NT)
    pre = dot(rim_cot[p].reshape(64, 128).astype(BF), wk)
    mask = jnp.where(left, masks[1], masks[0])
    grads = []
    for i in range(8):
        rows = slice(8 * i, 8 * i + 8)
        piece = pre[rows] * mask
        piece = jnp.where(left, skew(piece, 16 * i + 8), skew(piece, 16 * i - 8))[:, :128]
        grads.append(piece * activation(vol[rows])[1])
    rim_sum[p] = dot(jnp.concatenate(grads, axis=0).astype(BF), win, TN)


def positions_late(
    p, bb, dx, left, halo, pre_halo, prev_ref, e_fold, masks, sum_q, rim_sum, out_ref
):
    at = pl.multiple_of(bb * 16, 16)
    prev = prev_ref[p, :, pl.ds(at, 16), :].reshape(128, 256)
    win = jnp.concatenate([halo[8 + i, pl.ds(at, 32), :][:24] for i in range(8)], axis=0)
    vol = dot(win, prev, NT)
    pre = dot(
        jnp.concatenate([pre_halo[i, pl.ds(at, 32), :][:24] for i in range(8)], axis=0), e_fold
    )
    grads = []
    for i in range(8):
        for g in range(3):
            rows = slice(24 * i + 8 * g, 24 * i + 8 * g + 8)
            piece = pre[rows]
            if g != 1:
                piece = piece * masks[g // 2][:, :128]
            shift = (16 * i + 8 * (g - 1)) % 128
            piece = pltpu.roll(piece, shift, 1, stride=1, stride_axis=0)
            grads.append(piece * activation(vol[rows])[1])
    out = dot(jnp.concatenate(grads, axis=0).astype(BF), win, TN)
    own = pltpu.roll(sum_q[p, :, pl.ds(at, 24), :], (20 + dx) % 24, 1)[:, :16].reshape(128, 256)
    rim = jnp.where(bb == jnp.where(left, 7, 0), 1.0, 0.0) * rim_sum[p]
    out_ref[p, :, pl.ds(at, 16), :] = (out + own + rim).astype(BF).reshape(8, 16, 256)


def kernel(
    norm, shift_ref, prev_hbm, cur_hbm, cot_hbm, w_ref, e_ref, eye_ref,
    gc_hbm, gp_hbm, gw_ref,
    prev_in, cur_in, cot_in, gc_ref, gp_ref,
    prev_ref, cur_ref, cot_ref, rev_ref, cot_rev, flat0, flat1, msg_r, rim_s, rim_r,
    edge_s, edge_r0, edge_r1, edge_cot_s, edge_cot_r, own_all, wk_all, cot_x, own_pre, rim_cur, rim_cot,
    msg, tri_s, tri_r, halo0, halo1, pre_halo0, pre_halo1,
    sum_c, act_c, pre_c, sum_q, rim_sum, acc, ar0, ar1, ar2, ar3, ar4,
    side_ss, side_rs, row_ss, row_rs, s1, r1, s2, r2, s3, r3, s4, r4, load_sem, store_sem,
):
    row, col = lax.axis_index("row"), lax.axis_index("col")
    last = lax.axis_size("row") - 1
    left = col == 0
    owns = (own_all.at[0], own_all.at[1])
    halos, pre_halos = (halo0, halo1), (pre_halo0, pre_halo1)
    g1, g2, g3 = (row % 4) * 2 + col, (row // 4) % 4, row // 16

    def member(a, b, c):
        return ((c * 4 + b) * 4 + a // 2, a % 2)

    loads, stores = [], []
    for p in range(2):
        for source, target in ((prev_hbm, prev_in), (cur_hbm, cur_in), (cot_hbm, cot_in)):
            at = load_sem.at[len(loads)]
            loads.append(pltpu.make_async_copy(source.at[p], target.at[p], at))
        for source, target in ((gc_ref, gc_hbm), (gp_ref, gp_hbm)):
            at = store_sem.at[len(stores)]
            stores.append(pltpu.make_async_copy(source.at[p], target.at[p], at))
    for copy in loads:
        copy.start()

    barrier = pltpu.get_barrier_semaphore()

    def greet(target):
        pl.semaphore_signal(barrier, inc=1, device_id=target, device_id_type=MESH)

    for d in range(1, 8):
        greet(member((g1 + d) % 8, g2, g3))
    for d in range(1, 4):
        greet(member(g1, (g2 + d) % 4, g3))
        greet(member(g1, g2, (g3 + d) % 4))
    greet(((row + 1) % (last + 1), col))
    greet(((row + last) % (last + 1), col))

    def side(p, k):
        src, dst = (
            (edge_s.at[p], (edge_r0, edge_r1)[p]), (edge_cot_s.at[p], edge_cot_r.at[p])
        )[k]
        return pltpu.make_async_remote_copy(
            src_ref=src, dst_ref=dst, send_sem=side_ss.at[p, k],
            recv_sem=side_rs.at[p, k], device_id=(row, 1 - col), device_id_type=MESH,
        )

    def along(p, way, k):
        s, r = ((msg, msg_r), (rim_s, rim_r), (tri_s, tri_r))[k]
        src, dst = s.at[p, way], r.at[p, way]
        target = jnp.where(row == last, row, row + 1) if way else jnp.where(row == 0, row, row - 1)
        return pltpu.make_async_remote_copy(
            src_ref=src, dst_ref=dst, send_sem=row_ss.at[p, way, k],
            recv_sem=row_rs.at[p, way, k], device_id=(target, col), device_id_type=MESH,
        )

    def pack(p):
        dy = shift_ref[p, 0]

        def chunk(i, carry):
            at = pl.ds(pl.multiple_of(i * 16, 16), 16)
            pos = prev_in[p, at].astype(F32)
            cell = pltpu.roll(cur_in[p, at].astype(F32), (4 + dy) % 8, 1)
            low = iota((16, 8, 128), 1) < 4 + dy
            msg[p, 0, at] = jnp.where(low, pos, cell).astype(BF)
            msg[p, 1, at] = jnp.where(low, cell, pos).astype(BF)
            return carry

        lax.fori_loop(0, 16, chunk, 0)

    def send(p, k):
        @pl.when(row > 0)
        def _():
            along(p, 0, k).start()

        @pl.when(row < last)
        def _():
            along(p, 1, k).start()

    mirror = iota((128, 128), 0) // 8 * 8 + 7 - iota((128, 128), 0) % 8 == iota((128, 128), 1)
    mirror = jnp.where(mirror, 1.0, 0.0).astype(BF)
    ident = jnp.where(iota((128, 128), 0) == iota((128, 128), 1), 1.0, 0.0).astype(BF)

    def spread_rows(flat, x):
        flat[0 : x.shape[0] * 8] = x.reshape(x.shape[0] * 8, 128)

    def picked(flat, y, channels):
        return flat[pl.ds(y, channels, stride=8), :].astype(BF)

    def aligner(offset):
        take = iota((WIDE, 128), 1) + 8 == iota((WIDE, 128), 0) + offset
        return jnp.where(take, 1.0, 0.0).astype(BF)

    def rim_place(tile, offset):
        tile = pltpu.roll(tile, offset % 8, tile.ndim - 2)
        at = iota(tile.shape, tile.ndim - 2)
        keep = jnp.where(left, at, -1 - at) >= jnp.where(left, offset, -offset)
        return jnp.where(keep, tile, 0.0)

    def rim_add(x, rim):
        zero = jnp.zeros_like(rim)
        low, high = jnp.where(left, zero, rim), jnp.where(left, rim, zero)
        return jnp.concatenate([x[:8] + low, x[8:128], x[128:136] + high, x[136:]], axis=0)

    def turn_prev(p):
        both = jnp.concatenate([ident, aligner(4 + shift_ref[p, 1])], axis=0)
        spread_rows(flat0, prev_in[p].astype(F32))
        for y in range(8):
            x = dot(both, picked(flat0, y, 256), NT).astype(BF)
            prev_ref[p, y] = x[:128]
            owns[p][y] = x[128:]

    def turn_cells(p):
        two = jnp.concatenate([ident, mirror], axis=0)
        three = jnp.concatenate([ident, mirror, aligner(4 - shift_ref[p, 1])], axis=0)
        spread_rows(flat1, cur_in[p].astype(F32))
        for y in range(8):
            x = dot(two, picked(flat1, y, 256), NT).astype(BF)
            cur_ref[p, y] = x[:128]
            rev_ref[p, y] = x[128:]
        spread_rows(flat0, cot_in[p].astype(F32))
        for y in range(8):
            x = dot(three, picked(flat0, y, 128), NT)
            cot_ref[p, y] = x[:128].astype(BF)
            cot_rev[p, y] = x[128:256].astype(BF)
            cot_x[p, y] = x[256:]

    start = jnp.where(left, 112, 0)

    def edges(p):
        for y in range(8):
            pick = []
            for ref in (prev_ref, cur_ref):
                tile = ref[p, y, pl.ds(pl.multiple_of(start, 16), 16), :].astype(F32)
                pick.append(jnp.where(left, tile[8:], tile[:8]))
            edge_s[p, y] = jnp.concatenate(pick, axis=0).astype(BF)
        for y in range(0, 8, 2):
            pick = []
            for yy in (y, y + 1):
                tile = cot_ref[p, yy, pl.ds(pl.multiple_of(start, 16), 16), :].astype(F32)
                pick.append(jnp.where(left, tile[8:], tile[:8]))
            edge_cot_s[p, y // 2] = jnp.concatenate(pick, axis=0).astype(BF)
        for k in range(2):
            side(p, k).start()

    for copy in loads[:2]:
        copy.wait()
    pack(0)
    pl.semaphore_wait(barrier, 15)
    send(0, 0)
    for copy in loads[2:]:
        copy.wait()
    turn_prev(0)
    turn_cells(0)
    edges(0)
    pack(1)
    turn_prev(1)
    turn_cells(1)
    edges(1)

    w81 = w_ref[...]
    e = e_ref[...]
    w9 = dot(w81, eye_ref[...], TN).astype(BF)
    wk = dot(w9, e)
    e_fold = (e[:, :128].astype(F32) + e[:, 128:].astype(F32)).astype(BF)
    turns = [(16 * (shift_ref[p, 0] + 12)) % 256 for p in range(2)]
    back = [(16 * (4 - shift_ref[p, 0])) % 256 for p in range(2)]
    wks = [pltpu.roll(wk, turns[p], 1).astype(BF) for p in range(2)]
    sub, lane = iota((8, 256), 0), iota((8, 256), 1) % 16
    masks = (jnp.where(lane >= 8 - sub, 1.0, 0.0), jnp.where(lane < 8 - sub, 1.0, 0.0))
    for p in range(2):
        wk_all[p] = wks[p]
    tri_lane = iota((WIDE, 128), 1)
    acc[...] = jnp.zeros_like(acc)
    sum_q[:, :, 0:8] = jnp.zeros((2, 8, 8, 256), F32)

    def join(p):
        dy, dx = shift_ref[p, 0], shift_ref[p, 1]
        own, edge_r = owns[p], (edge_r0, edge_r1)[p]
        for k in range(2):
            side(p, k).wait()
        for y in range(8):
            edge = edge_r[y].astype(F32)
            rim = rim_place(edge[:8], 4 - dx)
            zero = jnp.zeros_like(rim)
            for at, piece in ((0, jnp.where(left, zero, rim)), (128, jnp.where(left, rim, zero))):
                tile = own[y, at : at + 16].astype(F32) + jnp.concatenate([piece, zero], axis=0)
                own[y, at : at + 16] = tile.astype(BF)
            rim_cur[p, y] = rim_place(edge[8:], 4 + dx)
            at = 8 * (y % 2)
            rim = rim_place(edge_cot_r[p, y // 2].astype(F32)[at : at + 8], 4 + dx)
            rim_cot[p, y] = rim
            own_pre[y] = dot(rim_add(cot_x[p, y], rim).astype(BF), w9)

        def tile(s, up):
            is_prev = (s < 4 + dy) if up else (s >= 4 + dy)
            at = jnp.where(is_prev, s, jnp.where(s < 4 + dy, s + 4 - dy, s - 4 - dy))
            both = edge_r[at].astype(F32)
            return jnp.where(is_prev, both[:8], both[8:])

        for k in range(4):
            for way in range(2):
                pair = [tile(2 * k, way == 0), tile(2 * k + 1, way == 0)]
                rim_s[p, way, k] = jnp.concatenate(pair, axis=0).astype(BF)

        def cell_row(t):
            return own_pre[jnp.where(t < 4 + dy, t + 4 - dy, t - 4 - dy)]

        for s in range(4):
            near, away = cell_row(s), cell_row(7 - s)
            tri_s[p, 1, s] = jnp.where(
                tri_lane >= 9 * (8 - s), near, pltpu.roll(away, 128 - 9 * (s + 1), 1)
            ).astype(BF)
            tri_s[p, 0, s] = jnp.where(
                tri_lane < 9 * (8 - s), near, pltpu.roll(away, 9 * (8 - s), 1)
            ).astype(BF)
        send(p, 1)
        send(p, 2)

    join(0)
    send(1, 0)
    join(1)

    def arrive(p):
        dy, dx = shift_ref[p, 0], shift_ref[p, 1]
        halo = halos[p]
        take_p, take_c = aligner(4 + dx), aligner(4 - dx)

        def receive(k, buffer):
            for way, edge_row in ((1, 0), (0, last)):

                @pl.when(row != edge_row)
                def _():
                    along(p, way, k).wait_recv()

                @pl.when(row == edge_row)
                def _():
                    part = buffer.at[p, way]
                    part[...] = jnp.zeros(part.shape, BF)

        for k, buffer in enumerate((msg_r, rim_r, tri_r)):
            receive(k, buffer)

        def sort(i, carry):
            at = pl.ds(pl.multiple_of(i * 16, 16), 16)
            to = pl.ds(pl.multiple_of(i * 128, 128), 128)
            up, down = msg_r[p, 0, at].astype(F32), msg_r[p, 1, at].astype(F32)
            low = iota((16, 8, 128), 1) < 4 + dy
            flat0[to] = jnp.where(low, up, down).reshape(128, 128)
            flat1[to] = jnp.where(low, down, up).reshape(128, 128)
            return carry

        lax.fori_loop(0, 16, sort, 0)
        for s in range(8):
            at = 8 * (s % 2)
            up = rim_r[p, 0, s // 2].astype(F32)[at : at + 8]
            down = rim_r[p, 1, s // 2].astype(F32)[at : at + 8]
            low = s < 4 + dy
            x = dot(take_p, picked(flat0, s, 256), NT)
            rim = rim_place(jnp.where(low, up, down), 4 - dx)
            halo[s] = rim_add(x, rim).astype(BF)
            x = dot(take_c, picked(flat1, s, 256), NT)
            rim = rim_place(jnp.where(low, down, up), 4 + dx)
            halo[8 + s] = rim_add(x, rim).astype(BF)
        for s in range(4):
            up, down = tri_r[p, 0, s].astype(F32), tri_r[p, 1, s].astype(F32)
            near = tri_lane >= 9 * (8 - s)
            x = jnp.where(near == (s < 4 + dy), jnp.where(s < 4 + dy, down, up), 0.0)
            pre_halos[p][s] = x.astype(BF)
            down = pltpu.roll(down, 9 * (s + 1), 1)
            up = pltpu.roll(up, 128 - 9 * (8 - s), 1)
            near = tri_lane >= 9 * (s + 1)
            x = jnp.where(near == (7 - s < 4 + dy), jnp.where(7 - s < 4 + dy, down, up), 0.0)
            pre_halos[p][7 - s] = jnp.where(tri_lane < 81, x, 0.0).astype(BF)

    def loop(lo, hi, work):
        def body(bb, carry):
            work(bb)
            return carry

        lax.fori_loop(lo, hi, body, 0)

    def early(i):
        p, bb = i // 8, i % 8
        cells_early(
            p, bb, own_all, cur_ref, rev_ref, cot_ref, wk_all[p], sum_c, act_c, pre_c, sum_q)

    def late_cells(p, bb):
        cells_late(
            p, bb, shift_ref[p, 0], halos[p], cur_ref, rev_ref, cot_rev, sum_c, act_c, pre_c,
            gc_ref, acc)

    def late_positions(p, bb):
        positions_late(
            p, bb, shift_ref[p, 1], left, halos[p], pre_halos[p], prev_ref, e_fold, masks,
            sum_q, rim_sum, gp_ref)

    def late(bb):
        late_cells(0, bb)
        late_positions(0, bb)

    loop(0, 16, early)
    for p in range(2):
        rim_positions(p, left, rim_cur, rim_cot, prev_ref, wks[p], masks, rim_sum)
    arrive(0)
    loop(0, 8, late)
    stores[0].start()
    stores[1].start()
    arrive(1)
    loop(0, 8, lambda bb: late_cells(1, bb))

    stores[2].start()

    turned = (pltpu.roll(acc[0], back[0], 1) + pltpu.roll(acc[1], back[1], 1)).T
    for u in range(9):
        ar0[9 * u : 9 * u + 9] = turned[16 * u : 16 * u + 9]
    ar0[81:128] = jnp.zeros((47, 128), F32)

    def share(ref, i):
        return ref.at[pl.ds(pl.multiple_of(i * 16, 16), 16)]

    def first(d):
        peer = (g1 + d) % 8
        return pltpu.make_async_remote_copy(
            src_ref=share(ar0, peer), dst_ref=ar1.at[g1], send_sem=s1.at[peer],
            recv_sem=r1.at[g1], device_id=member(peer, g2, g3), device_id_type=MESH,
        )

    def second(d):
        peer = (g2 + d) % 4
        return pltpu.make_async_remote_copy(
            src_ref=ar2.at[g2], dst_ref=ar2.at[g2], send_sem=s2.at[peer],
            recv_sem=r2.at[g2], device_id=member(g1, peer, g3), device_id_type=MESH,
        )

    def third(d):
        peer = (g3 + d) % 4
        return pltpu.make_async_remote_copy(
            src_ref=ar3.at[g3], dst_ref=ar3.at[g3], send_sem=s3.at[peer],
            recv_sem=r3.at[g3], device_id=member(g1, g2, peer), device_id_type=MESH,
        )

    def fourth(d):
        peer = (g1 + d) % 8
        return pltpu.make_async_remote_copy(
            src_ref=ar4.at[g1], dst_ref=ar4.at[g1], send_sem=s4.at[peer],
            recv_sem=r4.at[g1], device_id=member(peer, g2, g3), device_id_type=MESH,
        )

    def got(buffer, sends, receives, source):
        pltpu.make_async_remote_copy(
            src_ref=buffer.at[source], dst_ref=buffer.at[source], send_sem=sends.at[source],
            recv_sem=receives.at[source], device_id=(row, 1 - col), device_id_type=MESH,
        ).wait_recv()

    def some_positions(lo, hi):
        loop(lo, hi, lambda bb: late_positions(1, bb))

    for d in range(1, 8):
        first(d).start()
    some_positions(0, 2)
    ar1[g1] = ar0[pl.ds(pl.multiple_of(g1 * 16, 16), 16)]
    for d in range(1, 8):
        first(d).wait_send()
        got(ar1, s1, r1, (g1 + d) % 8)
    ar2[g2] = jnp.sum(ar1[...], axis=0)
    for d in range(1, 4):
        second(d).start()
    some_positions(2, 4)
    for d in range(1, 4):
        second(d).wait_send()
        got(ar2, s2, r2, (g2 + d) % 4)
    ar3[g3] = jnp.sum(ar2[...], axis=0)
    for d in range(1, 4):
        third(d).start()
    some_positions(4, 6)
    for d in range(1, 4):
        third(d).wait_send()
        got(ar3, s3, r3, (g3 + d) % 4)
    ar4[g1] = jnp.sum(ar3[...], axis=0)
    for d in range(1, 8):
        fourth(d).start()
    some_positions(6, 8)
    stores[3].start()
    for d in range(1, 8):
        fourth(d).wait_send()
        got(ar4, s4, r4, (g1 + d) % 8)
    gw_ref[...] = ar4[...].reshape(128, 128)[:81] * norm
    for copy in stores:
        copy.wait()

    for p in range(2):
        for k in range(3):

            @pl.when(row > 0)
            def _():
                along(p, 0, k).wait_send()

            @pl.when(row < last)
            def _():
                along(p, 1, k).wait_send()


def spread_matrix():
    e = np.zeros((128, 256), np.float32)
    for u in range(9):
        for v in range(9):
            e[9 * u + v, 16 * u + v] = 1.0 / 32.0
    return e


def local(current, previous, shift, weight, cotangent):
    pairs, channels, rows, cols = current.shape
    e = jnp.asarray(spread_matrix(), BF)
    eye = jnp.asarray(np.eye(81, 128), BF)
    total = pairs * rows * lax.axis_size("row") * cols * lax.axis_size("col")
    vmem = pl.BlockSpec(memory_space=pltpu.VMEM)
    hbm = pl.BlockSpec(memory_space=pl.ANY)
    dma = pltpu.SemaphoreType.DMA
    v = pltpu.VMEM
    gc, gp, gw = pl.pallas_call(
        functools.partial(kernel, 1.0 / math.sqrt(total)),
        in_specs=[pl.BlockSpec(memory_space=pltpu.SMEM)] + [hbm] * 3 + [vmem] * 3,
        out_specs=[hbm, hbm, vmem],
        out_shape=[
            jax.ShapeDtypeStruct((2, 8, 128, 256), BF),
            jax.ShapeDtypeStruct((2, 8, 128, 256), BF),
            jax.ShapeDtypeStruct((81, 128), F32),
        ],
        scratch_shapes=[
            v((2, 256, 8, 128), BF), v((2, 256, 8, 128), BF), v((2, 128, 8, 128), BF),
            v((2, 8, 128, 256), BF), v((2, 8, 128, 256), BF),
            v((2, 8, 128, 256), BF), v((2, 8, 128, 256), BF), v((2, 8, 128, 128), BF),
            v((2, 8, 128, 256), BF), v((2, 8, 128, 128), BF),
            v((2048, 128), F32), v((2048, 128), F32),
            v((2, 2, 256, 8, 128), BF), v((2, 2, 4, 16, 256), BF), v((2, 2, 4, 16, 256), BF),
            v((2, 8, 16, 256), BF), v((8, 16, 256), BF), v((8, 16, 256), BF),
            v((2, 4, 16, 128), BF), v((2, 4, 16, 128), BF),
            v((2, 8, WIDE, 256), BF), v((2, 128, 256), BF),
            v((2, 8, WIDE, 128), F32), v((8, WIDE, 128), F32),
            v((2, 8, 8, 256), F32), v((2, 8, 8, 128), F32),
            v((2, 2, 256, 8, 128), BF),
            v((2, 2, 4, WIDE, 128), BF), v((2, 2, 4, WIDE, 128), BF),
            v((16, WIDE, 256), BF), v((16, WIDE, 256), BF),
            v((8, WIDE, 128), BF), v((8, WIDE, 128), BF),
            v((2, 8, 128, 256), F32),
            v((2, 8, 128, 128), F32), v((2, 8, 128, 128), F32),
            v((2, 8, WIDE, 256), F32), v((2, 128, 256), F32),
            v((2, 128, 256), F32),
            v((128, 128), F32), v((8, 16, 128), F32), v((4, 16, 128), F32), v((4, 16, 128), F32),
            v((8, 16, 128), F32),
            dma((2, 2)), dma((2, 2)), dma((2, 2, 3)), dma((2, 2, 3)),
            dma((8,)), dma((8,)), dma((4,)), dma((4,)), dma((4,)), dma((4,)), dma((8,)), dma((8,)),
            dma((6,)), dma((4,)),
        ],
        compiler_params=pltpu.CompilerParams(
            collective_id=0, has_side_effects=True, vmem_limit_bytes=56 << 20
        ),
        cost_estimate=pl.CostEstimate(
            flops=3_000_000_000, bytes_accessed=8 << 20, transcendentals=1_500_000
        ),
    )(shift, previous, current, cotangent, weight.T, e, eye)
    return gc.transpose(0, 3, 1, 2), gp.transpose(0, 3, 1, 2), gw.T


def solution(mesh):
    grid = P(None, None, "row", "col")
    return jax.shard_map(
        local,
        mesh=mesh,
        in_specs=(grid, grid, P(), P(), grid),
        out_specs=(grid, grid, P()),
        check_vma=False,
    )
```

```python
import functools
import math

import jax
import jax.numpy as jnp
import numpy as np
from jax import lax
from jax.experimental import pallas as pl
from jax.experimental.pallas import tpu as pltpu
from jax.sharding import PartitionSpec as P

BF = jnp.bfloat16
F32 = jnp.float32
MESH = pl.DeviceIdType.MESH
NT = (((1,), (1,)), ((), ()))
TN = (((0,), (0,)), ((), ()))
NN = (((1,), (0,)), ((), ()))
WIDE = 144


def dot(a, b, dims=NN):
    return lax.dot_general(a, b, dims, preferred_element_type=F32)


def iota(shape, axis):
    return lax.broadcasted_iota(jnp.int32, shape, axis)


def skew(x, shift):
    return pltpu.roll(x, shift % 256, 1, stride=1, stride_axis=0)


def activation(vol_dot):
    half = vol_dot * (1.0 / 32.0)
    q = 1.0 + jnp.tanh(half)
    act = half * q
    return act, q + act * (2.0 - q)


def cell_block(p, bb, rows_of, cur_ref, rev_ref):
    at = pl.multiple_of(bb * 16, 16)
    cur = cur_ref[p, :, pl.ds(at, 16), :].reshape(128, 256)
    rows = [rows_of(i, at) for i in range(8)]
    win = jnp.concatenate([r[0:16] for r in rows] + [r[8:24] for r in rows], axis=0)
    rev = rev_ref[p, :, pl.ds(at, 16), :].reshape(128, 256)
    return win, dot(jnp.concatenate([cur, rev], axis=0), win, NT)


def split_grads(grads):
    zero = jnp.zeros((8, 128), F32)
    full = [
        jnp.concatenate([zero, g] if i % 2 else [g, zero], axis=1) for i, g in enumerate(grads)
    ]
    return jnp.concatenate(full, axis=0).astype(BF)


def cells_early(p, bb, own, cur_ref, rev_ref, cot_ref, wk, sum_c, act_c, pre_c, sum_q):
    win, vol = cell_block(p, bb, lambda i, at: own[i, pl.ds(at, 32), :], cur_ref, rev_ref)
    at = pl.multiple_of(bb * 16, 16)
    pre = dot(cot_ref[p, :, pl.ds(at, 16), :].reshape(128, 128), wk)
    grads, acts, rest = [], [], []
    for i in range(16):
        y, odd = divmod(i, 2)
        rows = slice(8 * i, 8 * i + 8)
        lanes = slice(128 * odd, 128 * odd + 128)
        slope = activation(vol[rows, lanes])[1]
        piece = skew(pre[rows], 16 * y)
        grads.append(piece[:, :128] * slope)
        rest.append(piece[:, 128:])
        acts.append(activation(vol[128 + 8 * i : 136 + 8 * i, lanes])[0])
    act_c[p, bb] = jnp.concatenate(acts, axis=0)
    pre_c[p, bb] = jnp.concatenate(rest, axis=0)
    grad = split_grads(grads)
    sum_c[p, bb] = dot(grad, win)
    cur = cur_ref[p, :, pl.ds(at, 16), :].reshape(128, 256)
    back = dot(grad, cur, TN)
    for i in range(8):
        even, odd = back[16 * i : 16 * i + 16], back[128 + 16 * i : 128 + 16 * i + 16]
        sum_q[p, i, pl.ds(at, 8), :] += even[:8]
        sum_q[p, i, pl.ds(at + 8, 8), :] = even[8:] + odd[:8]
        sum_q[p, i, pl.ds(at + 16, 8), :] = odd[8:]


def cells_late(p, bb, dy, halo, cur_ref, rev_ref, cot_rev_ref, sum_c, act_c, pre_c, out_ref, acc_ref):
    def rows_of(i, at):
        return halo[i, pl.ds(at, 32), :]

    win, vol = cell_block(p, bb, rows_of, cur_ref, rev_ref)
    at = pl.multiple_of(bb * 16, 16)
    cot_rev = cot_rev_ref[p, :, pl.ds(at, 16), :].reshape(128, 128)
    act_own, pre = act_c[p, bb], pre_c[p, bb]
    grads, acts = [], []
    for i in range(16):
        y, odd = divmod(i, 2)
        rows = slice(8 * i, 8 * i + 8)
        lanes = slice(128 * odd, 128 * odd + 128)
        grads.append(pre[rows] * activation(vol[rows, lanes])[1])
        act = activation(vol[128 + 8 * i : 136 + 8 * i, lanes])[0]
        act = jnp.concatenate([act_own[rows], act], axis=1)
        acts.append(skew(act, 249 - 16 * y))
    act = jnp.concatenate(acts, axis=0).astype(BF)
    acc_ref[p] += dot(cot_rev, act, TN)
    out = sum_c[p, bb] + dot(split_grads(grads), win)
    out_ref[p, :, pl.ds(at, 16), :] = out.astype(BF).reshape(8, 16, 256)


def rim_positions(p, left, rim_cur, rim_cot, prev_ref, wk, masks, rim_sum):
    at = pl.multiple_of(jnp.where(left, 112, 0), 16)
    prev = prev_ref[p, :, pl.ds(at, 16), :].reshape(128, 256)
    win = rim_cur[p].reshape(64, 256).astype(BF)
    vol = dot(win, prev, NT)
    pre = dot(rim_cot[p].reshape(64, 128).astype(BF), wk)
    mask = jnp.where(left, masks[1], masks[0])
    grads = []
    for i in range(8):
        rows = slice(8 * i, 8 * i + 8)
        piece = pre[rows] * mask
        piece = jnp.where(left, skew(piece, 16 * i + 8), skew(piece, 16 * i - 8))[:, :128]
        grads.append(piece * activation(vol[rows])[1])
    rim_sum[p] = dot(jnp.concatenate(grads, axis=0).astype(BF), win, TN)


def positions_late(
    p, bb, dx, left, halo, pre_halo, prev_ref, e_fold, masks, sum_q, rim_sum, out_ref
):
    at = pl.multiple_of(bb * 16, 16)
    prev = prev_ref[p, :, pl.ds(at, 16), :].reshape(128, 256)
    win = jnp.concatenate([halo[8 + i, pl.ds(at, 32), :][:24] for i in range(8)], axis=0)
    vol = dot(win, prev, NT)
    pre = dot(
        jnp.concatenate([pre_halo[i, pl.ds(at, 32), :][:24] for i in range(8)], axis=0), e_fold
    )
    grads = []
    for i in range(8):
        for g in range(3):
            rows = slice(24 * i + 8 * g, 24 * i + 8 * g + 8)
            piece = pre[rows]
            if g != 1:
                piece = piece * masks[g // 2][:, :128]
            shift = (16 * i + 8 * (g - 1)) % 128
            piece = pltpu.roll(piece, shift, 1, stride=1, stride_axis=0)
            grads.append(piece * activation(vol[rows])[1])
    out = dot(jnp.concatenate(grads, axis=0).astype(BF), win, TN)
    own = pltpu.roll(sum_q[p, :, pl.ds(at, 24), :], (20 + dx) % 24, 1)[:, :16].reshape(128, 256)
    rim = jnp.where(bb == jnp.where(left, 7, 0), 1.0, 0.0) * rim_sum[p]
    out_ref[p, :, pl.ds(at, 16), :] = (out + own + rim).astype(BF).reshape(8, 16, 256)


def kernel(
    norm, shift_ref, prev_hbm, cur_hbm, cot_hbm, w_ref, e_ref, eye_ref,
    gc_hbm, gp_hbm, gw_ref,
    prev_in, cur_in, cot_in, gc_ref, gp_ref,
    prev_ref, cur_ref, cot_ref, rev_ref, cot_rev, flat0, flat1, msg_r, rim_s, rim_r,
    edge_s, edge_r0, edge_r1, edge_cot_s, edge_cot_r, own0, own1, cot_x, own_pre, rim_cur, rim_cot,
    msg, tri_s, tri_r, halo0, halo1, pre_halo0, pre_halo1,
    sum_c, act_c, pre_c, sum_q, rim_sum, acc, ar0, ar1, ar2, ar3, ar4,
    side_ss, side_rs, row_ss, row_rs, s1, r1, s2, r2, s3, r3, s4, r4, load_sem, store_sem,
):
    row, col = lax.axis_index("row"), lax.axis_index("col")
    last = lax.axis_size("row") - 1
    left = col == 0
    owns = (own0, own1)
    halos, pre_halos = (halo0, halo1), (pre_halo0, pre_halo1)
    g1, g2, g3 = (row % 4) * 2 + col, (row // 4) % 4, row // 16

    def member(a, b, c):
        return ((c * 4 + b) * 4 + a // 2, a % 2)

    loads, stores = [], []
    for p in range(2):
        for source, target in ((prev_hbm, prev_in), (cur_hbm, cur_in), (cot_hbm, cot_in)):
            at = load_sem.at[len(loads)]
            loads.append(pltpu.make_async_copy(source.at[p], target.at[p], at))
        for source, target in ((gc_ref, gc_hbm), (gp_ref, gp_hbm)):
            at = store_sem.at[len(stores)]
            stores.append(pltpu.make_async_copy(source.at[p], target.at[p], at))
    for copy in loads:
        copy.start()

    barrier = pltpu.get_barrier_semaphore()

    def greet(target):
        pl.semaphore_signal(barrier, inc=1, device_id=target, device_id_type=MESH)

    for d in range(1, 8):
        greet(member((g1 + d) % 8, g2, g3))
    for d in range(1, 4):
        greet(member(g1, (g2 + d) % 4, g3))
        greet(member(g1, g2, (g3 + d) % 4))
    greet(((row + 1) % (last + 1), col))
    greet(((row + last) % (last + 1), col))

    def side(p, k):
        src, dst = (
            (edge_s.at[p], (edge_r0, edge_r1)[p]), (edge_cot_s.at[p], edge_cot_r.at[p])
        )[k]
        return pltpu.make_async_remote_copy(
            src_ref=src, dst_ref=dst, send_sem=side_ss.at[p, k],
            recv_sem=side_rs.at[p, k], device_id=(row, 1 - col), device_id_type=MESH,
        )

    def along(p, way, k):
        s, r = ((msg, msg_r), (rim_s, rim_r), (tri_s, tri_r))[k]
        src, dst = s.at[p, way], r.at[p, way]
        target = jnp.where(row == last, row, row + 1) if way else jnp.where(row == 0, row, row - 1)
        return pltpu.make_async_remote_copy(
            src_ref=src, dst_ref=dst, send_sem=row_ss.at[p, way, k],
            recv_sem=row_rs.at[p, way, k], device_id=(target, col), device_id_type=MESH,
        )

    def pack(p):
        dy = shift_ref[p, 0]

        def chunk(i, carry):
            at = pl.ds(pl.multiple_of(i * 16, 16), 16)
            pos = prev_in[p, at].astype(F32)
            cell = pltpu.roll(cur_in[p, at].astype(F32), (4 + dy) % 8, 1)
            low = iota((16, 8, 128), 1) < 4 + dy
            msg[p, 0, at] = jnp.where(low, pos, cell).astype(BF)
            msg[p, 1, at] = jnp.where(low, cell, pos).astype(BF)
            return carry

        lax.fori_loop(0, 16, chunk, 0)

    def send(p, k):
        @pl.when(row > 0)
        def _():
            along(p, 0, k).start()

        @pl.when(row < last)
        def _():
            along(p, 1, k).start()

    mirror = iota((128, 128), 0) // 8 * 8 + 7 - iota((128, 128), 0) % 8 == iota((128, 128), 1)
    mirror = jnp.where(mirror, 1.0, 0.0).astype(BF)
    ident = jnp.where(iota((128, 128), 0) == iota((128, 128), 1), 1.0, 0.0).astype(BF)

    def spread_rows(flat, x):
        flat[0 : x.shape[0] * 8] = x.reshape(x.shape[0] * 8, 128)

    def picked(flat, y, channels):
        return flat[pl.ds(y, channels, stride=8), :].astype(BF)

    def aligner(offset):
        take = iota((WIDE, 128), 1) + 8 == iota((WIDE, 128), 0) + offset
        return jnp.where(take, 1.0, 0.0).astype(BF)

    def rim_place(tile, offset):
        tile = pltpu.roll(tile, offset % 8, tile.ndim - 2)
        at = iota(tile.shape, tile.ndim - 2)
        keep = jnp.where(left, at, -1 - at) >= jnp.where(left, offset, -offset)
        return jnp.where(keep, tile, 0.0)

    def rim_add(x, rim):
        zero = jnp.zeros_like(rim)
        low, high = jnp.where(left, zero, rim), jnp.where(left, rim, zero)
        return jnp.concatenate([x[:8] + low, x[8:128], x[128:136] + high, x[136:]], axis=0)

    def turn_prev(p):
        both = jnp.concatenate([ident, aligner(4 + shift_ref[p, 1])], axis=0)
        spread_rows(flat0, prev_in[p].astype(F32))
        for y in range(8):
            x = dot(both, picked(flat0, y, 256), NT).astype(BF)
            prev_ref[p, y] = x[:128]
            owns[p][y] = x[128:]

    def turn_cells(p):
        two = jnp.concatenate([ident, mirror], axis=0)
        three = jnp.concatenate([ident, mirror, aligner(4 - shift_ref[p, 1])], axis=0)
        spread_rows(flat1, cur_in[p].astype(F32))
        for y in range(8):
            x = dot(two, picked(flat1, y, 256), NT).astype(BF)
            cur_ref[p, y] = x[:128]
            rev_ref[p, y] = x[128:]
        spread_rows(flat0, cot_in[p].astype(F32))
        for y in range(8):
            x = dot(three, picked(flat0, y, 128), NT)
            cot_ref[p, y] = x[:128].astype(BF)
            cot_rev[p, y] = x[128:256].astype(BF)
            cot_x[p, y] = x[256:]

    start = jnp.where(left, 112, 0)

    def edges(p):
        for y in range(8):
            pick = []
            for ref in (prev_ref, cur_ref):
                tile = ref[p, y, pl.ds(pl.multiple_of(start, 16), 16), :].astype(F32)
                pick.append(jnp.where(left, tile[8:], tile[:8]))
            edge_s[p, y] = jnp.concatenate(pick, axis=0).astype(BF)
        for y in range(0, 8, 2):
            pick = []
            for yy in (y, y + 1):
                tile = cot_ref[p, yy, pl.ds(pl.multiple_of(start, 16), 16), :].astype(F32)
                pick.append(jnp.where(left, tile[8:], tile[:8]))
            edge_cot_s[p, y // 2] = jnp.concatenate(pick, axis=0).astype(BF)
        for k in range(2):
            side(p, k).start()

    for copy in loads[:2]:
        copy.wait()
    pack(0)
    pl.semaphore_wait(barrier, 15)
    send(0, 0)
    for copy in loads[2:]:
        copy.wait()
    turn_prev(0)
    turn_cells(0)
    edges(0)
    pack(1)
    turn_prev(1)
    turn_cells(1)
    edges(1)

    w81 = w_ref[...]
    e = e_ref[...]
    w9 = dot(w81, eye_ref[...], TN).astype(BF)
    wk = dot(w9, e)
    e_fold = (e[:, :128].astype(F32) + e[:, 128:].astype(F32)).astype(BF)
    turns = [(16 * (shift_ref[p, 0] + 12)) % 256 for p in range(2)]
    back = [(16 * (4 - shift_ref[p, 0])) % 256 for p in range(2)]
    wks = [pltpu.roll(wk, turns[p], 1).astype(BF) for p in range(2)]
    sub, lane = iota((8, 256), 0), iota((8, 256), 1) % 16
    masks = (jnp.where(lane >= 8 - sub, 1.0, 0.0), jnp.where(lane < 8 - sub, 1.0, 0.0))
    tri_lane = iota((WIDE, 128), 1)
    acc[...] = jnp.zeros_like(acc)
    sum_q[:, :, 0:8] = jnp.zeros((2, 8, 8, 256), F32)

    def join(p):
        dy, dx = shift_ref[p, 0], shift_ref[p, 1]
        own, edge_r = owns[p], (edge_r0, edge_r1)[p]
        for k in range(2):
            side(p, k).wait()
        for y in range(8):
            edge = edge_r[y].astype(F32)
            rim = rim_place(edge[:8], 4 - dx)
            zero = jnp.zeros_like(rim)
            for at, piece in ((0, jnp.where(left, zero, rim)), (128, jnp.where(left, rim, zero))):
                tile = own[y, at : at + 16].astype(F32) + jnp.concatenate([piece, zero], axis=0)
                own[y, at : at + 16] = tile.astype(BF)
            rim_cur[p, y] = rim_place(edge[8:], 4 + dx)
            at = 8 * (y % 2)
            rim = rim_place(edge_cot_r[p, y // 2].astype(F32)[at : at + 8], 4 + dx)
            rim_cot[p, y] = rim
            own_pre[y] = dot(rim_add(cot_x[p, y], rim).astype(BF), w9)

        def tile(s, up):
            is_prev = (s < 4 + dy) if up else (s >= 4 + dy)
            at = jnp.where(is_prev, s, jnp.where(s < 4 + dy, s + 4 - dy, s - 4 - dy))
            both = edge_r[at].astype(F32)
            return jnp.where(is_prev, both[:8], both[8:])

        for k in range(4):
            for way in range(2):
                pair = [tile(2 * k, way == 0), tile(2 * k + 1, way == 0)]
                rim_s[p, way, k] = jnp.concatenate(pair, axis=0).astype(BF)

        def cell_row(t):
            return own_pre[jnp.where(t < 4 + dy, t + 4 - dy, t - 4 - dy)]

        for s in range(4):
            near, away = cell_row(s), cell_row(7 - s)
            tri_s[p, 1, s] = jnp.where(
                tri_lane >= 9 * (8 - s), near, pltpu.roll(away, 128 - 9 * (s + 1), 1)
            ).astype(BF)
            tri_s[p, 0, s] = jnp.where(
                tri_lane < 9 * (8 - s), near, pltpu.roll(away, 9 * (8 - s), 1)
            ).astype(BF)
        send(p, 1)
        send(p, 2)

    join(0)
    send(1, 0)
    join(1)

    def arrive(p):
        dy, dx = shift_ref[p, 0], shift_ref[p, 1]
        halo = halos[p]
        take_p, take_c = aligner(4 + dx), aligner(4 - dx)

        def receive(k, buffer):
            for way, edge_row in ((1, 0), (0, last)):

                @pl.when(row != edge_row)
                def _():
                    along(p, way, k).wait_recv()

                @pl.when(row == edge_row)
                def _():
                    part = buffer.at[p, way]
                    part[...] = jnp.zeros(part.shape, BF)

        for k, buffer in enumerate((msg_r, rim_r, tri_r)):
            receive(k, buffer)

        def sort(i, carry):
            at = pl.ds(pl.multiple_of(i * 16, 16), 16)
            to = pl.ds(pl.multiple_of(i * 128, 128), 128)
            up, down = msg_r[p, 0, at].astype(F32), msg_r[p, 1, at].astype(F32)
            low = iota((16, 8, 128), 1) < 4 + dy
            flat0[to] = jnp.where(low, up, down).reshape(128, 128)
            flat1[to] = jnp.where(low, down, up).reshape(128, 128)
            return carry

        lax.fori_loop(0, 16, sort, 0)
        for s in range(8):
            at = 8 * (s % 2)
            up = rim_r[p, 0, s // 2].astype(F32)[at : at + 8]
            down = rim_r[p, 1, s // 2].astype(F32)[at : at + 8]
            low = s < 4 + dy
            x = dot(take_p, picked(flat0, s, 256), NT)
            rim = rim_place(jnp.where(low, up, down), 4 - dx)
            halo[s] = rim_add(x, rim).astype(BF)
            x = dot(take_c, picked(flat1, s, 256), NT)
            rim = rim_place(jnp.where(low, down, up), 4 + dx)
            halo[8 + s] = rim_add(x, rim).astype(BF)
        for s in range(4):
            up, down = tri_r[p, 0, s].astype(F32), tri_r[p, 1, s].astype(F32)
            near = tri_lane >= 9 * (8 - s)
            x = jnp.where(near == (s < 4 + dy), jnp.where(s < 4 + dy, down, up), 0.0)
            pre_halos[p][s] = x.astype(BF)
            down = pltpu.roll(down, 9 * (s + 1), 1)
            up = pltpu.roll(up, 128 - 9 * (8 - s), 1)
            near = tri_lane >= 9 * (s + 1)
            x = jnp.where(near == (7 - s < 4 + dy), jnp.where(7 - s < 4 + dy, down, up), 0.0)
            pre_halos[p][7 - s] = jnp.where(tri_lane < 81, x, 0.0).astype(BF)

    def loop(lo, hi, work):
        def body(bb, carry):
            work(bb)
            return carry

        lax.fori_loop(lo, hi, body, 0)

    def early(p):
        def work(i):
            for bb in [4 * i + k for k in range(4)]:
                cells_early(
                    p, bb, owns[p], cur_ref, rev_ref, cot_ref, wks[p], sum_c, act_c, pre_c, sum_q)

        loop(0, 2, work)
        rim_positions(p, left, rim_cur, rim_cot, prev_ref, wks[p], masks, rim_sum)

    def late_cells(p, bb):
        cells_late(
            p, bb, shift_ref[p, 0], halos[p], cur_ref, rev_ref, cot_rev, sum_c, act_c, pre_c,
            gc_ref, acc)

    def late_positions(p, bb):
        positions_late(
            p, bb, shift_ref[p, 1], left, halos[p], pre_halos[p], prev_ref, e_fold, masks,
            sum_q, rim_sum, gp_ref)

    def late(i):
        for bb in [4 * i + k for k in range(4)]:
            late_cells(0, bb)
            late_positions(0, bb)

    early(0)
    early(1)
    arrive(0)
    loop(0, 2, late)
    stores[0].start()
    stores[1].start()
    arrive(1)
    loop(0, 2, lambda i: [late_cells(1, 4 * i + k) for k in range(4)])

    stores[2].start()

    turned = (pltpu.roll(acc[0], back[0], 1) + pltpu.roll(acc[1], back[1], 1)).T
    for u in range(9):
        ar0[9 * u : 9 * u + 9] = turned[16 * u : 16 * u + 9]
    ar0[81:128] = jnp.zeros((47, 128), F32)

    def share(ref, i):
        return ref.at[pl.ds(pl.multiple_of(i * 16, 16), 16)]

    def first(d):
        peer = (g1 + d) % 8
        return pltpu.make_async_remote_copy(
            src_ref=share(ar0, peer), dst_ref=ar1.at[g1], send_sem=s1.at[peer],
            recv_sem=r1.at[g1], device_id=member(peer, g2, g3), device_id_type=MESH,
        )

    def second(d):
        peer = (g2 + d) % 4
        return pltpu.make_async_remote_copy(
            src_ref=ar2.at[g2], dst_ref=ar2.at[g2], send_sem=s2.at[peer],
            recv_sem=r2.at[g2], device_id=member(g1, peer, g3), device_id_type=MESH,
        )

    def third(d):
        peer = (g3 + d) % 4
        return pltpu.make_async_remote_copy(
            src_ref=ar3.at[g3], dst_ref=ar3.at[g3], send_sem=s3.at[peer],
            recv_sem=r3.at[g3], device_id=member(g1, g2, peer), device_id_type=MESH,
        )

    def fourth(d):
        peer = (g1 + d) % 8
        return pltpu.make_async_remote_copy(
            src_ref=ar4.at[g1], dst_ref=ar4.at[g1], send_sem=s4.at[peer],
            recv_sem=r4.at[g1], device_id=member(peer, g2, g3), device_id_type=MESH,
        )

    def got(buffer, sends, receives, source):
        pltpu.make_async_remote_copy(
            src_ref=buffer.at[source], dst_ref=buffer.at[source], send_sem=sends.at[source],
            recv_sem=receives.at[source], device_id=(row, 1 - col), device_id_type=MESH,
        ).wait_recv()

    def some_positions(lo, hi):
        loop(0, 1, lambda i: [late_positions(1, k) for k in range(lo, hi)])

    for d in range(1, 8):
        first(d).start()
    some_positions(0, 2)
    ar1[g1] = ar0[pl.ds(pl.multiple_of(g1 * 16, 16), 16)]
    for d in range(1, 8):
        first(d).wait_send()
        got(ar1, s1, r1, (g1 + d) % 8)
    ar2[g2] = jnp.sum(ar1[...], axis=0)
    for d in range(1, 4):
        second(d).start()
    some_positions(2, 4)
    for d in range(1, 4):
        second(d).wait_send()
        got(ar2, s2, r2, (g2 + d) % 4)
    ar3[g3] = jnp.sum(ar2[...], axis=0)
    for d in range(1, 4):
        third(d).start()
    some_positions(4, 6)
    for d in range(1, 4):
        third(d).wait_send()
        got(ar3, s3, r3, (g3 + d) % 4)
    ar4[g1] = jnp.sum(ar3[...], axis=0)
    for d in range(1, 8):
        fourth(d).start()
    some_positions(6, 8)
    stores[3].start()
    for d in range(1, 8):
        fourth(d).wait_send()
        got(ar4, s4, r4, (g1 + d) % 8)
    gw_ref[...] = ar4[...].reshape(128, 128)[:81] * norm
    for copy in stores:
        copy.wait()

    for p in range(2):
        for k in range(3):

            @pl.when(row > 0)
            def _():
                along(p, 0, k).wait_send()

            @pl.when(row < last)
            def _():
                along(p, 1, k).wait_send()


def spread_matrix():
    e = np.zeros((128, 256), np.float32)
    for u in range(9):
        for v in range(9):
            e[9 * u + v, 16 * u + v] = 1.0 / 32.0
    return e


def local(current, previous, shift, weight, cotangent):
    pairs, channels, rows, cols = current.shape
    e = jnp.asarray(spread_matrix(), BF)
    eye = jnp.asarray(np.eye(81, 128), BF)
    total = pairs * rows * lax.axis_size("row") * cols * lax.axis_size("col")
    vmem = pl.BlockSpec(memory_space=pltpu.VMEM)
    hbm = pl.BlockSpec(memory_space=pl.ANY)
    dma = pltpu.SemaphoreType.DMA
    v = pltpu.VMEM
    gc, gp, gw = pl.pallas_call(
        functools.partial(kernel, 1.0 / math.sqrt(total)),
        in_specs=[pl.BlockSpec(memory_space=pltpu.SMEM)] + [hbm] * 3 + [vmem] * 3,
        out_specs=[hbm, hbm, vmem],
        out_shape=[
            jax.ShapeDtypeStruct((2, 8, 128, 256), BF),
            jax.ShapeDtypeStruct((2, 8, 128, 256), BF),
            jax.ShapeDtypeStruct((81, 128), F32),
        ],
        scratch_shapes=[
            v((2, 256, 8, 128), BF), v((2, 256, 8, 128), BF), v((2, 128, 8, 128), BF),
            v((2, 8, 128, 256), BF), v((2, 8, 128, 256), BF),
            v((2, 8, 128, 256), BF), v((2, 8, 128, 256), BF), v((2, 8, 128, 128), BF),
            v((2, 8, 128, 256), BF), v((2, 8, 128, 128), BF),
            v((2048, 128), F32), v((2048, 128), F32),
            v((2, 2, 256, 8, 128), BF), v((2, 2, 4, 16, 256), BF), v((2, 2, 4, 16, 256), BF),
            v((2, 8, 16, 256), BF), v((8, 16, 256), BF), v((8, 16, 256), BF),
            v((2, 4, 16, 128), BF), v((2, 4, 16, 128), BF),
            v((8, WIDE, 256), BF), v((8, WIDE, 256), BF),
            v((2, 8, WIDE, 128), F32), v((8, WIDE, 128), F32),
            v((2, 8, 8, 256), F32), v((2, 8, 8, 128), F32),
            v((2, 2, 256, 8, 128), BF),
            v((2, 2, 4, WIDE, 128), BF), v((2, 2, 4, WIDE, 128), BF),
            v((16, WIDE, 256), BF), v((16, WIDE, 256), BF),
            v((8, WIDE, 128), BF), v((8, WIDE, 128), BF),
            v((2, 8, 128, 256), F32),
            v((2, 8, 128, 128), F32), v((2, 8, 128, 128), F32),
            v((2, 8, WIDE, 256), F32), v((2, 128, 256), F32),
            v((2, 128, 256), F32),
            v((128, 128), F32), v((8, 16, 128), F32), v((4, 16, 128), F32), v((4, 16, 128), F32),
            v((8, 16, 128), F32),
            dma((2, 2)), dma((2, 2)), dma((2, 2, 3)), dma((2, 2, 3)),
            dma((8,)), dma((8,)), dma((4,)), dma((4,)), dma((4,)), dma((4,)), dma((8,)), dma((8,)),
            dma((6,)), dma((4,)),
        ],
        compiler_params=pltpu.CompilerParams(
            collective_id=0, has_side_effects=True, vmem_limit_bytes=56 << 20
        ),
        cost_estimate=pl.CostEstimate(
            flops=3_000_000_000, bytes_accessed=8 << 20, transcendentals=1_500_000
        ),
    )(shift, previous, current, cotangent, weight.T, e, eye)
    return gc.transpose(0, 3, 1, 2), gp.transpose(0, 3, 1, 2), gw.T


def solution(mesh):
    grid = P(None, None, "row", "col")
    return jax.shard_map(
        local,
        mesh=mesh,
        in_specs=(grid, grid, P(), P(), grid),
        out_specs=(grid, grid, P()),
        check_vma=False,
    )
```
